512 devices in a mesh: box: 128 (over z, x, core), rhs: 4 (over y).
Axes of the slice: x: 4, y: 4, z: 16, core: 2. Of those that a mesh axis runs over, the one named last changes fastest.
Arguments:
- charges: bfloat16 [64, 1572864], P(None, ('box', 'rhs')), may hold values from -6 to 6
- points: float32 [3, 1572864], P(None, ('box', 'rhs')), may hold values from 1 to 1.2
- leaf_basis: bfloat16 [64, 1572864], P(None, ('box', 'rhs')), may hold values from -0.5 to 0.5
- leaf_parent: int32 [512, 24], P(('box', 'rhs')), may hold values from 0 to 5, never falling along the last dimension, each value on 1 to 8 neighbouring positions
- leaf_up: bfloat16 [12288, 64, 64], P(('box', 'rhs')), may hold values from -0.375 to 0.375
- leaf_down: bfloat16 [12288, 64, 64], P(('box', 'rhs')), may hold values from -0.75 to 0.75
- box_up: bfloat16 [3072, 64, 64], P(('box', 'rhs')), may hold values from -0.3125 to 0.3125
- box_down: bfloat16 [3072, 64, 64], P(('box', 'rhs')), may hold values from -0.75 to 0.75
- top_up: bfloat16 [8, 2, 64, 64], replicated, may hold values from -0.5 to 0.5
- top_down: bfloat16 [8, 2, 64, 64], replicated, may hold values from -0.75 to 0.75
- top_coupling: bfloat16 [8, 2, 64, 64], replicated, may hold values from -0.5 to 0.5
- leaf_sources: int32 [12288, 16], P(('box', 'rhs')), may hold values from 0 to 12287, as said below
- leaf_classes: int32 [12288, 16], P(('box', 'rhs')), may hold values from 0 to 31
- leaf_coupling: bfloat16 [32, 64, 64], replicated, may hold values from -0.1875 to 0.1875
- box_sources: int32 [3072, 8], P(('box', 'rhs')), may hold values from 0 to 3071, as said below
- box_classes: int32 [3072, 8], P(('box', 'rhs')), may hold values from 0 to 31
- box_coupling: bfloat16 [32, 64, 64], replicated, may hold values from -0.25 to 0.25
- near_leaves: int32 [12288, 27], P(('box', 'rhs')), may hold values from 0 to 12287, as said below
- near_count: int32 [12288], P(('box', 'rhs')), may hold values from 1 to 27
Outputs:
- potentials: float32 [64, 1572864], P(None, ('box', 'rhs'))
The draws below stay inside these ranges and needn't reach their ends.
Inputs may be any that keep to these rules, and one draw needn't show every extreme that they name: `leaf_parent`: within each row the entries never fall, and each of the 6 boxes is named by 1 to 8 leaves. `leaf_sources`: the 16 entries of a leaf are different leaves, never the leaf itself and never one of its near_leaves entries, of its own group or an adjacent group. `box_sources`: the 8 entries of a box are different level-one boxes, never the box itself, of its own group or an adjacent group. `near_leaves`: slot 0 of leaf t holds t; the other slots hold different leaves of the same or an adjacent group.
All inputs are finite; a program needn't handle non-finite values.
Results may differ from the reference program's by a relative error of at most 0.0065.
Values may be sent and summed in bfloat16 or wider, within the bound.
No kernel may reach another device: no remote copies, remote signals or barrier semaphores. Data moves between devices by JAX's collectives and lax.ppermute only.
A program may use at most 128 MiB of HBM per device.

```python
import math
import jax
import jax.numpy as jnp
import numpy as np
from jax import lax

R = 64
K = 64
M = 128
LD = 24
ADM = 16
ADMB = 8
NEAR = 27
CLASSES = 32
TOPL = 8
LEAVES = 12288
BOX1 = 3072
NPTS = 1572864
N_BOX = 128
N_RHS = 4
DEVICES = 512


def window_pick(key, per_group, picks):
    row_total = per_group * DEVICES
    span_size = 3 * per_group
    row_ids = jnp.arange(row_total, dtype=jnp.int32)
    offsets = jnp.arange(span_size, dtype=jnp.int32)
    candidate = (row_ids[:, None] // per_group - 1) * per_group + offsets[None, :]
    usable = (candidate >= 0) & (candidate < row_total) & (candidate != row_ids[:, None])
    scores = jax.random.randint(key, (row_total, span_size), 0, 1 << 20, dtype=jnp.int32) * span_size + offsets[None, :]
    scores = jnp.where(usable, scores, -1)
    chosen = lax.top_k(scores, picks)[1]
    return jnp.take_along_axis(candidate, chosen, axis=1).astype(jnp.int32)


def leaf_lists(key):
    shared_key = jax.random.fold_in(key, 20)
    return window_pick(shared_key, LD, NEAR - 1 + ADM)


def draw_leaf_sources(key, part):
    both = leaf_lists(key)
    return both[:, NEAR - 1:].astype(jnp.int32)


def draw_box_sources(key, part):
    key = jax.random.fold_in(key, 12)
    return window_pick(key, LD // 4, ADMB)


def draw_near_leaves(key, part):
    both = leaf_lists(key)
    others = both[:, :NEAR - 1]
    own_ids = jnp.arange(LD * DEVICES, dtype=jnp.int32)[:, None]
    return jnp.concatenate([own_ids, others], axis=1).astype(jnp.int32)


def draw_near_count(key, part):
    key = jax.random.fold_in(key, 14)
    first_key, second_key, third_key = jax.random.split(key, 3)
    ceiling = jax.random.randint(first_key, (DEVICES,), max(1, NEAR // 3), NEAR + 1, dtype=jnp.int32)
    per_leaf = jnp.repeat(ceiling, LD)
    dropped = jax.random.randint(second_key, (LD * DEVICES,), 0, per_leaf // 2 + 1, dtype=jnp.int32)
    counts = per_leaf - dropped
    special = jax.random.randint(third_key, (), 0, LD * DEVICES, dtype=jnp.int32)
    counts = jnp.where(jnp.arange(LD * DEVICES, dtype=jnp.int32) == special, NEAR, counts)
    return counts.astype(jnp.int32)


def plant(values, own_key, smallest, top_value):
    place = [jax.random.randint(jax.random.fold_in(own_key, axis), (), 0, length) for axis, length in enumerate(values.shape)]
    widest = values.shape.index(max(values.shape))
    next_to = place[:widest] + [(place[widest] + 1) % values.shape[widest]] + place[widest + 1:]
    return values.at[tuple(place)].set(smallest).at[tuple(next_to)].set(top_value)


def shard_levels(key, shape, cuts, least, high):
    factor_of = 1.0
    for axis_at, shards_of in cuts:
        heights = jax.random.uniform(jax.random.fold_in(jax.random.fold_in(key, 6), axis_at), (shards_of,), jnp.float32, least / len(cuts), high / len(cuts))
        factor_of = factor_of * jnp.repeat(jnp.exp(heights), shape[axis_at] // shards_of).reshape((-1,) + (1,) * (len(shape) - 1 - axis_at))
    return factor_of


def profile(count, total, reach, skew):
    weights = [(1 << 20) // math.isqrt(standing ** skew) + 1 for standing in range(2, count + 1)]
    surplus, holding = total - reach - (count - 1), [1] * (count - 1)
    while surplus > 0:
        movable = [i for i in range(count - 1) if holding[i] < reach]
        mass, budget = sum([weights[i] for i in movable]), surplus
        for i in movable:
            more = min(reach - holding[i], max(1, budget * weights[i] // mass), surplus)
            holding[i] = holding[i] + more
            surplus = surplus - more
    return np.array([reach] + holding)


def ragged_sizes(rng, amount, total, bound, skew):
    if amount == 2:
        one = jax.random.randint(rng, (), max(1, total - bound), min(bound, total - 1) + 1)
        return jnp.stack([one, total - one])
    lengths = jnp.asarray(profile(amount, total, bound, skew), jnp.int32)
    pairs = (amount - 1) // 2
    donor, sink = lengths[1:1 + 2 * pairs:2], lengths[2:2 + 2 * pairs:2]
    margin = jnp.minimum(donor - 1, bound - sink)
    passed = jax.random.randint(jax.random.fold_in(rng, 1), (pairs,), 0, 1 << 20) % (margin + 1)
    lengths = lengths.at[1:1 + 2 * pairs:2].set(donor - passed).at[2:2 + 2 * pairs:2].set(sink + passed)
    return lengths[jax.random.permutation(jax.random.fold_in(rng, 2), amount)]


def bell_draw(rng, dims, width, bound, cuts=(), kind=jnp.bfloat16):
    values = jax.random.normal(rng, dims, jnp.float32) * width
    if len(cuts) > 0:
        values = shard_levels(rng, dims, cuts, -0.22, 0.18) * values
    return jnp.clip(values, min=-bound, max=bound).astype(kind)


def setup_inputs(seed: int = 0) -> dict:
    splits = jax.random.split(jax.random.key(seed), 20)
    charges = bell_draw(splits[0], (R, NPTS), 1.0, 6.0, ((1, 512),))
    points = jnp.clip(1.0 + 0.20000005 * jax.random.uniform(splits[1], (3, NPTS), jnp.float32) ** shard_levels(splits[1], (3, NPTS), ((1, 512),), -0.2, 0.2), 1.0, 1.2)
    leaf_basis = bell_draw(splits[2], (K, NPTS), M ** -0.5, 0.5, ((1, 512),))
    leaf_parent = jax.vmap(lambda own: jnp.searchsorted(jnp.cumsum(ragged_sizes(own, LD // 4, LD, 8, 0)), jnp.arange(LD), side="right"))(jax.random.split(splits[3], DEVICES)).reshape((DEVICES, LD)).astype(jnp.int32)
    leaf_up = bell_draw(splits[4], (LEAVES, K, K), (4 * K) ** -0.5, 0.375, ((0, 512),))
    leaf_down = bell_draw(splits[5], (LEAVES, K, K), K ** -0.5, 0.75, ((0, 512),))
    box_up = bell_draw(splits[6], (BOX1, K, K), ((LD // 4) * K) ** -0.5, 0.3125, ((0, 512),))
    box_down = bell_draw(splits[7], (BOX1, K, K), K ** -0.5, 0.75, ((0, 512),))
    top_up = bell_draw(splits[8], (TOPL, 2, K, K), (2 * K) ** -0.5, 0.5)
    top_down = bell_draw(splits[9], (TOPL, 2, K, K), K ** -0.5, 0.75)
    top_coupling = bell_draw(splits[10], (TOPL, 2, K, K), (2 * K) ** -0.5, 0.5)
    leaf_sources = draw_leaf_sources(jax.random.fold_in(splits[19], 71), 0)
    leaf_classes = plant(jax.random.randint(splits[12], (LEAVES, ADM), 0, CLASSES), jax.random.fold_in(splits[12], 1), 0, CLASSES - 1).astype(jnp.int32)
    leaf_coupling = bell_draw(splits[13], (CLASSES, K, K), (ADM * K) ** -0.5, 0.1875)
    box_sources = draw_box_sources(jax.random.fold_in(splits[19], 71), 0)
    box_classes = plant(jax.random.randint(splits[15], (BOX1, ADMB), 0, CLASSES), jax.random.fold_in(splits[15], 1), 0, CLASSES - 1).astype(jnp.int32)
    box_coupling = bell_draw(splits[16], (CLASSES, K, K), (ADMB * K) ** -0.5, 0.25)
    near_leaves = draw_near_leaves(jax.random.fold_in(splits[19], 71), 0)
    near_count = draw_near_count(jax.random.fold_in(splits[19], 71), 0)
    return dict(charges=charges, points=points, leaf_basis=leaf_basis, leaf_parent=leaf_parent, leaf_up=leaf_up, leaf_down=leaf_down, box_up=box_up, box_down=box_down, top_up=top_up, top_down=top_down, top_coupling=top_coupling, leaf_sources=leaf_sources, leaf_classes=leaf_classes, leaf_coupling=leaf_coupling, box_sources=box_sources, box_classes=box_classes, box_coupling=box_coupling, near_leaves=near_leaves, near_count=near_count)


delta_squared = 0.0001

def high_dot(vectors, matrix):
    return jnp.einsum('rik,kj->rij', vectors, matrix.astype(jnp.float32), precision=lax.Precision.HIGHEST)

def couple_level(coef, sources, classes, coupling):
    summed = jnp.zeros((coef.shape[0], sources.shape[0], coef.shape[2]), jnp.float32)
    for column in range(sources.shape[1]):
        picked = coef[:, sources[:, column], :].astype(jnp.float32)
        blocks = coupling[classes[:, column]].astype(jnp.float32)
        summed = summed + jnp.einsum('rnk,nkj->rnj', picked, blocks)
    return summed

def near_field(grouped, points, near_leaves, near_count, leaf_total):
    point_grid = points.reshape(3, leaf_total, M)
    block_leaves = LD * math.gcd(leaf_total // LD, 8)
    block_count = leaf_total // block_leaves
    near_scale = 0.5 / math.sqrt(NEAR * M)

    def one_block(block_index):
        first_leaf = block_index * block_leaves
        targets = lax.dynamic_slice_in_dim(point_grid, first_leaf, block_leaves, 1)
        near_rows = lax.dynamic_slice_in_dim(near_leaves, first_leaf, block_leaves, 0)
        counts = lax.dynamic_slice_in_dim(near_count, first_leaf, block_leaves, 0)

        def slot_step(slot_index, summed):
            column = lax.dynamic_index_in_dim(near_rows, slot_index, 1, keepdims=False)
            source_points = jnp.take(point_grid, column, axis=1)
            squared = jnp.zeros((block_leaves, M, M), jnp.float32)
            for axis_index in range(3):
                offset = targets[axis_index][:, :, None] - source_points[axis_index][:, None, :]
                squared = squared + offset * offset
            kernel = jnp.where(slot_index < counts[:, None, None], near_scale * lax.rsqrt(squared + delta_squared), 0.0).astype(jnp.bfloat16)
            source_charges = jnp.take(grouped, column, axis=1)
            return summed + jnp.einsum('lim,rlm->rli', kernel.astype(jnp.float32), source_charges)
        return lax.fori_loop(0, NEAR, slot_step, jnp.zeros((R, block_leaves, M), jnp.float32))
    pieces = lax.map(one_block, jnp.arange(block_count, dtype=jnp.int32))
    return jnp.transpose(pieces, (1, 0, 2, 3)).reshape(R, leaf_total, M)

def reference(charges, points, leaf_basis, leaf_parent, leaf_up, leaf_down, box_up, box_down, top_up, top_down, top_coupling, leaf_sources, leaf_classes, leaf_coupling, box_sources, box_classes, box_coupling, near_leaves, near_count):
    group_total = N_BOX * N_RHS
    leaf_total = LD * group_total
    box_per_group = LD // 4
    box_total = box_per_group * group_total
    grouped = charges.astype(jnp.float32).reshape(R, leaf_total, M)
    basis_grid = leaf_basis.astype(jnp.float32).reshape(K, leaf_total, M)
    leaf_coef = jnp.einsum('rlm,klm->rlk', grouped, basis_grid).astype(jnp.bfloat16)
    parent_ids = (jnp.arange(group_total, dtype=jnp.int32)[:, None] * box_per_group + leaf_parent).reshape(-1)
    lifted = jnp.einsum('rlk,lkj->rlj', leaf_coef.astype(jnp.float32), leaf_up.astype(jnp.float32))
    box_coef = jax.ops.segment_sum(jnp.transpose(lifted, (1, 0, 2)), parent_ids, num_segments=box_total)
    box_coef = jnp.transpose(box_coef, (1, 0, 2)).astype(jnp.bfloat16)
    lifted_box = jnp.einsum('rpk,pkj->rpj', box_coef.astype(jnp.float32), box_up.astype(jnp.float32))
    ascent = lifted_box.reshape(R, group_total, box_per_group, K).sum(axis=2)
    tier_count = group_total.bit_length() - 1
    top_level = tier_count - 2
    ascents = [ascent]
    for height in range(top_level):
        current = ascents[-1]
        ascents.append(high_dot(current[:, 0::2], top_up[height, 0]) + high_dot(current[:, 1::2], top_up[height, 1]))
    fields = []
    for height in range(top_level + 1):
        current = ascents[height]
        box_ids = jnp.arange(current.shape[1], dtype=jnp.int32)
        fields.append(high_dot(current[:, box_ids ^ 2], top_coupling[height, 0]) + high_dot(current[:, box_ids ^ 3], top_coupling[height, 1]))
    descent = fields[top_level]
    for height in reversed(range(top_level)):
        box_ids = jnp.arange(fields[height].shape[1], dtype=jnp.int32)
        spread = descent[:, box_ids // 2]
        matrices = top_down[height][box_ids % 2].astype(jnp.float32)
        descent = fields[height] + jnp.einsum('rij,ijk->rik', spread, matrices, precision=lax.Precision.HIGHEST)
    group_local = descent.astype(jnp.bfloat16)
    leaf_field = couple_level(leaf_coef, leaf_sources, leaf_classes, leaf_coupling)
    box_field = couple_level(box_coef, box_sources, box_classes, box_coupling)
    owner_group = jnp.arange(box_total, dtype=jnp.int32) // box_per_group
    box_local = (box_field + jnp.einsum('rpj,pjk->rpk', group_local[:, owner_group].astype(jnp.float32), box_down.astype(jnp.float32))).astype(jnp.bfloat16)
    leaf_local = (leaf_field + jnp.einsum('rlj,ljk->rlk', box_local[:, parent_ids].astype(jnp.float32), leaf_down.astype(jnp.float32))).astype(jnp.bfloat16)
    far_part = jnp.einsum('rlk,klm->rlm', leaf_local.astype(jnp.float32), basis_grid)
    near_part = near_field(grouped, points, near_leaves, near_count, leaf_total)
    return (near_part + far_part).reshape(R, leaf_total * M)
```

```python
import math

import jax
import jax.numpy as jnp
import numpy as np
from jax import lax
from jax.experimental import pallas as pl
from jax.experimental.pallas import tpu as pltpu
from jax.sharding import PartitionSpec as P

BF = jnp.bfloat16
F32 = jnp.float32
AXES = ("box", "rhs")

R = 64
K = 64
M = 128
LD = 24
BX = 6
ADM = 16
ADMB = 8
NEAR = 27
FR = 16
ROWS = R + FR
FX = 32
UNROLL = 8
LOW = 32
SLOTS = LD * (NEAR + 1) + 2 * UNROLL

DELTA2 = 0.0001
INV_SCALE = 2.0 * math.sqrt(NEAR * M)
CENTRE = 1.1

PARTS = ((0, 0), (0, 1), (0, 2), (1, 0), (1, 1), (1, 2), (2, 0), (2, 1))

VMEM = pl.BlockSpec(memory_space=pltpu.VMEM)
SMEM = pl.BlockSpec(memory_space=pltpu.SMEM)
ANY = pl.BlockSpec(memory_space=pl.ANY)


def params():
    return pltpu.CompilerParams(vmem_limit_bytes=40 * 1024 * 1024)


def sds(shape, dtype):
    return jax.ShapeDtypeStruct(shape, dtype)


def dot(a, b):
    return jnp.dot(a, b, preferred_element_type=F32)


def dot_nt(a, b):
    return lax.dot_general(a, b, (((1,), (1,)), ((), ())), preferred_element_type=F32)


def dot2(x, m):
    hi = x.astype(BF)
    lo = (x - hi.astype(F32)).astype(BF)
    return dot(hi, m) + dot(lo, m)


def expansion():
    out = np.zeros((8 * FR, 8, M), np.float32)
    for leaf in range(8):
        e = 0
        for a, _ in PARTS:
            for c in range(3):
                out[FR * leaf + 3 * a + c, leaf, e] = 1.0
                e += 1
        for c in range(3):
            out[FR * leaf + 9 + c, leaf, e] = 1.0
            e += 1
        for c in range(3):
            out[FR * leaf + 12, leaf, e] = 1.0
            e += 1
    return out.reshape(8 * FR, 8 * M)


def split3(x):
    hi = x.astype(BF).astype(F32)
    rest = x - hi
    mid = rest.astype(BF).astype(F32)
    return hi, mid, rest - mid


def pack_body(charges, points, sent, target, feat, wide):
    p = (points[...] - CENTRE) * INV_SCALE
    parts = split3(p)
    norm = p[0:1] * p[0:1] + p[1:2] * p[1:2] + p[2:3] * p[2:3]
    source_norm = split3(norm)
    target_norm = split3(norm + DELTA2 * INV_SCALE * INV_SCALE)
    feat[...] = jnp.zeros(feat.shape, F32)
    wide[...] = jnp.zeros(wide.shape, F32)
    one = jnp.ones(norm.shape, F32)
    for a in range(3):
        feat[3 * a : 3 * a + 3, :] = parts[a]
        feat[9 + a : 10 + a, :] = source_norm[a]
    feat[12:13, :] = one
    for n, (_, b) in enumerate(PARTS):
        wide[3 * n : 3 * n + 3, :] = -2.0 * parts[b]
    base = 3 * len(PARTS)
    for a in range(3):
        wide[base + a : base + a + 1, :] = one
        wide[base + 3 + a : base + 4 + a, :] = target_norm[a]
    for leaf in range(LD):
        cols = pl.ds(leaf * M, M)
        sent[leaf, 0:R, :] = charges[:, cols]
        target[leaf, :, :] = wide[:, cols].astype(BF)
    for o in range(LD // 8):
        rows = jnp.concatenate([feat[:, pl.ds((8 * o + i) * M, M)] for i in range(8)], axis=0)
        turned = rows.T.astype(BF)
        for i in range(8):
            sent[8 * o + i, R:ROWS, :] = turned[FR * i : FR * (i + 1), :]


def pack(charges, points):
    return pl.pallas_call(
        pack_body,
        in_specs=[VMEM, VMEM],
        out_specs=[VMEM, VMEM],
        out_shape=[sds((LD, ROWS, M), BF), sds((LD, FX, M), BF)],
        scratch_shapes=[pltpu.VMEM((FR, LD * M), F32), pltpu.VMEM((FX, LD * M), F32)],
        compiler_params=params(),
        name="pack_points",
    )(charges, points)


def up_body(charges, basis, leaf_up, box_up, parents, code, coef, ascent, own, halo, sizes, acc):
    acc[...] = jnp.zeros(acc.shape, F32)
    po = jnp.int32(0)
    ph = jnp.int32(0)
    for leaf in range(LD):
        cols = pl.ds(leaf * M, M)
        c = dot_nt(charges[:, cols], basis[:, cols])
        if leaf % 2 == 0:
            even = c
        else:
            coef[leaf // 2] = jnp.concatenate([even, c], axis=1).astype(BF)
        acc[parents[leaf]] += dot(c.astype(BF), leaf_up[leaf])
        for s in range(NEAR):
            x = code[leaf, s]
            own[po] = x
            halo[ph] = x
            po = po + ((x >> 16) & 1)
            ph = ph + (x >> 17)
        own[po] = leaf << 8 | LD
        halo[ph] = leaf << 8 | (2 * LD)
        po = (po + 1) & -2
        ph = (ph + 1) & -2
    for n in range(2 * UNROLL):
        own[po + n] = LD << 8 | LD
        halo[ph + n] = LD << 8 | (2 * LD)
    sizes[0] = (po // 2 + UNROLL - 1) // UNROLL
    sizes[1] = (ph // 2 + UNROLL - 1) // UNROLL
    total = jnp.zeros((R, K), F32)
    for box in range(BX):
        b = acc[box]
        if box % 2 == 0:
            even = b
        else:
            coef[(LD + box) // 2] = jnp.concatenate([even, b], axis=1).astype(BF)
        total = total + dot(b.astype(BF), box_up[box])
    ascent[...] = jnp.concatenate([total[: R // 2], total[R // 2 :]], axis=1).astype(BF)


def climb(charges, basis, leaf_up, box_up, parents, code):
    return pl.pallas_call(
        up_body,
        in_specs=[VMEM, VMEM, VMEM, VMEM, SMEM, SMEM],
        out_specs=[VMEM, VMEM, SMEM, SMEM, SMEM],
        out_shape=[
            sds(((LD + BX) // 2, R, 2 * K), BF),
            sds((R // 2, 2 * K), BF),
            sds((SLOTS,), jnp.int32),
            sds((SLOTS,), jnp.int32),
            sds((2,), jnp.int32),
        ],
        scratch_shapes=[pltpu.VMEM((BX, R, K), F32)],
        compiler_params=params(),
        name="leaf_to_group",
    )(charges, basis, leaf_up, box_up, parents, code)


def near_body(which, blocks, *refs):
    sizes, slots, target, expand = refs[:4]
    sources = refs[4 : 4 + blocks]
    rest = refs[4 + blocks :]
    if which == 1:
        start_from, _, out, table, feats, acc, sems = rest
    else:
        out, table, feats, acc, sems = rest
    count = blocks * LD
    copies = [
        pltpu.make_async_copy(src, table.at[pl.ds(n * LD, LD)], sems.at[n])
        for n, src in enumerate(sources)
    ]
    for copy in copies:
        copy.start()
    if which == 1:
        acc[0:LD] = start_from[...]
        acc[LD] = jnp.zeros((R, M), F32)
    else:
        acc[...] = jnp.zeros(acc.shape, F32)
    table[count] = jnp.zeros((ROWS, M), BF)
    for copy in copies:
        copy.wait()
    for o in range(count // 8):
        rows = jnp.concatenate([table[8 * o + i, R:ROWS, :] for i in range(8)], axis=0)
        spread = dot(rows, expand[...]).astype(BF)
        for i in range(8):
            feats[8 * o + i] = spread[:, M * i : M * (i + 1)]
    lane = lax.broadcasted_iota(jnp.int32, (M, M), 1)
    ones = 3 * len(PARTS) + 3
    feats[count] = jnp.where((lane >= ones) & (lane < ones + 3), 1.0, 0.0).astype(BF)
    pad = jnp.zeros((M - FX, M), BF)

    def step(it, _):
        for u in range(UNROLL):
            at = (it * UNROLL + u) * 2
            first, second = slots[at], slots[at + 1]
            s0, s1 = first & 255, second & 255
            t = (first >> 8) & 255
            rows = jnp.concatenate([feats[s0], feats[s1]], axis=0)
            square = dot(rows, jnp.concatenate([target[jnp.minimum(t, LD - 1)], pad], axis=0))
            kernel = lax.rsqrt(square).astype(BF)
            weights = jnp.concatenate([table[s0, 0:R, :], table[s1, 0:R, :]], axis=1)
            acc[t] += dot(weights, kernel)
        return 0

    lax.fori_loop(0, sizes[which], step, 0)
    out[...] = acc[0:LD]


def near(which, sizes, slots, target, expand, sources, extra):
    blocks = len(sources)
    pairs = 400 if which else 200
    return pl.pallas_call(
        lambda *refs: near_body(which, blocks, *refs),
        in_specs=[SMEM, SMEM, VMEM, VMEM] + [ANY] * blocks + ([VMEM, ANY] if which else []),
        out_specs=VMEM,
        out_shape=sds((LD, R, M), F32),
        scratch_shapes=[
            pltpu.VMEM((blocks * LD + 1, ROWS, M), BF),
            pltpu.VMEM((blocks * LD + 1, M, M), BF),
            pltpu.VMEM((LD + 1, R, M), F32),
            pltpu.SemaphoreType.DMA((blocks,)),
        ],
        compiler_params=params(),
        cost_estimate=pl.CostEstimate(
            flops=pairs * 2 * 256 * 128 * 320, bytes_accessed=2 << 20, transcendentals=pairs << 15
        ),
        name="near_halo" if which else "near_own",
    )(sizes, slots, target, expand, *sources, *extra)


def level_up(nodes, matrices):
    count = nodes.shape[0] // 2
    pairs = nodes.reshape(count, 2, R // 2, 2 * K)
    left = pairs[:, 0].reshape(count * (R // 2), 2 * K)
    right = pairs[:, 1].reshape(count * (R // 2), 2 * K)
    if nodes.dtype == BF:
        out = dot(left, matrices[0]) + dot(right, matrices[1])
    else:
        out = dot2(left, matrices[0]) + dot2(right, matrices[1])
    return out.reshape(count, R // 2, 2 * K)


def block_fields(nodes, up, coupling, held, place, fields):
    out = []
    for h in range(4):
        count = LOW >> h
        held[0:count] = nodes.astype(F32)
        q = place >> h
        out.append(dot2(held[q ^ 2], coupling[h, 0]) + dot2(held[q ^ 3], coupling[h, 1]))
        if h < 3 or fields is None:
            nodes = level_up(nodes, (up[h, 0], up[h, 1]))
    return out, nodes


def low_body(place, nodes, up, coupling, down, _, top, field, held):
    me = place[0]
    fields, nodes = block_fields(nodes[...], up, coupling, held, me & (LOW - 1), None)
    top[...] = nodes.astype(BF)
    total = fields[3]
    for h in (2, 1, 0):
        total = fields[h] + dot2(total, down[h, (me >> h) & 1])
    field[...] = total


def low_tree(place, nodes, mats, order):
    return pl.pallas_call(
        low_body,
        in_specs=[SMEM, VMEM, VMEM, VMEM, VMEM, ANY],
        out_specs=[VMEM, VMEM],
        out_shape=[sds((2, R // 2, 2 * K), BF), sds((R // 2, 2 * K), F32)],
        scratch_shapes=[pltpu.VMEM((LOW, R // 2, 2 * K), F32)],
        compiler_params=params(),
        name="coarse_low",
    )(place, nodes, *mats, order)


def couple_body(codes, box_codes, matrices, box_matrices, left, mine, right, _, leaf_field, box_field, table, low, high, sems):
    pairs = (LD + BX) // 2
    copies = [
        pltpu.make_async_copy(src, table.at[pl.ds(n * pairs, pairs)], sems.at[n])
        for n, src in enumerate((left, mine, right))
    ]
    for copy in copies:
        copy.start()
    for copy in copies:
        copy.wait()
    first = lax.broadcasted_iota(jnp.int32, (R, 2 * K), 1) < K
    for n in range(3):
        for i in range(pairs):
            x = table[n * pairs + i].astype(F32)
            y = pltpu.roll(x, K, 1)
            at = 2 * (n * pairs + i)
            low[at] = jnp.where(first, x, 0.0).astype(BF)
            low[at + 1] = jnp.where(first, y, 0.0).astype(BF)
            high[at] = jnp.where(first, 0.0, y).astype(BF)
            high[at + 1] = jnp.where(first, 0.0, x).astype(BF)

    def gather(codes, row, mats, width):
        total = jnp.zeros((R, K), F32)
        for g in range(width // 4):
            c = [codes[row, 4 * g + i] for i in range(4)]
            s = [x & 255 for x in c]
            vec = jnp.concatenate([low[s[0]] + high[s[1]], low[s[2]] + high[s[3]]], axis=1)
            mat = jnp.concatenate([mats[x >> 8] for x in c], axis=0)
            total = total + dot(vec, mat)
        return total

    def step(it, _):
        for u in range(6):
            row = it * 6 + u
            leaf_field[row] = gather(codes, row, matrices, ADM)
        return 0

    lax.fori_loop(0, LD // 6, step, 0)
    for box in range(BX):
        box_field[box] = gather(box_codes, box, box_matrices, ADMB)


def couple(codes, box_codes, matrices, box_matrices, coefs, order):
    pairs = (LD + BX) // 2
    return pl.pallas_call(
        couple_body,
        in_specs=[SMEM, SMEM, VMEM, VMEM, ANY, ANY, ANY, ANY],
        out_specs=[VMEM, VMEM],
        out_shape=[sds((LD, R, K), F32), sds((BX, R, K), F32)],
        scratch_shapes=[
            pltpu.VMEM((3 * pairs, R, 2 * K), BF),
            pltpu.VMEM((6 * pairs, R, 2 * K), BF),
            pltpu.VMEM((6 * pairs, R, 2 * K), BF),
            pltpu.SemaphoreType.DMA((3,)),
        ],
        compiler_params=params(),
        cost_estimate=pl.CostEstimate(flops=1 << 30, bytes_accessed=1 << 20, transcendentals=0),
        name="couple_levels",
    )(codes, box_codes, matrices, box_matrices, *coefs, order)


def final_body(place, nodes, up, coupling, down, low_down, low_field, parents, leaf_field, box_field, box_down, leaf_down, basis, near_part, out, held, boxes):
    me = place[0]
    block = nodes[...].reshape(LOW, R // 2, 2 * K)
    fields, _ = block_fields(block, up, coupling, held, (me >> 4) & (LOW - 1), True)
    total = fields[3]
    for h in (2, 1, 0):
        total = fields[h] + dot2(total, down[h, (me >> (h + 4)) & 1])
    for h in (3, 2, 1, 0):
        total = dot2(total, low_down[h, (me >> h) & 1])
    total = total + low_field[...]
    group = jnp.concatenate([total[:, :K], total[:, K:]], axis=0).astype(BF)
    for box in range(BX):
        boxes[box] = (box_field[box] + dot(group, box_down[box])).astype(BF)
    for leaf in range(LD):
        cols = pl.ds(leaf * M, M)
        field = leaf_field[leaf] + dot(boxes[parents[leaf]], leaf_down[leaf])
        out[:, cols] = near_part[leaf] + dot(field.astype(BF), basis[:, cols])


def finish(place, nodes, high_mats, low_down, low_field, parents, fields, box_down, leaf_down, basis, near_part):
    return pl.pallas_call(
        final_body,
        in_specs=[SMEM] + [VMEM] * 6 + [SMEM] + [VMEM] * 6,
        out_specs=VMEM,
        out_shape=sds((R, LD * M), F32),
        scratch_shapes=[pltpu.VMEM((LOW, R // 2, 2 * K), F32), pltpu.VMEM((BX, R, K), BF)],
        compiler_params=params(),
        name="group_to_points",
    )(place, nodes, *high_mats, low_down, low_field, parents, *fields, box_down, leaf_down, basis, near_part)


def doubled(m):
    edge = ((0, 0),) * (m.ndim - 2)
    return jnp.pad(m, edge + ((0, K), (0, K))) + jnp.pad(m, edge + ((K, 0), (K, 0)))


def exchange(x):
    count = lax.axis_size(AXES)
    left = lax.ppermute(x, AXES, [(i, i + 1) for i in range(count - 1)])
    right = lax.ppermute(x, AXES, [(i + 1, i) for i in range(count - 1)])
    return left, right


def local(
    charges,
    points,
    leaf_basis,
    leaf_parent,
    leaf_up,
    leaf_down,
    box_up,
    box_down,
    top_up,
    top_down,
    top_coupling,
    leaf_sources,
    leaf_classes,
    leaf_coupling,
    box_sources,
    box_classes,
    box_coupling,
    near_leaves,
    near_count,
):
    count = lax.axis_size(AXES)
    device = lax.axis_index(AXES)
    place = device.astype(jnp.int32).reshape(1)
    parents = leaf_parent[0]
    pairs = (LD + BX) // 2

    sent, target = pack(charges, points)
    sent_left, sent_right = exchange(sent)

    rel = near_leaves - device * LD
    mine = (rel >= 0) & (rel < LD)
    used = jnp.arange(NEAR, dtype=jnp.int32)[None, :] < near_count[:, None]
    row = jnp.where(rel < 0, rel + LD, rel)
    leaf_ids = jnp.arange(LD, dtype=jnp.int32)[:, None]
    flags = jnp.where(used, jnp.where(mine, 1, 2), 0)
    code = row | leaf_ids << 8 | flags << 16

    coef, ascent, own, halo, sizes = climb(charges, leaf_basis, leaf_up, box_up, parents, code)

    blocks = count // LOW
    low_groups = [[b * LOW + i for i in range(LOW)] for b in range(blocks)]
    high_groups = [[b * LOW + i for b in range(blocks)] for i in range(LOW)]
    low_nodes = lax.all_gather(ascent, AXES, axis_index_groups=low_groups)
    coef_left, coef_right = exchange(coef)

    expand = jnp.asarray(expansion(), BF)
    near_own = near(0, sizes, own, target, expand, (sent,), ())

    low_mats = [doubled(m[0:4]) for m in (top_up, top_coupling, top_down)]
    high_mats = [doubled(m[4:8]) for m in (top_up, top_coupling, top_down)]
    top, low_field = low_tree(place, low_nodes, low_mats, near_own)
    high_nodes = lax.all_gather(top, AXES, axis_index_groups=high_groups)

    near_all = near(1, sizes, halo, target, expand, (sent_left, sent_right), (near_own, low_field))

    def table_row(sources, classes, width, start):
        rel = sources - (device - 1) * width
        block = (rel >= width).astype(jnp.int32) + (rel >= 2 * width).astype(jnp.int32)
        return rel + block * (2 * pairs - width) + start | classes << 8

    codes = table_row(leaf_sources, leaf_classes, LD, 0)
    box_codes = table_row(box_sources, box_classes, BX, LD)
    fields = couple(
        codes, box_codes, leaf_coupling, box_coupling, (coef_left, coef, coef_right), low_field
    )
    return finish(
        place, high_nodes, high_mats, low_mats[2], low_field, parents, fields, box_down, leaf_down, leaf_basis, near_all
    )


def solution(mesh):
    split = P(AXES)
    return jax.shard_map(
        local,
        mesh=mesh,
        in_specs=(
            P(None, AXES),
            P(None, AXES),
            P(None, AXES),
            split,
            split,
            split,
            split,
            split,
            P(),
            P(),
            P(),
            split,
            split,
            P(),
            split,
            split,
            P(),
            split,
            split,
        ),
        out_specs=P(None, AXES),
        check_vma=False,
    )
```

```python
import math

import jax
import jax.numpy as jnp
import numpy as np
from jax import lax
from jax.experimental import pallas as pl
from jax.experimental.pallas import tpu as pltpu
from jax.sharding import PartitionSpec as P

BF = jnp.bfloat16
F32 = jnp.float32
AXES = ("box", "rhs")

R = 64
K = 64
M = 128
LD = 24
BX = 6
ADM = 16
ADMB = 8
NEAR = 27
FR = 16
ROWS = R + FR
FX = 32
UNROLL = 8
PAIRS = (LD + BX) // 2
SENT = LD + PAIRS * R // ROWS
SLOTS = LD * (NEAR + 1) + 2 * UNROLL

DELTA2 = 0.0001
INV_SCALE = 2.0 * math.sqrt(NEAR * M)
CENTRE = 1.1

PARTS = ((0, 0), (0, 1), (0, 2), (1, 0), (1, 1), (1, 2), (2, 0), (2, 1))

VMEM = pl.BlockSpec(memory_space=pltpu.VMEM)
SMEM = pl.BlockSpec(memory_space=pltpu.SMEM)
ANY = pl.BlockSpec(memory_space=pl.ANY)


def params():
    return pltpu.CompilerParams(vmem_limit_bytes=24 * 1024 * 1024)


def sds(shape, dtype):
    return jax.ShapeDtypeStruct(shape, dtype)


def dot(a, b):
    return jnp.dot(a, b, preferred_element_type=F32)


def dot_nt(a, b):
    return lax.dot_general(a, b, (((1,), (1,)), ((), ())), preferred_element_type=F32)


def dot2(x, m):
    hi = x.astype(BF)
    lo = (x - hi.astype(F32)).astype(BF)
    return dot(hi, m) + dot(lo, m)


def expansion():
    out = np.zeros((8 * FR, 8, M), np.float32)
    for leaf in range(8):
        e = 0
        for a, _ in PARTS:
            for c in range(3):
                out[FR * leaf + 3 * a + c, leaf, e] = 1.0
                e += 1
        for c in range(3):
            out[FR * leaf + 9 + c, leaf, e] = 1.0
            e += 1
        for c in range(3):
            out[FR * leaf + 12, leaf, e] = 1.0
            e += 1
    return out.reshape(8 * FR, 8 * M)


def split3(x):
    hi = x.astype(BF).astype(F32)
    rest = x - hi
    mid = rest.astype(BF).astype(F32)
    return hi, mid, rest - mid


def load(copies):
    for copy in copies:
        copy.start()
    return copies


def first_body(charges_in, points_in, basis_in, leaf_up_in, box_up_in, parents, code, sent, target, ascent, own, left, right, sizes, charges, points, basis, leaf_up, box_up, feat, wide, acc, sems):
    moves = ((points_in, points), (charges_in, charges), (basis_in, basis), (leaf_up_in, leaf_up), (box_up_in, box_up))
    copies = load([pltpu.make_async_copy(a, b, sems.at[n]) for n, (a, b) in enumerate(moves)])
    acc[...] = jnp.zeros(acc.shape, F32)
    copies[1].wait()
    copies[2].wait()
    copies[3].wait()
    lists = (own, left, right)
    at = [jnp.int32(0)] * 3
    for group in range(LD // 8):
        leaves = range(8 * group, 8 * group + 8)
        c = [dot_nt(charges[:, pl.ds(leaf * M, M)], basis[:, pl.ds(leaf * M, M)]) for leaf in leaves]
        raised = [dot(c[i].astype(BF), leaf_up[leaf]) for i, leaf in enumerate(leaves)]
        for leaf in leaves:
            for s in range(NEAR):
                x = code[leaf, s]
                for n in range(3):
                    lists[n][at[n]] = x
                    at[n] = at[n] + ((x >> (16 + n)) & 1)
            for n in range(3):
                lists[n][at[n]] = leaf << 8 | LD
                at[n] = (at[n] + 1) & -2
        for i in range(0, 8, 2):
            put_coef(sent, (8 * group + i) // 2, jnp.concatenate([c[i], c[i + 1]], axis=1).astype(BF))
        for i, leaf in enumerate(leaves):
            acc[parents[leaf]] += raised[i]
    for n in range(3):
        for i in range(2 * UNROLL):
            lists[n][at[n] + i] = LD << 8 | LD
        sizes[n] = (at[n] // 2 + UNROLL - 1) // UNROLL
    copies[4].wait()
    copies[0].wait()
    boxes = [acc[box] for box in range(BX)]
    raised = [dot(boxes[box].astype(BF), box_up[box]) for box in range(BX)]
    ascent[...] = (raised[0] + raised[1] + (raised[2] + raised[3]) + (raised[4] + raised[5])).astype(BF)
    for box in range(0, BX, 2):
        put_coef(sent, (LD + box) // 2, jnp.concatenate([boxes[box], boxes[box + 1]], axis=1).astype(BF))

    p = (points[...] - CENTRE) * INV_SCALE
    parts = split3(p)
    norm = p[0:1] * p[0:1] + p[1:2] * p[1:2] + p[2:3] * p[2:3]
    source_norm = split3(norm)
    target_norm = split3(norm + DELTA2 * INV_SCALE * INV_SCALE)
    feat[...] = jnp.zeros(feat.shape, F32)
    wide[...] = jnp.zeros(wide.shape, F32)
    one = jnp.ones(norm.shape, F32)
    for a in range(3):
        feat[3 * a : 3 * a + 3, :] = parts[a]
        feat[9 + a : 10 + a, :] = source_norm[a]
    feat[12:13, :] = one
    for n, (_, b) in enumerate(PARTS):
        wide[3 * n : 3 * n + 3, :] = -2.0 * parts[b]
    base = 3 * len(PARTS)
    for a in range(3):
        wide[base + a : base + a + 1, :] = one
        wide[base + 3 + a : base + 4 + a, :] = target_norm[a]
    turned = []
    for o in range(LD // 8):
        rows = jnp.concatenate([feat[:, pl.ds((8 * o + i) * M, M)] for i in range(8)], axis=0)
        turned.append(rows.T.astype(BF))
    for leaf in range(LD):
        cols = pl.ds(leaf * M, M)
        sent[leaf, 0:R, :] = charges[:, cols]
        i = leaf % 8
        sent[leaf, R:ROWS, :] = turned[leaf // 8][FR * i : FR * (i + 1), :]
        target[leaf, :, :] = wide[:, cols].astype(BF)


def coef_places(pair):
    rows = [pair * R + 16 * i for i in range(R // 16)]
    return [(r // ROWS, r % ROWS) for r in rows]


def put_coef(sent, pair, value):
    for i, (block, row) in enumerate(coef_places(pair)):
        sent[LD + block, row : row + 16, :] = value[16 * i : 16 * i + 16]


def first(charges, points, basis, leaf_up, box_up, parents, code):
    return pl.pallas_call(
        first_body,
        in_specs=[ANY] * 5 + [SMEM, SMEM],
        out_specs=[VMEM] * 3 + [SMEM] * 4,
        out_shape=[
            sds((SENT, ROWS, M), BF),
            sds((LD, FX, M), BF),
            sds((R, K), BF),
            sds((SLOTS,), jnp.int32),
            sds((SLOTS,), jnp.int32),
            sds((SLOTS,), jnp.int32),
            sds((3,), jnp.int32),
        ],
        scratch_shapes=[
            pltpu.VMEM((R, LD * M), BF),
            pltpu.VMEM((3, LD * M), F32),
            pltpu.VMEM((K, LD * M), BF),
            pltpu.VMEM((LD, K, K), BF),
            pltpu.VMEM((BX, K, K), BF),
            pltpu.VMEM((FR, LD * M), F32),
            pltpu.VMEM((FX, LD * M), F32),
            pltpu.VMEM((BX, R, K), F32),
            pltpu.SemaphoreType.DMA((5,)),
        ],
        compiler_params=params(),
        name="points_to_group",
    )(charges, points, basis, leaf_up, box_up, parents, code)


def near_body(which, sizes, slots, target, expand, source, *rest):
    if which:
        start_from, _, acc, table, feats, sem = rest
    else:
        _, acc, table, feats, sem = rest
    copy = pltpu.make_async_copy(source.at[pl.ds(0, LD)], table.at[pl.ds(0, LD)], sem)
    copy.start()
    if which:
        acc[...] = start_from[...]
    else:
        acc[...] = jnp.zeros(acc.shape, F32)
    table[LD] = jnp.zeros((ROWS, M), BF)
    lane = lax.broadcasted_iota(jnp.int32, (M, M), 1)
    ones = 3 * len(PARTS) + 3
    feats[LD] = jnp.where((lane >= ones) & (lane < ones + 3), 1.0, 0.0).astype(BF)
    copy.wait()
    for o in range(LD // 8):
        rows = jnp.concatenate([table[8 * o + i, R:ROWS, :] for i in range(8)], axis=0)
        spread = dot(rows, expand[...]).astype(BF)
        for i in range(8):
            feats[8 * o + i] = spread[:, M * i : M * (i + 1)]
    pad = jnp.zeros((M - FX, M), BF)

    def step(it, _):
        t, kernels, weights = [], [], []
        for u in range(UNROLL):
            at = (it * UNROLL + u) * 2
            first, second = slots[at], slots[at + 1]
            s0, s1 = first & 255, second & 255
            t.append((first >> 8) & 255)
            rows = jnp.concatenate([feats[s0], feats[s1]], axis=0)
            square = dot(rows, jnp.concatenate([target[jnp.minimum(t[u], LD - 1)], pad], axis=0))
            kernels.append(lax.rsqrt(square).astype(BF))
            weights.append(jnp.concatenate([table[s0, 0:R, :], table[s1, 0:R, :]], axis=1))
        terms = [dot(weights[u], kernels[u]) for u in range(UNROLL)]
        for u in range(UNROLL):
            acc[t[u]] += terms[u]
        return 0

    lax.fori_loop(0, sizes[which], step, 0)


def near(which, sizes, slots, target, expand, source, extra):
    pairs = 100
    return pl.pallas_call(
        lambda *refs: near_body(which, *refs),
        in_specs=[SMEM, SMEM, VMEM, VMEM, ANY] + ([VMEM, ANY] if which else [ANY]),
        out_specs=VMEM,
        out_shape=sds((LD + 1, R, M), F32),
        scratch_shapes=[
            pltpu.VMEM((LD + 1, ROWS, M), BF),
            pltpu.VMEM((LD + 1, M, M), BF),
            pltpu.SemaphoreType.DMA,
        ],
        compiler_params=params(),
        cost_estimate=pl.CostEstimate(
            flops=pairs * 2 * 256 * 128 * 320, bytes_accessed=2 << 20, transcendentals=pairs << 15
        ),
        name=("near_own", "near_left", "near_right")[which],
    )(sizes, slots, target, expand, source, *extra)


def bottom_body(place, mine, one, two, three, up, coupling, pair, field, held):
    q = place[0] & 3
    for k, ref in enumerate((mine, one, two, three)):
        held[q ^ k] = ref[...]
    left = jnp.concatenate([held[0], held[2]], axis=0)
    right = jnp.concatenate([held[1], held[3]], axis=0)
    raised = dot(left, up[0, 0]) + dot(right, up[0, 1])
    field[0] = dot(held[q ^ 2], coupling[0, 0]) + dot(held[q ^ 3], coupling[0, 1])
    pair[...] = raised.astype(BF).reshape(2, R, K)


def level_body(h, place, mine, one, two, three, up, coupling, _, pair, field, held, above):
    q = place[0] >> h
    s = (q >> 1) & 3
    for k, ref in enumerate((mine, one, two, three)):
        held[pl.ds(2 * (s ^ k), 2)] = ref[...]
    left = jnp.concatenate([held[2 * i] for i in range(4)], axis=0)
    right = jnp.concatenate([held[2 * i + 1] for i in range(4)], axis=0)
    raised = dot(left, up[h, 0]) + dot(right, up[h, 1])
    far = (q & 7) ^ 2
    low_field = dot(held[far], coupling[h, 0]) + dot(held[far ^ 1], coupling[h, 1])
    left = jnp.concatenate([raised[0:R], raised[2 * R : 3 * R]], axis=0)
    right = jnp.concatenate([raised[R : 2 * R], raised[3 * R :]], axis=0)
    top = dot2(left, up[h + 1, 0]) + dot2(right, up[h + 1, 1])
    above[...] = raised.reshape(4, R, K)
    pair[...] = top.astype(BF).reshape(2, R, K)
    field[0] = low_field
    far = s ^ 2
    field[1] = dot2(above[far], coupling[h + 1, 0]) + dot2(above[far ^ 1], coupling[h + 1, 1])


def level(h, place, mine, others, up, coupling, order):
    bottom = h < 0
    out = pl.pallas_call(
        bottom_body if bottom else lambda *refs: level_body(h, *refs),
        in_specs=[SMEM] + [VMEM] * 6 + ([] if bottom else [ANY]),
        out_specs=[VMEM, VMEM],
        out_shape=[sds((2, R, K), BF), sds((1 if bottom else 2, R, K), F32)],
        scratch_shapes=[pltpu.VMEM((4, R, K), BF)]
        if bottom
        else [pltpu.VMEM((8, R, K), BF), pltpu.VMEM((4, R, K), F32)],
        compiler_params=params(),
        name="coarse_levels",
    )
    return out(place, mine, *others, up, coupling, *order)


def couple_body(codes, box_codes, place, matrices, box_matrices, f0, f12, f34, f56, down, coupling, left, mine, right, leaf_field, box_field, base, tip, table, low, high, sems):
    blocks = SENT - LD
    copies = load(
        [
            pltpu.make_async_copy(src.at[pl.ds(LD, blocks)], table.at[pl.ds(n * blocks, blocks)], sems.at[n])
            for n, src in enumerate((left, mine, right))
        ]
    )
    me = place[0]
    fields = (f0[0], f12[0], f12[1], f34[0], f34[1], f56[0], f56[1])
    total = fields[6]
    chain = down[6, (me >> 6) & 1].astype(F32)
    for h in range(5, -1, -1):
        both = dot2(jnp.concatenate([total, chain], axis=0), down[h, (me >> h) & 1])
        total = fields[h] + both[:R]
        chain = both[R:]
    chain_high = chain.astype(BF)
    chain_low = (chain - chain_high.astype(F32)).astype(BF)
    for i in range(2):
        product = dot(coupling[7, i], chain_high) + dot(coupling[7, i], chain_low)
        upper = product.astype(BF)
        tip[i, 0] = upper
        tip[i, 1] = (product - upper.astype(F32)).astype(BF)
    base[...] = total
    for copy in copies:
        copy.wait()
    first = lax.broadcasted_iota(jnp.int32, (R, 2 * K), 1) < K
    for n in range(3):
        for group in range(PAIRS // 5):
            ready = []
            for i in range(5 * group, 5 * group + 5):
                x = jnp.concatenate(
                    [table[n * blocks + b, r : r + 16, :] for b, r in coef_places(i)], axis=0
                ).astype(F32)
                y = pltpu.roll(x, K, 1)
                ready.append(
                    [
                        jnp.where(first, x, 0.0).astype(BF),
                        jnp.where(first, y, 0.0).astype(BF),
                        jnp.where(first, 0.0, y).astype(BF),
                        jnp.where(first, 0.0, x).astype(BF),
                    ]
                )
            for i in range(5):
                at = 2 * (n * PAIRS + 5 * group + i)
                low[at], low[at + 1], high[at], high[at + 1] = ready[i]

    def gather(codes, row, mats, width):
        total = jnp.zeros((R, K), F32)
        for g in range(width // 4):
            c = [codes[row, 4 * g + i] for i in range(4)]
            s = [x & 255 for x in c]
            vec = jnp.concatenate([low[s[0]] + high[s[1]], low[s[2]] + high[s[3]]], axis=1)
            mat = jnp.concatenate([mats[x >> 8] for x in c], axis=0)
            total = total + dot(vec, mat)
        return total

    def step(it, _):
        rows = [it * 8 + u for u in range(8)]
        got = [gather(codes, row, matrices, ADM) for row in rows]
        for row, value in zip(rows, got):
            leaf_field[row] = value
        return 0

    lax.fori_loop(0, LD // 8, step, 0)
    got = [gather(box_codes, box, box_matrices, ADMB) for box in range(BX)]
    for box in range(BX):
        box_field[box] = got[box]


def couple(codes, box_codes, place, matrices, box_matrices, fields, down, coupling, sents):
    return pl.pallas_call(
        couple_body,
        in_specs=[SMEM] * 3 + [VMEM] * 8 + [ANY] * 3,
        out_specs=[VMEM] * 4,
        out_shape=[
            sds((LD, R, K), F32),
            sds((BX, R, K), F32),
            sds((R, K), F32),
            sds((2, 2, K, K), BF),
        ],
        scratch_shapes=[
            pltpu.VMEM((3 * (SENT - LD), ROWS, M), BF),
            pltpu.VMEM((6 * PAIRS, R, 2 * K), BF),
            pltpu.VMEM((6 * PAIRS, R, 2 * K), BF),
            pltpu.SemaphoreType.DMA((3,)),
        ],
        compiler_params=params(),
        cost_estimate=pl.CostEstimate(flops=1 << 30, bytes_accessed=1 << 20, transcendentals=0),
        name="couple_levels",
    )(codes, box_codes, place, matrices, box_matrices, *fields, down, coupling, *sents)


def final_body(place, other, base, tip, parents, leaf_field, box_field, box_down, leaf_down, basis, near_part, out, boxes):
    q = (place[0] >> 7) & 1
    total = base[...]
    for i in range(2):
        node = other[q ^ i]
        total = total + (dot(node, tip[i, 0]) + dot(node, tip[i, 1]))
    group = total.astype(BF)
    got = [(box_field[box] + dot(group, box_down[box])).astype(BF) for box in range(BX)]
    for box in range(BX):
        boxes[box] = got[box]
    for part in range(LD // 8):
        leaves = range(8 * part, 8 * part + 8)
        field = [
            (leaf_field[leaf] + dot(boxes[parents[leaf]], leaf_down[leaf])).astype(BF) for leaf in leaves
        ]
        got = [
            near_part[leaf] + dot(field[i], basis[:, pl.ds(leaf * M, M)]) for i, leaf in enumerate(leaves)
        ]
        for i, leaf in enumerate(leaves):
            out[:, pl.ds(leaf * M, M)] = got[i]


def finish(place, other, base, tip, parents, fields, box_down, leaf_down, basis, near_part):
    return pl.pallas_call(
        final_body,
        in_specs=[SMEM] + [VMEM] * 3 + [SMEM] + [VMEM] * 6,
        out_specs=VMEM,
        out_shape=sds((R, LD * M), F32),
        scratch_shapes=[pltpu.VMEM((BX, R, K), BF)],
        compiler_params=params(),
        name="group_to_points",
    )(place, other, base, tip, parents, *fields, box_down, leaf_down, basis, near_part)


def exchange(x):
    count = lax.axis_size(AXES)
    left = lax.ppermute(x, AXES, [(i, i + 1) for i in range(count - 1)])
    right = lax.ppermute(x, AXES, [(i + 1, i) for i in range(count - 1)])
    return left, right


def partners(x, bit, ways):
    count = lax.axis_size(AXES)
    return [lax.ppermute(x, AXES, [(i, i ^ (k << bit)) for i in range(count)]) for k in range(1, ways)]


def local(
    charges,
    points,
    leaf_basis,
    leaf_parent,
    leaf_up,
    leaf_down,
    box_up,
    box_down,
    top_up,
    top_down,
    top_coupling,
    leaf_sources,
    leaf_classes,
    leaf_coupling,
    box_sources,
    box_classes,
    box_coupling,
    near_leaves,
    near_count,
):
    device = lax.axis_index(AXES)
    place = device.astype(jnp.int32).reshape(1)
    parents = leaf_parent[0]

    rel = near_leaves - device * LD
    used = jnp.arange(NEAR, dtype=jnp.int32)[None, :] < near_count[:, None]
    side = jnp.where(rel < 0, 2, jnp.where(rel < LD, 1, 4))
    row = rel + jnp.where(rel < 0, LD, jnp.where(rel < LD, 0, -LD))
    leaf_ids = jnp.arange(LD, dtype=jnp.int32)[:, None]
    code = row | leaf_ids << 8 | jnp.where(used, side, 0) << 16

    sent, target, ascent, own, left, right, sizes = first(
        charges, points, leaf_basis, leaf_up, box_up, parents, code
    )
    expand = jnp.asarray(expansion(), BF)

    pair, f0 = level(-1, place, ascent, partners(ascent, 0, 4), top_up, top_coupling, ())
    sent_left, sent_right = exchange(sent)
    others = partners(pair, 2, 4)
    near_part = near(0, sizes, own, target, expand, sent, (f0,))
    pair, f12 = level(1, place, pair, others, top_up, top_coupling, (near_part,))
    others = partners(pair, 4, 4)
    near_part = near(1, sizes, left, target, expand, sent_left, (near_part, f12))
    pair, f34 = level(3, place, pair, others, top_up, top_coupling, (near_part,))
    others = partners(pair, 6, 4)
    near_part = near(2, sizes, right, target, expand, sent_right, (near_part, f34))
    pair, f56 = level(5, place, pair, others, top_up, top_coupling, (near_part,))
    (other,) = partners(pair, 8, 2)

    def table_row(sources, classes, width, start):
        rel = sources - (device - 1) * width
        block = (rel >= width).astype(jnp.int32) + (rel >= 2 * width).astype(jnp.int32)
        return rel + block * (2 * PAIRS - width) + start | classes << 8

    codes = table_row(leaf_sources, leaf_classes, LD, 0)
    box_codes = table_row(box_sources, box_classes, BX, LD)
    leaf_field, box_field, base, tip = couple(
        codes,
        box_codes,
        place,
        leaf_coupling,
        box_coupling,
        (f0, f12, f34, f56),
        top_down,
        top_coupling,
        (sent_left, sent, sent_right),
    )
    return finish(
        place, other, base, tip, parents, (leaf_field, box_field), box_down, leaf_down, leaf_basis, near_part
    )


def solution(mesh):
    split = P(AXES)
    return jax.shard_map(
        local,
        mesh=mesh,
        in_specs=(
            P(None, AXES),
            P(None, AXES),
            P(None, AXES),
            split,
            split,
            split,
            split,
            split,
            P(),
            P(),
            P(),
            split,
            split,
            P(),
            split,
            split,
            P(),
            split,
            split,
        ),
        out_specs=P(None, AXES),
        check_vma=False,
    )
```

```python
import math

import jax
import jax.numpy as jnp
import numpy as np
from jax import lax
from jax.experimental import pallas as pl
from jax.experimental.pallas import tpu as pltpu
from jax.sharding import PartitionSpec as P

BF = jnp.bfloat16
F32 = jnp.float32
AXES = ("box", "rhs")

R = 64
K = 64
M = 128
LD = 24
BX = 6
ADM = 16
ADMB = 8
NEAR = 27
FR = 16
ROWS = R + FR
FX = 32
UNROLL = 8
LOW = 32
PAIRS = (LD + BX) // 2
SENT = LD + PAIRS * R // ROWS
SLOTS = LD * (NEAR + 1) + 2 * UNROLL

DELTA2 = 0.0001
INV_SCALE = 2.0 * math.sqrt(NEAR * M)
CENTRE = 1.1

PARTS = ((0, 0), (0, 1), (0, 2), (1, 0), (1, 1), (1, 2), (2, 0), (2, 1))

VMEM = pl.BlockSpec(memory_space=pltpu.VMEM)
SMEM = pl.BlockSpec(memory_space=pltpu.SMEM)
ANY = pl.BlockSpec(memory_space=pl.ANY)
HBM = pl.BlockSpec(memory_space=pltpu.HBM)


def params(mib=24):
    return pltpu.CompilerParams(vmem_limit_bytes=mib * 1024 * 1024)


def sds(shape, dtype):
    return jax.ShapeDtypeStruct(shape, dtype)


def dot(a, b):
    return jnp.dot(a, b, preferred_element_type=F32)


def dot_nt(a, b):
    return lax.dot_general(a, b, (((1,), (1,)), ((), ())), preferred_element_type=F32)


def dot2(x, m):
    hi = x.astype(BF)
    lo = (x - hi.astype(F32)).astype(BF)
    return dot(hi, m) + dot(lo, m)


def expansion(leaf):
    row = lax.broadcasted_iota(jnp.int32, (8 * FR, M), 0) - FR * leaf
    e = lax.broadcasted_iota(jnp.int32, (8 * FR, M), 1)
    third = (e * 43) >> 7
    part = jnp.where(e < 9, 0, jnp.where(e < 18, 3, 6))
    source = jnp.where(e < 24, part + e - 3 * third, jnp.where(e < 27, e - 15, jnp.where(e < 30, 12, -M)))
    return jnp.where(row == source, 1.0, 0.0).astype(BF)


def split3(x):
    hi = x.astype(BF).astype(F32)
    rest = x - hi
    mid = rest.astype(BF).astype(F32)
    return hi, mid, rest - mid


def load(copies):
    for copy in copies:
        copy.start()
    return copies


def first_body(charges_in, points_in, basis_in, leaf_up_in, box_up_in, parents, code, sent, target, ascent, own, left, right, sizes, charges, points, basis, leaf_up, box_up, feat, wide, acc, sems):
    moves = ((points_in, points), (charges_in, charges), (basis_in, basis), (leaf_up_in, leaf_up), (box_up_in, box_up))
    copies = load([pltpu.make_async_copy(a, b, sems.at[n]) for n, (a, b) in enumerate(moves)])
    acc[...] = jnp.zeros(acc.shape, F32)
    copies[1].wait()
    copies[2].wait()
    copies[3].wait()
    lists = (own, left, right)
    at = [jnp.int32(0)] * 3
    for group in range(LD // 8):
        leaves = range(8 * group, 8 * group + 8)
        c = [dot_nt(charges[:, pl.ds(leaf * M, M)], basis[:, pl.ds(leaf * M, M)]) for leaf in leaves]
        raised = [dot(c[i].astype(BF), leaf_up[leaf]) for i, leaf in enumerate(leaves)]
        for leaf in leaves:
            for part in range(0, NEAR, 9):
                row = [code[leaf, part + s] for s in range(9)]
                for x in row:
                    for n in range(3):
                        lists[n][at[n]] = x
                        at[n] = at[n] + ((x >> (16 + n)) & 1)
            for n in range(3):
                lists[n][at[n]] = leaf << 8 | LD
                at[n] = (at[n] + 1) & -2
        for i in range(0, 8, 2):
            put_coef(sent, (8 * group + i) // 2, jnp.concatenate([c[i], c[i + 1]], axis=1).astype(BF))
        for i, leaf in enumerate(leaves):
            acc[parents[leaf]] += raised[i]
    for n in range(3):
        for i in range(2 * UNROLL):
            lists[n][at[n] + i] = LD << 8 | LD
        sizes[n] = (at[n] // 2 + UNROLL - 1) // UNROLL
    copies[4].wait()
    copies[0].wait()
    boxes = [acc[box] for box in range(BX)]
    raised = [dot(boxes[box].astype(BF), box_up[box]) for box in range(BX)]
    ascent[...] = (raised[0] + raised[1] + (raised[2] + raised[3]) + (raised[4] + raised[5])).astype(BF)
    for box in range(0, BX, 2):
        put_coef(sent, (LD + box) // 2, jnp.concatenate([boxes[box], boxes[box + 1]], axis=1).astype(BF))

    p = (points[...] - CENTRE) * INV_SCALE
    parts = split3(p)
    norm = p[0:1] * p[0:1] + p[1:2] * p[1:2] + p[2:3] * p[2:3]
    source_norm = split3(norm)
    target_norm = split3(norm + DELTA2 * INV_SCALE * INV_SCALE)
    feat[...] = jnp.zeros(feat.shape, F32)
    wide[...] = jnp.zeros(wide.shape, F32)
    one = jnp.ones(norm.shape, F32)
    for a in range(3):
        feat[3 * a : 3 * a + 3, :] = parts[a]
        feat[9 + a : 10 + a, :] = source_norm[a]
    feat[12:13, :] = one
    for n, (_, b) in enumerate(PARTS):
        wide[3 * n : 3 * n + 3, :] = -2.0 * parts[b]
    base = 3 * len(PARTS)
    for a in range(3):
        wide[base + a : base + a + 1, :] = one
        wide[base + 3 + a : base + 4 + a, :] = target_norm[a]
    turned = []
    for o in range(LD // 8):
        rows = jnp.concatenate([feat[:, pl.ds((8 * o + i) * M, M)] for i in range(8)], axis=0)
        turned.append(rows.T.astype(BF))
    for leaf in range(LD):
        cols = pl.ds(leaf * M, M)
        sent[leaf, 0:R, :] = charges[:, cols]
        i = leaf % 8
        sent[leaf, R:ROWS, :] = turned[leaf // 8][FR * i : FR * (i + 1), :]
        target[leaf, :, :] = wide[:, cols].astype(BF)


def coef_places(pair):
    rows = [pair * R + 16 * i for i in range(R // 16)]
    return [(r // ROWS, r % ROWS) for r in rows]


def put_coef(sent, pair, value):
    for i, (block, row) in enumerate(coef_places(pair)):
        sent[LD + block, row : row + 16, :] = value[16 * i : 16 * i + 16]


def first(charges, points, basis, leaf_up, box_up, parents, code):
    return pl.pallas_call(
        first_body,
        in_specs=[HBM] * 5 + [SMEM, SMEM],
        out_specs=[VMEM] * 3 + [SMEM] * 4,
        out_shape=[
            sds((SENT, ROWS, M), BF),
            sds((LD, FX, M), BF),
            sds((R, K), BF),
            sds((SLOTS,), jnp.int32),
            sds((SLOTS,), jnp.int32),
            sds((SLOTS,), jnp.int32),
            sds((3,), jnp.int32),
        ],
        scratch_shapes=[
            pltpu.VMEM((R, LD * M), BF),
            pltpu.VMEM((3, LD * M), F32),
            pltpu.VMEM((K, LD * M), BF),
            pltpu.VMEM((LD, K, K), BF),
            pltpu.VMEM((BX, K, K), BF),
            pltpu.VMEM((FR, LD * M), F32),
            pltpu.VMEM((FX, LD * M), F32),
            pltpu.VMEM((BX, R, K), F32),
            pltpu.SemaphoreType.DMA((5,)),
        ],
        compiler_params=params(60),
        name="points_to_group",
    )(charges, points, basis, leaf_up, box_up, parents, code)


def near_body(which, sizes, slots, target, source, *rest):
    if which:
        start_from, _, acc, table, feats, sem = rest
    else:
        acc, table, feats, sem = rest
    copy = pltpu.make_async_copy(source.at[pl.ds(0, LD)], table.at[pl.ds(0, LD)], sem)
    copy.start()
    if which:
        acc[...] = start_from[...]
    else:
        acc[...] = jnp.zeros(acc.shape, F32)
    table[LD] = jnp.zeros((ROWS, M), BF)
    lane = lax.broadcasted_iota(jnp.int32, (M, M), 1)
    ones = 3 * len(PARTS) + 3
    feats[LD] = jnp.where((lane >= ones) & (lane < ones + 3), 1.0, 0.0).astype(BF)
    copy.wait()
    expand = [expansion(i) for i in range(8)]
    for o in range(LD // 8):
        rows = jnp.concatenate([table[8 * o + i, R:ROWS, :] for i in range(8)], axis=0)
        spread = [dot(rows, expand[i]).astype(BF) for i in range(8)]
        for i in range(8):
            feats[8 * o + i] = spread[i]
    pad = jnp.zeros((M - FX, M), BF)

    def step(it, _):
        t, kernels, weights = [], [], []
        for u in range(UNROLL):
            at = (it * UNROLL + u) * 2
            first, second = slots[at], slots[at + 1]
            s0, s1 = first & 255, second & 255
            t.append((first >> 8) & 255)
            rows = jnp.concatenate([feats[s0], feats[s1]], axis=0)
            square = dot(rows, jnp.concatenate([target[jnp.minimum(t[u], LD - 1)], pad], axis=0))
            kernels.append(lax.rsqrt(square).astype(BF))
            weights.append(jnp.concatenate([table[s0, 0:R, :], table[s1, 0:R, :]], axis=1))
        terms = [dot(weights[u], kernels[u]) for u in range(UNROLL)]
        for u in range(UNROLL):
            acc[t[u]] += terms[u]
        return 0

    lax.fori_loop(0, sizes[which], step, 0)


def near(which, sizes, slots, target, source, extra):
    pairs = 100
    return pl.pallas_call(
        lambda *refs: near_body(which, *refs),
        in_specs=[SMEM, SMEM, VMEM, ANY] + ([VMEM, ANY] if which else []),
        out_specs=VMEM,
        out_shape=sds((LD + 1, R, M), F32),
        scratch_shapes=[
            pltpu.VMEM((LD + 1, ROWS, M), BF),
            pltpu.VMEM((LD + 1, M, M), BF),
            pltpu.SemaphoreType.DMA,
        ],
        compiler_params=params(),
        cost_estimate=pl.CostEstimate(
            flops=pairs * 2 * 256 * 128 * 320, bytes_accessed=2 << 20, transcendentals=pairs << 15
        ),
        name=("near_own", "near_left", "near_right")[which],
    )(sizes, slots, target, source, *extra)


def raise_nodes(nodes, matrices):
    count = nodes.shape[0] // 2
    left = jnp.concatenate([nodes[2 * i] for i in range(count)], axis=0)
    right = jnp.concatenate([nodes[2 * i + 1] for i in range(count)], axis=0)
    mul = dot if nodes.dtype == BF else dot2
    return (mul(left, matrices[0]) + mul(right, matrices[1])).reshape(count, R, K)


def low_body(place, nodes, up, coupling, _, top, field, held):
    levels = [nodes[...]]
    for h in range(4):
        levels.append(raise_nodes(levels[h], (up[h, 0], up[h, 1])))
    top[...] = levels[4].astype(BF)
    start = 0
    for h in range(1, 4):
        held[start : start + (LOW >> h)] = levels[h]
        start += LOW >> h
    me = place[0] & (LOW - 1)
    near = me ^ 2
    out = [dot(nodes[near], coupling[0, 0]) + dot(nodes[near ^ 1], coupling[0, 1])]
    start = 0
    for h in range(1, 4):
        near = ((me >> h) ^ 2) + start
        far = ((me >> h) ^ 3) + start
        out.append(dot2(held[near], coupling[h, 0]) + dot2(held[far], coupling[h, 1]))
        start += LOW >> h
    for h in range(4):
        field[h] = out[h]


def low_tree(place, nodes, up, coupling, order):
    return pl.pallas_call(
        low_body,
        in_specs=[SMEM, VMEM, VMEM, VMEM, ANY],
        out_specs=[VMEM, VMEM],
        out_shape=[sds((2, R, K), BF), sds((4, R, K), F32)],
        scratch_shapes=[pltpu.VMEM((LOW, R, K), F32)],
        compiler_params=params(),
        name="coarse_low",
    )(place, nodes, up, coupling, order)


def split2(x):
    hi = x.astype(BF)
    return hi, (x - hi.astype(F32)).astype(BF)


def couple_body(codes, box_codes, place, matrices, box_matrices, low_field, down, coupling, left, mine, right, leaf_field, box_field, base, tip, table, low, high, sems):
    blocks = SENT - LD
    copies = load(
        [
            pltpu.make_async_copy(src.at[pl.ds(LD, blocks)], table.at[pl.ds(n * blocks, blocks)], sems.at[n])
            for n, src in enumerate((left, mine, right))
        ]
    )
    me = place[0]
    total = low_field[3]
    chain = down[3, (me >> 3) & 1].astype(F32)
    for h in range(2, -1, -1):
        both = dot2(jnp.concatenate([total, chain], axis=0), down[h, (me >> h) & 1])
        total = low_field[h] + both[:R]
        chain = both[R:]
    tips = []
    for h in range(4, 8):
        hi, lo = split2(chain)
        stack = jnp.concatenate([coupling[h, 0], coupling[h, 1], down[min(h, 6), (me >> h) & 1]], axis=0)
        product = dot(stack, hi) + dot(stack, lo)
        tips.append((split2(product[0:K]), split2(product[K : 2 * K])))
        chain = product[2 * K :]
    base[...] = total
    for h in range(4):
        for i in range(2):
            for n in range(2):
                tip[h, i, n] = tips[h][i][n]
    for copy in copies:
        copy.wait()
    first = lax.broadcasted_iota(jnp.int32, (R, 2 * K), 1) < K
    for n in range(3):
        for group in range(PAIRS // 5):
            ready = []
            for i in range(5 * group, 5 * group + 5):
                x = jnp.concatenate(
                    [table[n * blocks + b, r : r + 16, :] for b, r in coef_places(i)], axis=0
                ).astype(F32)
                y = pltpu.roll(x, K, 1)
                ready.append(
                    [
                        jnp.where(first, x, 0.0).astype(BF),
                        jnp.where(first, y, 0.0).astype(BF),
                        jnp.where(first, 0.0, y).astype(BF),
                        jnp.where(first, 0.0, x).astype(BF),
                    ]
                )
            for i in range(5):
                at = 2 * (n * PAIRS + 5 * group + i)
                low[at], low[at + 1], high[at], high[at + 1] = ready[i]

    def gather(codes, row, mats, width):
        total = jnp.zeros((R, K), F32)
        for g in range(width // 4):
            c = [codes[row, 4 * g + i] for i in range(4)]
            s = [x & 255 for x in c]
            vec = jnp.concatenate([low[s[0]] + high[s[1]], low[s[2]] + high[s[3]]], axis=1)
            mat = jnp.concatenate([mats[x >> 8] for x in c], axis=0)
            total = total + dot(vec, mat)
        return total

    def step(it, _):
        rows = [it * 8 + u for u in range(8)]
        got = [gather(codes, row, matrices, ADM) for row in rows]
        for row, value in zip(rows, got):
            leaf_field[row] = value
        return 0

    lax.fori_loop(0, LD // 8, step, 0)
    got = [gather(box_codes, box, box_matrices, ADMB) for box in range(BX)]
    for box in range(BX):
        box_field[box] = got[box]


def couple(codes, box_codes, place, matrices, box_matrices, low_field, down, coupling, sents):
    return pl.pallas_call(
        couple_body,
        in_specs=[SMEM] * 3 + [VMEM] * 5 + [ANY] * 3,
        out_specs=[VMEM] * 4,
        out_shape=[
            sds((LD, R, K), F32),
            sds((BX, R, K), F32),
            sds((R, K), F32),
            sds((4, 2, 2, K, K), BF),
        ],
        scratch_shapes=[
            pltpu.VMEM((3 * (SENT - LD), ROWS, M), BF),
            pltpu.VMEM((6 * PAIRS, R, 2 * K), BF),
            pltpu.VMEM((6 * PAIRS, R, 2 * K), BF),
            pltpu.SemaphoreType.DMA((3,)),
        ],
        compiler_params=params(),
        cost_estimate=pl.CostEstimate(flops=1 << 30, bytes_accessed=1 << 20, transcendentals=0),
        name="couple_levels",
    )(codes, box_codes, place, matrices, box_matrices, low_field, down, coupling, *sents)


def final_body(place, nodes, up, base, tip, parents, leaf_field, box_field, box_down, leaf_down, basis, near_part, out, boxes, held):
    block = nodes[...].reshape(LOW, R, K)
    start = 0
    levels = [block]
    for h in range(3):
        levels.append(raise_nodes(levels[h], (up[4 + h, 0], up[4 + h, 1])))
    for h in range(4):
        held[start : start + (LOW >> h)] = levels[h].astype(F32)
        start += LOW >> h
    me = (place[0] >> 4) & (LOW - 1)
    total = base[...]
    start = 0
    for h in range(4):
        for i in range(2):
            hi, lo = split2(held[((me >> h) ^ (2 + i)) + start])
            total = total + (dot(hi, tip[h, i, 0]) + dot(hi, tip[h, i, 1]) + dot(lo, tip[h, i, 0]))
        start += LOW >> h
    group = total.astype(BF)
    got = [(box_field[box] + dot(group, box_down[box])).astype(BF) for box in range(BX)]
    for box in range(BX):
        boxes[box] = got[box]
    for part in range(LD // 8):
        leaves = range(8 * part, 8 * part + 8)
        field = [
            (leaf_field[leaf] + dot(boxes[parents[leaf]], leaf_down[leaf])).astype(BF) for leaf in leaves
        ]
        got = [
            near_part[leaf] + dot(field[i], basis[:, pl.ds(leaf * M, M)]) for i, leaf in enumerate(leaves)
        ]
        for i, leaf in enumerate(leaves):
            out[:, pl.ds(leaf * M, M)] = got[i]


def finish(place, nodes, up, base, tip, parents, fields, box_down, leaf_down, basis, near_part):
    return pl.pallas_call(
        final_body,
        in_specs=[SMEM] + [VMEM] * 4 + [SMEM] + [VMEM] * 6,
        out_specs=VMEM,
        out_shape=sds((R, LD * M), F32),
        scratch_shapes=[pltpu.VMEM((BX, R, K), BF), pltpu.VMEM((2 * LOW, R, K), F32)],
        compiler_params=params(),
        name="group_to_points",
    )(place, nodes, up, base, tip, parents, *fields, box_down, leaf_down, basis, near_part)


def exchange(x):
    count = lax.axis_size(AXES)
    left = lax.ppermute(x, AXES, [(i, i + 1) for i in range(count - 1)])
    right = lax.ppermute(x, AXES, [(i + 1, i) for i in range(count - 1)])
    return left, right


def gather_groups(x, groups):
    many = jnp.broadcast_to(x[None], (len(groups[0]),) + x.shape)
    return lax.all_to_all(many, AXES, 0, 0, axis_index_groups=groups, tiled=True)


def local(
    charges,
    points,
    leaf_basis,
    leaf_parent,
    leaf_up,
    leaf_down,
    box_up,
    box_down,
    top_up,
    top_down,
    top_coupling,
    leaf_sources,
    leaf_classes,
    leaf_coupling,
    box_sources,
    box_classes,
    box_coupling,
    near_leaves,
    near_count,
):
    device = lax.axis_index(AXES)
    place = device.astype(jnp.int32).reshape(1)
    parents = leaf_parent[0]

    rel = near_leaves - device * LD
    used = jnp.arange(NEAR, dtype=jnp.int32)[None, :] < near_count[:, None]
    side = jnp.where(rel < 0, 2, jnp.where(rel < LD, 1, 4))
    row = rel + jnp.where(rel < 0, LD, jnp.where(rel < LD, 0, -LD))
    leaf_ids = jnp.arange(LD, dtype=jnp.int32)[:, None]
    code = row | leaf_ids << 8 | jnp.where(used, side, 0) << 16

    sent, target, ascent, own, left, right, sizes = first(
        charges, points, leaf_basis, leaf_up, box_up, parents, code
    )

    blocks = lax.axis_size(AXES) // LOW
    low_groups = [[b * LOW + i for i in range(LOW)] for b in range(blocks)]
    high_groups = [[b * LOW + i for b in range(blocks)] for i in range(LOW)]

    low_nodes = gather_groups(ascent, low_groups)
    sent_left, sent_right = exchange(sent)
    near_part = near(0, sizes, own, target, sent, ())
    top, low_field = low_tree(place, low_nodes, top_up, top_coupling, near_part)
    high_nodes = gather_groups(top, high_groups)
    near_part = near(1, sizes, left, target, sent_left, (near_part, low_field))
    near_part = near(2, sizes, right, target, sent_right, (near_part, low_field))

    def table_row(sources, classes, width, start):
        rel = sources - (device - 1) * width
        block = (rel >= width).astype(jnp.int32) + (rel >= 2 * width).astype(jnp.int32)
        return rel + block * (2 * PAIRS - width) + start | classes << 8

    codes = table_row(leaf_sources, leaf_classes, LD, 0)
    box_codes = table_row(box_sources, box_classes, BX, LD)
    leaf_field, box_field, base, tip = couple(
        codes,
        box_codes,
        place,
        leaf_coupling,
        box_coupling,
        low_field,
        top_down,
        top_coupling,
        (sent_left, sent, sent_right),
    )
    return finish(
        place, high_nodes, top_up, base, tip, parents, (leaf_field, box_field), box_down, leaf_down, leaf_basis, near_part
    )


def solution(mesh):
    split = P(AXES)
    return jax.shard_map(
        local,
        mesh=mesh,
        in_specs=(
            P(None, AXES),
            P(None, AXES),
            P(None, AXES),
            split,
            split,
            split,
            split,
            split,
            P(),
            P(),
            P(),
            split,
            split,
            P(),
            split,
            split,
            P(),
            split,
            split,
        ),
        out_specs=P(None, AXES),
        check_vma=False,
    )
```

```python
import math

import jax
import jax.numpy as jnp
import numpy as np
from jax import lax
from jax.experimental import pallas as pl
from jax.experimental.pallas import tpu as pltpu
from jax.sharding import PartitionSpec as P

BF = jnp.bfloat16
F32 = jnp.float32
AXES = ("box", "rhs")

R = 64
K = 64
M = 128
LD = 24
BX = 6
ADM = 16
ADMB = 8
NEAR = 27
FR = 16
ROWS = R + FR
FX = 32
UNROLL = 16
LOW = 32
PAIRS = (LD + BX) // 2
SENT = LD + PAIRS * R // ROWS
SLOTS = LD * (NEAR + 1) + 2 * UNROLL + 32
ALL = 3 * LD

DELTA2 = 0.0001
INV_SCALE = 2.0 * math.sqrt(NEAR * M)
CENTRE = 1.1

PARTS = ((0, 0), (0, 1), (0, 2), (1, 0), (1, 1), (1, 2), (2, 0), (2, 1))

VMEM = pl.BlockSpec(memory_space=pltpu.VMEM)
SMEM = pl.BlockSpec(memory_space=pltpu.SMEM)
ANY = pl.BlockSpec(memory_space=pl.ANY)
HBM = pl.BlockSpec(memory_space=pltpu.HBM)


def params(mib=24):
    return pltpu.CompilerParams(vmem_limit_bytes=mib * 1024 * 1024)


def sds(shape, dtype):
    return jax.ShapeDtypeStruct(shape, dtype)


def dot(a, b):
    return jnp.dot(a, b, preferred_element_type=F32)


def dot_nt(a, b):
    return lax.dot_general(a, b, (((1,), (1,)), ((), ())), preferred_element_type=F32)


def dot2(x, m):
    hi = x.astype(BF)
    lo = (x - hi.astype(F32)).astype(BF)
    return dot(hi, m) + dot(lo, m)


def expansion(leaf):
    row = lax.broadcasted_iota(jnp.int32, (8 * FR, M), 0) - FR * leaf
    e = lax.broadcasted_iota(jnp.int32, (8 * FR, M), 1)
    third = (e * 43) >> 7
    part = jnp.where(e < 9, 0, jnp.where(e < 18, 3, 6))
    source = jnp.where(e < 24, part + e - 3 * third, jnp.where(e < 27, e - 15, jnp.where(e < 30, 12, -M)))
    return jnp.where(row == source, 1.0, 0.0).astype(BF)


def split3(x):
    hi = x.astype(BF).astype(F32)
    rest = x - hi
    mid = rest.astype(BF).astype(F32)
    return hi, mid, rest - mid


def load(copies):
    for copy in copies:
        copy.start()
    return copies


def first_body(charges_in, points_in, basis_in, leaf_up_in, box_up_in, parents, sent, target, ascent, charges, points, basis, leaf_up, box_up, feat, wide, acc, sems):
    moves = ((points_in, points), (charges_in, charges), (basis_in, basis), (leaf_up_in, leaf_up), (box_up_in, box_up))
    copies = load([pltpu.make_async_copy(a, b, sems.at[n]) for n, (a, b) in enumerate(moves)])
    acc[...] = jnp.zeros(acc.shape, F32)
    copies[1].wait()
    copies[2].wait()
    copies[3].wait()
    for group in range(LD // 8):
        leaves = range(8 * group, 8 * group + 8)
        c = [dot_nt(charges[:, pl.ds(leaf * M, M)], basis[:, pl.ds(leaf * M, M)]) for leaf in leaves]
        raised = [dot(c[i].astype(BF), leaf_up[leaf]) for i, leaf in enumerate(leaves)]
        for i in range(0, 8, 2):
            put_coef(sent, (8 * group + i) // 2, jnp.concatenate([c[i], c[i + 1]], axis=1).astype(BF))
        for i, leaf in enumerate(leaves):
            acc[parents[leaf]] += raised[i]
    copies[4].wait()
    copies[0].wait()
    boxes = [acc[box] for box in range(BX)]
    raised = [dot(boxes[box].astype(BF), box_up[box]) for box in range(BX)]
    total = raised[0] + raised[1] + (raised[2] + raised[3]) + (raised[4] + raised[5])
    packed = jnp.concatenate([total[: R // 2], total[R // 2 :]], axis=1).astype(BF)
    for i in range(LOW):
        ascent[i] = packed
    for box in range(0, BX, 2):
        put_coef(sent, (LD + box) // 2, jnp.concatenate([boxes[box], boxes[box + 1]], axis=1).astype(BF))

    p = (points[...] - CENTRE) * INV_SCALE
    parts = split3(p)
    norm = p[0:1] * p[0:1] + p[1:2] * p[1:2] + p[2:3] * p[2:3]
    source_norm = split3(norm)
    target_norm = split3(norm + DELTA2 * INV_SCALE * INV_SCALE)
    feat[...] = jnp.zeros(feat.shape, F32)
    wide[...] = jnp.zeros(wide.shape, F32)
    one = jnp.ones(norm.shape, F32)
    for a in range(3):
        feat[3 * a : 3 * a + 3, :] = parts[a]
        feat[9 + a : 10 + a, :] = source_norm[a]
    feat[12:13, :] = one
    for n, (_, b) in enumerate(PARTS):
        wide[3 * n : 3 * n + 3, :] = -2.0 * parts[b]
    base = 3 * len(PARTS)
    for a in range(3):
        wide[base + a : base + a + 1, :] = one
        wide[base + 3 + a : base + 4 + a, :] = target_norm[a]
    turned = []
    for o in range(LD // 8):
        rows = jnp.concatenate([feat[:, pl.ds((8 * o + i) * M, M)] for i in range(8)], axis=0)
        turned.append(rows.T.astype(BF))
    for leaf in range(LD):
        cols = pl.ds(leaf * M, M)
        sent[leaf, 0:R, :] = charges[:, cols]
        i = leaf % 8
        sent[leaf, R:ROWS, :] = turned[leaf // 8][FR * i : FR * (i + 1), :]
        target[leaf, :, :] = wide[:, cols].astype(BF)


def coef_places(pair):
    rows = [pair * R + 16 * i for i in range(R // 16)]
    return [(r // ROWS, r % ROWS) for r in rows]


def put_coef(sent, pair, value):
    for i, (block, row) in enumerate(coef_places(pair)):
        sent[LD + block, row : row + 16, :] = value[16 * i : 16 * i + 16]


def first(charges, points, basis, leaf_up, box_up, parents):
    return pl.pallas_call(
        first_body,
        in_specs=[HBM] * 5 + [SMEM],
        out_specs=[VMEM] * 3,
        out_shape=[
            sds((SENT, ROWS, M), BF),
            sds((LD, FX, M), BF),
            sds((LOW, R // 2, 2 * K), BF),
        ],
        scratch_shapes=[
            pltpu.VMEM((R, LD * M), BF),
            pltpu.VMEM((3, LD * M), F32),
            pltpu.VMEM((K, LD * M), BF),
            pltpu.VMEM((LD, K, K), BF),
            pltpu.VMEM((BX, K, K), BF),
            pltpu.VMEM((FR, LD * M), F32),
            pltpu.VMEM((FX, LD * M), F32),
            pltpu.VMEM((BX, R, K), F32),
            pltpu.SemaphoreType.DMA((5,)),
        ],
        compiler_params=params(60),
        name="points_to_group",
    )(charges, points, basis, leaf_up, box_up, parents)


def twice(m):
    zero = jnp.zeros_like(m)
    return jnp.concatenate([jnp.concatenate([m, zero], axis=1), jnp.concatenate([zero, m], axis=1)], axis=0)


def unpack(x):
    return jnp.concatenate([x[:, :K], x[:, K:]], axis=0)


def raise_nodes(nodes, matrices):
    count = nodes.shape[0] // 2
    left = jnp.concatenate([nodes[2 * i] for i in range(count)], axis=0)
    right = jnp.concatenate([nodes[2 * i + 1] for i in range(count)], axis=0)
    mul = dot if nodes.dtype == BF else dot2
    return (mul(left, twice(matrices[0])) + mul(right, twice(matrices[1]))).reshape(count, R // 2, 2 * K)


def low_body(place, nodes, up, coupling, top, field, held):
    levels = [nodes[...]]
    for h in range(4):
        levels.append(raise_nodes(levels[h], (up[h, 0], up[h, 1])))
    packed = levels[4].astype(BF).reshape(R, 2 * K)
    for i in range(top.shape[0]):
        top[i] = packed
    start = 0
    for h in range(4):
        held[start : start + (LOW >> h)] = levels[h].astype(F32)
        start += LOW >> h
    me = place[0] & (LOW - 1)
    start = 0
    out = []
    for h in range(4):
        q = me >> h
        near, far = unpack(held[(q ^ 2) + start]), unpack(held[(q ^ 3) + start])
        out.append(dot2(near, coupling[h, 0]) + dot2(far, coupling[h, 1]))
        start += LOW >> h
    for h in range(4):
        field[h] = out[h]


def low_tree(place, nodes, up, coupling, blocks):
    return pl.pallas_call(
        low_body,
        in_specs=[SMEM, VMEM, VMEM, VMEM],
        out_specs=[VMEM, VMEM],
        out_shape=[sds((blocks, R, 2 * K), BF), sds((4, R, K), F32)],
        scratch_shapes=[pltpu.VMEM((2 * LOW, R // 2, 2 * K), F32)],
        compiler_params=params(),
        name="coarse_low",
    )(place, nodes, up, coupling)


def split2(x):
    hi = x.astype(BF)
    return hi, (x - hi.astype(F32)).astype(BF)


def fields_body(near_leaves, near_count, leaf_sources, leaf_classes, box_sources, box_classes, place, low_field, down, coupling, target_in, matrices_in, box_matrices_in, left, mine, right, acc, leaf_field, box_field, base, tip, table, coefs, feats, target, matrices, box_matrices, low, high, slots, sems):
    blocks = SENT - LD
    sources = (left, mine, right)
    moves = [(src.at[pl.ds(0, LD)], table.at[pl.ds(n * LD, LD)]) for n, src in enumerate(sources)]
    moves += [(src.at[pl.ds(LD, blocks)], coefs.at[pl.ds(n * blocks, blocks)]) for n, src in enumerate(sources)]
    moves += [(target_in, target), (matrices_in, matrices), (box_matrices_in, box_matrices)]
    copies = load([pltpu.make_async_copy(a, b, sems.at[n]) for n, (a, b) in enumerate(moves)])

    me = place[0]
    at = jnp.int32(0)
    for t in range(LD):
        shift = (t << 8) - (me - 1) * LD
        for part in range(0, NEAR, 9):
            row = [near_leaves[t, part + s] for s in range(9)]
            for s in range(9):
                slots[at + part + s] = row[s] + shift
        slots[at + near_count[t]] = t << 8 | ALL
        at = at + ((near_count[t] + 1) & -2)
    for i in range(2 * UNROLL):
        slots[at + i] = LD << 8 | ALL

    total = low_field[3]
    chain = down[3, (me >> 3) & 1].astype(F32)
    for h in range(2, -1, -1):
        both = dot2(jnp.concatenate([total, chain], axis=0), down[h, (me >> h) & 1])
        total = low_field[h] + both[:R]
        chain = both[R:]
    tips = []
    for h in range(4, 8):
        hi, lo = split2(chain)
        stack = jnp.concatenate([coupling[h, 0], coupling[h, 1], down[min(h, 6), (me >> h) & 1]], axis=0)
        product = dot(stack, hi) + dot(stack, lo)
        tips.append((split2(product[0:K]), split2(product[K : 2 * K])))
        chain = product[2 * K :]
    base[...] = total
    for h in range(4):
        for i in range(2):
            for n in range(2):
                tip[h, i, n] = tips[h][i][n]

    acc[...] = jnp.zeros(acc.shape, F32)
    table[ALL] = jnp.zeros((ROWS, M), BF)
    lane = lax.broadcasted_iota(jnp.int32, (M, M), 1)
    ones = 3 * len(PARTS) + 3
    feats[ALL] = jnp.where((lane >= ones) & (lane < ones + 3), 1.0, 0.0).astype(BF)
    for copy in copies:
        copy.wait()

    first = lax.broadcasted_iota(jnp.int32, (R, 2 * K), 1) < K
    for n in range(3):
        for group in range(PAIRS // 5):
            ready = []
            for i in range(5 * group, 5 * group + 5):
                x = jnp.concatenate(
                    [coefs[n * blocks + b, r : r + 16, :] for b, r in coef_places(i)], axis=0
                ).astype(F32)
                y = pltpu.roll(x, K, 1)
                ready.append(
                    [
                        jnp.where(first, x, 0.0).astype(BF),
                        jnp.where(first, y, 0.0).astype(BF),
                        jnp.where(first, 0.0, y).astype(BF),
                        jnp.where(first, 0.0, x).astype(BF),
                    ]
                )
            for i in range(5):
                at_row = 2 * (5 * group + i)
                row = n * LD + at_row if at_row < LD else ALL + n * BX + at_row - LD
                low[row], low[row + 1], high[row], high[row + 1] = ready[i]

    def gather(sources, classes, row, mats, width, shift):
        total = jnp.zeros((R, K), F32)
        for g in range(width // 4):
            s = [sources[row, 4 * g + i] - shift for i in range(4)]
            vec = jnp.concatenate([low[s[0]] + high[s[1]], low[s[2]] + high[s[3]]], axis=1)
            mat = jnp.concatenate([mats[classes[row, 4 * g + i]] for i in range(4)], axis=0)
            total = total + dot(vec, mat)
        return total

    def couple(it, _):
        rows = [it * 8 + u for u in range(8)]
        got = [gather(leaf_sources, leaf_classes, row, matrices, ADM, (me - 1) * LD) for row in rows]
        for row, value in zip(rows, got):
            leaf_field[row] = value
        return 0

    lax.fori_loop(0, LD // 8, couple, 0)
    got = [gather(box_sources, box_classes, box, box_matrices, ADMB, (me - 1) * BX - ALL) for box in range(BX)]
    for box in range(BX):
        box_field[box] = got[box]

    expand = [expansion(i) for i in range(8)]
    for o in range(ALL // 8):
        rows = jnp.concatenate([table[8 * o + i, R:ROWS, :] for i in range(8)], axis=0)
        spread = [dot(rows, expand[i]).astype(BF) for i in range(8)]
        for i in range(8):
            feats[8 * o + i] = spread[i]
    pad = jnp.zeros((M - FX, M), BF)

    def near(it, _):
        t, kernels, weights = [], [], []
        for u in range(UNROLL):
            place_of = (it * UNROLL + u) * 2
            one, two = slots[place_of], slots[place_of + 1]
            s0, s1 = one & 255, two & 255
            t.append(one >> 8)
            rows = jnp.concatenate([feats[s0], feats[s1]], axis=0)
            square = dot(rows, jnp.concatenate([target[jnp.minimum(t[u], LD - 1)], pad], axis=0))
            kernels.append(lax.rsqrt(square).astype(BF))
            weights.append(jnp.concatenate([table[s0, 0:R, :], table[s1, 0:R, :]], axis=1))
        terms = [dot(weights[u], kernels[u]) for u in range(UNROLL)]
        for u in range(UNROLL):
            acc[t[u]] += terms[u]
        return 0

    lax.fori_loop(0, (at // 2 + UNROLL - 1) // UNROLL, near, 0)


def fields(indices, place, low_field, down, coupling, target, matrices, box_matrices, sents):
    return pl.pallas_call(
        fields_body,
        in_specs=[SMEM] * 7 + [VMEM] * 3 + [ANY] * 6,
        out_specs=[VMEM] * 5,
        out_shape=[
            sds((LD + 1, R, M), F32),
            sds((LD, R, K), F32),
            sds((BX, R, K), F32),
            sds((R, K), F32),
            sds((4, 2, 2, K, K), BF),
        ],
        scratch_shapes=[
            pltpu.VMEM((ALL + 1, ROWS, M), BF),
            pltpu.VMEM((3 * (SENT - LD), ROWS, M), BF),
            pltpu.VMEM((ALL + 1, M, M), BF),
            pltpu.VMEM((LD, FX, M), BF),
            pltpu.VMEM((matrices.shape[0], K, K), BF),
            pltpu.VMEM((matrices.shape[0], K, K), BF),
            pltpu.VMEM((6 * PAIRS, R, 2 * K), BF),
            pltpu.VMEM((6 * PAIRS, R, 2 * K), BF),
            pltpu.SMEM((SLOTS,), jnp.int32),
            pltpu.SemaphoreType.DMA((9,)),
        ],
        compiler_params=params(),
        cost_estimate=pl.CostEstimate(flops=8 << 30, bytes_accessed=4 << 20, transcendentals=8 << 20),
        name="near_and_coupled_fields",
    )(*indices, place, low_field, down, coupling, target, matrices, box_matrices, *sents)


def final_body(place, nodes, up, base, tip, parents, leaf_field_in, box_field, box_down, leaf_down_in, basis_in, near_in, out, boxes, held, leaf_field, leaf_down, basis, near_part, sems):
    moves = ((leaf_field_in, leaf_field), (leaf_down_in, leaf_down), (basis_in, basis), (near_in, near_part))
    copies = load([pltpu.make_async_copy(a, b, sems.at[n]) for n, (a, b) in enumerate(moves)])
    levels = [nodes[...].reshape(LOW, R // 2, 2 * K)]
    for h in range(3):
        levels.append(raise_nodes(levels[h], (up[4 + h, 0], up[4 + h, 1])))
    start = 0
    for h in range(4):
        held[start : start + (LOW >> h)] = levels[h].astype(F32)
        start += LOW >> h
    me = (place[0] >> 4) & (LOW - 1)
    total = base[...]
    start = 0
    for h in range(4):
        for i in range(2):
            hi, lo = split2(unpack(held[((me >> h) ^ (2 + i)) + start]))
            total = total + (dot(hi, tip[h, i, 0]) + dot(hi, tip[h, i, 1]) + dot(lo, tip[h, i, 0]))
        start += LOW >> h
    for copy in copies:
        copy.wait()
    group = total.astype(BF)
    got = [(box_field[box] + dot(group, box_down[box])).astype(BF) for box in range(BX)]
    for box in range(BX):
        boxes[box] = got[box]
    for part in range(LD // 8):
        leaves = range(8 * part, 8 * part + 8)
        field = [
            (leaf_field[leaf] + dot(boxes[parents[leaf]], leaf_down[leaf])).astype(BF) for leaf in leaves
        ]
        got = [
            near_part[leaf] + dot(field[i], basis[:, pl.ds(leaf * M, M)]) for i, leaf in enumerate(leaves)
        ]
        for i, leaf in enumerate(leaves):
            out[:, pl.ds(leaf * M, M)] = got[i]


def finish(place, nodes, up, base, tip, parents, leaf_field, box_field, box_down, leaf_down, basis, near_part):
    return pl.pallas_call(
        final_body,
        in_specs=[SMEM] + [VMEM] * 4 + [SMEM, ANY, VMEM, VMEM] + [ANY] * 3,
        out_specs=VMEM,
        out_shape=sds((R, LD * M), F32),
        scratch_shapes=[
            pltpu.VMEM((BX, R, K), BF),
            pltpu.VMEM((2 * LOW, R // 2, 2 * K), F32),
            pltpu.VMEM((LD, R, K), F32),
            pltpu.VMEM((LD, K, K), BF),
            pltpu.VMEM((K, LD * M), BF),
            pltpu.VMEM((LD + 1, R, M), F32),
            pltpu.SemaphoreType.DMA((4,)),
        ],
        compiler_params=params(),
        name="group_to_points",
    )(place, nodes, up, base, tip, parents, leaf_field, box_field, box_down, leaf_down, basis, near_part)


def exchange(x):
    count = lax.axis_size(AXES)
    left = lax.ppermute(x, AXES, [(i, i + 1) for i in range(count - 1)])
    right = lax.ppermute(x, AXES, [(i + 1, i) for i in range(count - 1)])
    return left, right


def gather_groups(copies, groups):
    return lax.all_to_all(copies, AXES, 0, 0, axis_index_groups=groups, tiled=True)


def local(
    charges,
    points,
    leaf_basis,
    leaf_parent,
    leaf_up,
    leaf_down,
    box_up,
    box_down,
    top_up,
    top_down,
    top_coupling,
    leaf_sources,
    leaf_classes,
    leaf_coupling,
    box_sources,
    box_classes,
    box_coupling,
    near_leaves,
    near_count,
):
    device = lax.axis_index(AXES)
    place = device.astype(jnp.int32).reshape(1)
    parents = leaf_parent[0]

    sent, target, ascent = first(charges, points, leaf_basis, leaf_up, box_up, parents)

    blocks = lax.axis_size(AXES) // LOW
    low_groups = [[b * LOW + i for i in range(LOW)] for b in range(blocks)]
    high_groups = [[b * LOW + i for b in range(blocks)] for i in range(LOW)]
    low_nodes = gather_groups(ascent, low_groups)
    sent_left, sent_right = exchange(sent)
    top, low_field = low_tree(place, low_nodes, top_up, top_coupling, blocks)
    high_nodes = gather_groups(top, high_groups)

    near_part, leaf_field, box_field, base, tip = fields(
        (near_leaves, near_count, leaf_sources, leaf_classes, box_sources, box_classes),
        place,
        low_field,
        top_down,
        top_coupling,
        target,
        leaf_coupling,
        box_coupling,
        (sent_left, sent, sent_right),
    )
    return finish(
        place, high_nodes, top_up, base, tip, parents, leaf_field, box_field, box_down, leaf_down, leaf_basis, near_part
    )


def solution(mesh):
    split = P(AXES)
    return jax.shard_map(
        local,
        mesh=mesh,
        in_specs=(
            P(None, AXES),
            P(None, AXES),
            P(None, AXES),
            split,
            split,
            split,
            split,
            split,
            P(),
            P(),
            P(),
            split,
            split,
            P(),
            split,
            split,
            P(),
            split,
            split,
        ),
        out_specs=P(None, AXES),
        check_vma=False,
    )
```

```python
import math

import jax
import jax.numpy as jnp
import numpy as np
from jax import lax
from jax.experimental import pallas as pl
from jax.experimental.pallas import tpu as pltpu
from jax.sharding import PartitionSpec as P

BF = jnp.bfloat16
F32 = jnp.float32
AXES = ("box", "rhs")

R = 64
K = 64
M = 128
LD = 24
BX = 6
ADM = 16
ADMB = 8
NEAR = 27
FR = 16
ROWS = R + FR
FX = 32
UNROLL = 16
LOW = 32
PAIRS = (LD + BX) // 2
SENT = LD + PAIRS * R // ROWS
SLOTS = LD * (NEAR + 1) + 2 * UNROLL + 32
ALL = 3 * LD
BOTH = 2 * LD

DELTA2 = 0.0001
INV_SCALE = 2.0 * math.sqrt(NEAR * M)
CENTRE = 1.1

PARTS = ((0, 0), (0, 1), (0, 2), (1, 0), (1, 1), (1, 2), (2, 0), (2, 1))

VMEM = pl.BlockSpec(memory_space=pltpu.VMEM)
SMEM = pl.BlockSpec(memory_space=pltpu.SMEM)
ANY = pl.BlockSpec(memory_space=pl.ANY)
HBM = pl.BlockSpec(memory_space=pltpu.HBM)


def params(mib=60.0):
    return pltpu.CompilerParams(vmem_limit_bytes=int(mib * 1024 * 1024))


def sds(shape, dtype):
    return jax.ShapeDtypeStruct(shape, dtype)


def dot(a, b):
    return jnp.dot(a, b, preferred_element_type=F32)


def dot_nt(a, b):
    return lax.dot_general(a, b, (((1,), (1,)), ((), ())), preferred_element_type=F32)


def dot2(x, m):
    hi = x.astype(BF)
    lo = (x - hi.astype(F32)).astype(BF)
    return dot(hi, m) + dot(lo, m)


def expansion(leaf):
    row = lax.broadcasted_iota(jnp.int32, (8 * FR, M), 0) - FR * leaf
    e = lax.broadcasted_iota(jnp.int32, (8 * FR, M), 1)
    third = (e * 43) >> 7
    part = jnp.where(e < 9, 0, jnp.where(e < 18, 3, 6))
    source = jnp.where(e < 24, part + e - 3 * third, jnp.where(e < 27, e - 15, jnp.where(e < 30, 12, -M)))
    return jnp.where(row == source, 1.0, 0.0).astype(BF)


def split3(x):
    hi = x.astype(BF).astype(F32)
    rest = x - hi
    mid = rest.astype(BF).astype(F32)
    return hi, mid, rest - mid


def load(copies):
    for copy in copies:
        copy.start()
    return copies


def first_body(charges_in, points_in, basis_in, leaf_up_in, box_up_in, parents, sent, target, ascent, charges, points, basis, leaf_up, box_up, feat, wide, acc, sems):
    moves = ((points_in, points), (charges_in, charges), (basis_in, basis), (leaf_up_in, leaf_up), (box_up_in, box_up))
    copies = load([pltpu.make_async_copy(a, b, sems.at[n]) for n, (a, b) in enumerate(moves)])
    acc[...] = jnp.zeros(acc.shape, F32)
    copies[1].wait()
    copies[2].wait()
    copies[3].wait()
    for group in range(LD // 8):
        leaves = range(8 * group, 8 * group + 8)
        c = [dot_nt(charges[:, pl.ds(leaf * M, M)], basis[:, pl.ds(leaf * M, M)]) for leaf in leaves]
        raised = [dot(c[i].astype(BF), leaf_up[leaf]) for i, leaf in enumerate(leaves)]
        for i in range(0, 8, 2):
            put_coef(sent, (8 * group + i) // 2, jnp.concatenate([c[i], c[i + 1]], axis=1).astype(BF))
        for i, leaf in enumerate(leaves):
            acc[parents[leaf]] += raised[i]
    copies[4].wait()
    copies[0].wait()
    boxes = [acc[box] for box in range(BX)]
    raised = [dot(boxes[box].astype(BF), box_up[box]) for box in range(BX)]
    total = raised[0] + raised[1] + (raised[2] + raised[3]) + (raised[4] + raised[5])
    packed = jnp.concatenate([total[: R // 2], total[R // 2 :]], axis=1).astype(BF)
    for i in range(LOW):
        ascent[i] = packed
    for box in range(0, BX, 2):
        put_coef(sent, (LD + box) // 2, jnp.concatenate([boxes[box], boxes[box + 1]], axis=1).astype(BF))

    p = (points[...] - CENTRE) * INV_SCALE
    parts = split3(p)
    norm = p[0:1] * p[0:1] + p[1:2] * p[1:2] + p[2:3] * p[2:3]
    source_norm = split3(norm)
    target_norm = split3(norm + DELTA2 * INV_SCALE * INV_SCALE)
    feat[...] = jnp.zeros(feat.shape, F32)
    wide[...] = jnp.zeros(wide.shape, F32)
    one = jnp.ones(norm.shape, F32)
    for a in range(3):
        feat[3 * a : 3 * a + 3, :] = parts[a]
        feat[9 + a : 10 + a, :] = source_norm[a]
    feat[12:13, :] = one
    for n, (_, b) in enumerate(PARTS):
        wide[3 * n : 3 * n + 3, :] = -2.0 * parts[b]
    base = 3 * len(PARTS)
    for a in range(3):
        wide[base + a : base + a + 1, :] = one
        wide[base + 3 + a : base + 4 + a, :] = target_norm[a]
    turned = []
    for o in range(LD // 8):
        rows = jnp.concatenate([feat[:, pl.ds((8 * o + i) * M, M)] for i in range(8)], axis=0)
        turned.append(rows.T.astype(BF))
    for leaf in range(LD):
        cols = pl.ds(leaf * M, M)
        sent[leaf, 0:R, :] = charges[:, cols]
        i = leaf % 8
        sent[leaf, R:ROWS, :] = turned[leaf // 8][FR * i : FR * (i + 1), :]
        target[leaf, :, :] = wide[:, cols].astype(BF)


def coef_places(pair):
    rows = [pair * R + 16 * i for i in range(R // 16)]
    return [(r // ROWS, r % ROWS) for r in rows]


def put_coef(sent, pair, value):
    for i, (block, row) in enumerate(coef_places(pair)):
        sent[LD + block, row : row + 16, :] = value[16 * i : 16 * i + 16]


def first(charges, points, basis, leaf_up, box_up, parents):
    return pl.pallas_call(
        first_body,
        in_specs=[HBM] * 5 + [SMEM],
        out_specs=[VMEM] * 3,
        out_shape=[
            sds((SENT, ROWS, M), BF),
            sds((LD, FX, M), BF),
            sds((LOW, R // 2, 2 * K), BF),
        ],
        scratch_shapes=[
            pltpu.VMEM((R, LD * M), BF),
            pltpu.VMEM((3, LD * M), F32),
            pltpu.VMEM((K, LD * M), BF),
            pltpu.VMEM((LD, K, K), BF),
            pltpu.VMEM((BX, K, K), BF),
            pltpu.VMEM((FR, LD * M), F32),
            pltpu.VMEM((FX, LD * M), F32),
            pltpu.VMEM((BX, R, K), F32),
            pltpu.SemaphoreType.DMA((5,)),
        ],
        compiler_params=params(),
        name="points_to_group",
    )(charges, points, basis, leaf_up, box_up, parents)


def twice(m):
    zero = jnp.zeros_like(m)
    return jnp.concatenate([jnp.concatenate([m, zero], axis=1), jnp.concatenate([zero, m], axis=1)], axis=0)


def unpack(x):
    return jnp.concatenate([x[:, :K], x[:, K:]], axis=0)


def raise_nodes(nodes, matrices):
    count = nodes.shape[0] // 2
    left = jnp.concatenate([nodes[2 * i] for i in range(count)], axis=0)
    right = jnp.concatenate([nodes[2 * i + 1] for i in range(count)], axis=0)
    mul = dot if nodes.dtype == BF else dot2
    return (mul(left, twice(matrices[0])) + mul(right, twice(matrices[1]))).reshape(count, R // 2, 2 * K)


def low_body(place, nodes, up, coupling, top, field, held):
    levels = [nodes[...]]
    for h in range(4):
        levels.append(raise_nodes(levels[h], (up[h, 0], up[h, 1])))
    packed = levels[4].astype(BF).reshape(R, 2 * K)
    for i in range(top.shape[0]):
        top[i] = packed
    start = 0
    for h in range(4):
        held[start : start + (LOW >> h)] = levels[h].astype(F32)
        start += LOW >> h
    me = place[0] & (LOW - 1)
    start = 0
    out = []
    for h in range(4):
        q = me >> h
        near, far = unpack(held[(q ^ 2) + start]), unpack(held[(q ^ 3) + start])
        out.append(dot2(near, coupling[h, 0]) + dot2(far, coupling[h, 1]))
        start += LOW >> h
    for h in range(4):
        field[h] = out[h]


def low_tree(place, nodes, up, coupling, blocks):
    return pl.pallas_call(
        low_body,
        in_specs=[SMEM, VMEM, VMEM, VMEM],
        out_specs=[VMEM, VMEM],
        out_shape=[sds((blocks, R, 2 * K), BF), sds((4, R, K), F32)],
        scratch_shapes=[pltpu.VMEM((2 * LOW, R // 2, 2 * K), F32)],
        compiler_params=params(63.5),
        name="coarse_low",
    )(place, nodes, up, coupling)


def split2(x):
    hi = x.astype(BF)
    return hi, (x - hi.astype(F32)).astype(BF)


def used_slots(near_leaves, near_count, slots, me, halo):
    null = BOTH if halo else LD
    at = jnp.int32(0)
    for t in range(LD):
        used = near_count[t]
        for part in range(0, NEAR, 9):
            row = [near_leaves[t, part + s] - me * LD for s in range(9)]
            for s, x in enumerate(row):
                mine = jnp.logical_and(x >= 0, x < LD)
                wanted = jnp.logical_not(mine) if halo else mine
                if halo:
                    x = jnp.where(x < 0, x + LD, x)
                slots[at] = x + (t << 8)
                at = at + jnp.where(jnp.logical_and(wanted, part + s < used), 1, 0)
        slots[at] = t << 8 | null
        at = (at + 1) & -2
    for i in range(2 * UNROLL):
        slots[at + i] = LD << 8 | null
    return (at // 2 + UNROLL - 1) // UNROLL


def spread_features(table, feats, count):
    lane = lax.broadcasted_iota(jnp.int32, (M, M), 1)
    ones = 3 * len(PARTS) + 3
    feats[count] = jnp.where((lane >= ones) & (lane < ones + 3), 1.0, 0.0).astype(BF)
    expand = [expansion(i) for i in range(8)]
    for o in range(count // 8):
        rows = jnp.concatenate([table[8 * o + i, R:ROWS, :] for i in range(8)], axis=0)
        spread = [dot(rows, expand[i]).astype(BF) for i in range(8)]
        for i in range(8):
            feats[8 * o + i] = spread[i]


def near_loop(steps, slots, table, feats, target, acc):
    pad = jnp.zeros((M - FX, M), BF)

    def near(it, _):
        t, kernels, weights = [], [], []
        for u in range(UNROLL):
            place_of = (it * UNROLL + u) * 2
            one, two = slots[place_of], slots[place_of + 1]
            s0, s1 = one & 255, two & 255
            t.append(one >> 8)
            rows = jnp.concatenate([feats[s0], feats[s1]], axis=0)
            square = dot(rows, jnp.concatenate([target[jnp.minimum(t[u], LD - 1)], pad], axis=0))
            kernels.append(lax.rsqrt(square).astype(BF))
            weights.append(jnp.concatenate([table[s0, 0:R, :], table[s1, 0:R, :]], axis=1))
        terms = [dot(weights[u], kernels[u]) for u in range(UNROLL)]
        for u in range(UNROLL):
            acc[t[u]] += terms[u]
        return 0

    lax.fori_loop(0, steps, near, 0)


def own_body(near_leaves, near_count, place, target_in, sent, acc, _, table, feats, target, slots, sems):
    moves = ((sent.at[pl.ds(0, LD)], table.at[pl.ds(0, LD)]), (target_in, target))
    copies = load([pltpu.make_async_copy(a, b, sems.at[n]) for n, (a, b) in enumerate(moves)])
    steps = used_slots(near_leaves, near_count, slots, place[0], False)
    acc[...] = jnp.zeros(acc.shape, F32)
    table[LD] = jnp.zeros((ROWS, M), BF)
    for copy in copies:
        copy.wait()
    spread_features(table, feats, LD)
    near_loop(steps, slots, table, feats, target, acc)


def near_own(near_leaves, near_count, place, target, sent):
    return pl.pallas_call(
        own_body,
        in_specs=[SMEM] * 3 + [ANY] * 2,
        out_specs=[VMEM, ANY],
        out_shape=[sds((LD + 1, R, M), F32), sds(sent.shape, sent.dtype)],
        input_output_aliases={4: 1},
        scratch_shapes=[
            pltpu.VMEM((LD + 1, ROWS, M), BF),
            pltpu.VMEM((LD + 1, M, M), BF),
            pltpu.VMEM((LD, FX, M), BF),
            pltpu.SMEM((SLOTS,), jnp.int32),
            pltpu.SemaphoreType.DMA((2,)),
        ],
        compiler_params=params(),
        cost_estimate=pl.CostEstimate(flops=2 << 30, bytes_accessed=2 << 20, transcendentals=4 << 20),
        name="near_own",
    )(near_leaves, near_count, place, target, sent)


def fields_body(near_leaves, near_count, leaf_sources, leaf_classes, box_sources, box_classes, place, low_field, down, coupling, near_in, target_in, matrices_in, box_matrices_in, left, mine, right, acc, leaf_field, box_field, base, tip, table, coefs, feats, target, matrices, box_matrices, low, high, slots, sems):
    blocks = SENT - LD
    sources = (left, mine, right)
    moves = [(left.at[pl.ds(0, LD)], table.at[pl.ds(0, LD)]), (right.at[pl.ds(0, LD)], table.at[pl.ds(LD, LD)])]
    moves += [(src.at[pl.ds(LD, blocks)], coefs.at[pl.ds(n * blocks, blocks)]) for n, src in enumerate(sources)]
    moves += [(target_in, target), (matrices_in, matrices), (box_matrices_in, box_matrices), (near_in, acc)]
    copies = load([pltpu.make_async_copy(a, b, sems.at[n]) for n, (a, b) in enumerate(moves)])
    me = place[0]
    steps = used_slots(near_leaves, near_count, slots, me, True)

    total = low_field[3]
    chain = down[3, (me >> 3) & 1].astype(F32)
    for h in range(2, -1, -1):
        both = dot2(jnp.concatenate([total, chain], axis=0), down[h, (me >> h) & 1])
        total = low_field[h] + both[:R]
        chain = both[R:]
    tips = []
    for h in range(4, 8):
        hi, lo = split2(chain)
        stack = jnp.concatenate([coupling[h, 0], coupling[h, 1], down[min(h, 6), (me >> h) & 1]], axis=0)
        product = dot(stack, hi) + dot(stack, lo)
        tips.append((split2(product[0:K]), split2(product[K : 2 * K])))
        chain = product[2 * K :]
    base[...] = total
    for h in range(4):
        for i in range(2):
            for n in range(2):
                tip[h, i, n] = tips[h][i][n]

    table[BOTH] = jnp.zeros((ROWS, M), BF)
    for copy in copies:
        copy.wait()

    first = lax.broadcasted_iota(jnp.int32, (R, 2 * K), 1) < K
    for n in range(3):
        for group in range(PAIRS // 5):
            ready = []
            for i in range(5 * group, 5 * group + 5):
                x = jnp.concatenate(
                    [coefs[n * blocks + b, r : r + 16, :] for b, r in coef_places(i)], axis=0
                ).astype(F32)
                y = pltpu.roll(x, K, 1)
                ready.append(
                    [
                        jnp.where(first, x, 0.0).astype(BF),
                        jnp.where(first, y, 0.0).astype(BF),
                        jnp.where(first, 0.0, y).astype(BF),
                        jnp.where(first, 0.0, x).astype(BF),
                    ]
                )
            for i in range(5):
                at_row = 2 * (5 * group + i)
                row = n * LD + at_row if at_row < LD else ALL + n * BX + at_row - LD
                low[row], low[row + 1], high[row], high[row + 1] = ready[i]

    def gather(source, kind, mats, width):
        total = jnp.zeros((R, K), F32)
        for g in range(width // 4):
            s = [source(4 * g + i) for i in range(4)]
            vec = jnp.concatenate([low[s[0]] + high[s[1]], low[s[2]] + high[s[3]]], axis=1)
            mat = jnp.concatenate([mats[kind(4 * g + i)] for i in range(4)], axis=0)
            total = total + dot(vec, mat)
        return total

    def couple(it, _):
        rows = [it * 8 + u for u in range(8)]
        got = [
            gather(
                lambda a: leaf_sources[a, row] - (me - 1) * LD, lambda a: leaf_classes[a, row], matrices, ADM
            )
            for row in rows
        ]
        for row, value in zip(rows, got):
            leaf_field[row] = value
        return 0

    lax.fori_loop(0, LD // 8, couple, 0)
    got = [
        gather(
            lambda a: box_sources[box, a] - (me - 1) * BX + ALL, lambda a: box_classes[box, a], box_matrices, ADMB
        )
        for box in range(BX)
    ]
    for box in range(BX):
        box_field[box] = got[box]

    spread_features(table, feats, BOTH)
    near_loop(steps, slots, table, feats, target, acc)


def fields(indices, place, low_field, down, coupling, near_part, target, matrices, box_matrices, sents):
    return pl.pallas_call(
        fields_body,
        in_specs=[SMEM] * 7 + [VMEM] * 3 + [ANY] * 7,
        out_specs=[VMEM] * 5,
        out_shape=[
            sds((LD + 1, R, M), F32),
            sds((LD, R, K), F32),
            sds((BX, R, K), F32),
            sds((R, K), F32),
            sds((4, 2, 2, K, K), BF),
        ],
        scratch_shapes=[
            pltpu.VMEM((BOTH + 1, ROWS, M), BF),
            pltpu.VMEM((3 * (SENT - LD), ROWS, M), BF),
            pltpu.VMEM((BOTH + 1, M, M), BF),
            pltpu.VMEM((LD, FX, M), BF),
            pltpu.VMEM((matrices.shape[0], K, K), BF),
            pltpu.VMEM((matrices.shape[0], K, K), BF),
            pltpu.VMEM((6 * PAIRS, R, 2 * K), BF),
            pltpu.VMEM((6 * PAIRS, R, 2 * K), BF),
            pltpu.SMEM((SLOTS,), jnp.int32),
            pltpu.SemaphoreType.DMA((9,)),
        ],
        compiler_params=params(),
        cost_estimate=pl.CostEstimate(flops=8 << 30, bytes_accessed=4 << 20, transcendentals=8 << 20),
        name="near_and_coupled_fields",
    )(*indices, place, low_field, down, coupling, near_part, target, matrices, box_matrices, *sents)


def final_body(place, nodes, up, base, tip, parents, leaf_field_in, box_field, box_down, leaf_down_in, basis_in, near_in, out, boxes, held, leaf_field, leaf_down, basis, near_part, sems):
    moves = ((leaf_field_in, leaf_field), (leaf_down_in, leaf_down), (basis_in, basis), (near_in, near_part))
    copies = load([pltpu.make_async_copy(a, b, sems.at[n]) for n, (a, b) in enumerate(moves)])
    levels = [nodes[...].reshape(LOW, R // 2, 2 * K)]
    for h in range(3):
        levels.append(raise_nodes(levels[h], (up[4 + h, 0], up[4 + h, 1])))
    start = 0
    for h in range(4):
        held[start : start + (LOW >> h)] = levels[h].astype(F32)
        start += LOW >> h
    me = (place[0] >> 4) & (LOW - 1)
    total = base[...]
    start = 0
    for h in range(4):
        for i in range(2):
            hi, lo = split2(unpack(held[((me >> h) ^ (2 + i)) + start]))
            total = total + (dot(hi, tip[h, i, 0]) + dot(hi, tip[h, i, 1]) + dot(lo, tip[h, i, 0]))
        start += LOW >> h
    for copy in copies:
        copy.wait()
    group = total.astype(BF)
    got = [(box_field[box] + dot(group, box_down[box])).astype(BF) for box in range(BX)]
    for box in range(BX):
        boxes[box] = got[box]
    for part in range(LD // 8):
        leaves = range(8 * part, 8 * part + 8)
        field = [
            (leaf_field[leaf] + dot(boxes[parents[leaf]], leaf_down[leaf])).astype(BF) for leaf in leaves
        ]
        got = [
            near_part[leaf] + dot(field[i], basis[:, pl.ds(leaf * M, M)]) for i, leaf in enumerate(leaves)
        ]
        for i, leaf in enumerate(leaves):
            out[:, pl.ds(leaf * M, M)] = got[i]


def finish(place, nodes, up, base, tip, parents, leaf_field, box_field, box_down, leaf_down, basis, near_part):
    return pl.pallas_call(
        final_body,
        in_specs=[SMEM] + [VMEM] * 4 + [SMEM, ANY, VMEM, VMEM] + [ANY] * 3,
        out_specs=VMEM,
        out_shape=sds((R, LD * M), F32),
        scratch_shapes=[
            pltpu.VMEM((BX, R, K), BF),
            pltpu.VMEM((2 * LOW, R // 2, 2 * K), F32),
            pltpu.VMEM((LD, R, K), F32),
            pltpu.VMEM((LD, K, K), BF),
            pltpu.VMEM((K, LD * M), BF),
            pltpu.VMEM((LD + 1, R, M), F32),
            pltpu.SemaphoreType.DMA((4,)),
        ],
        compiler_params=params(),
        name="group_to_points",
    )(place, nodes, up, base, tip, parents, leaf_field, box_field, box_down, leaf_down, basis, near_part)


def exchange(x):
    count = lax.axis_size(AXES)
    left = lax.ppermute(x, AXES, [(i, i + 1) for i in range(count - 1)])
    right = lax.ppermute(x, AXES, [(i + 1, i) for i in range(count - 1)])
    return left, right


def gather_groups(copies, groups):
    return lax.all_to_all(copies, AXES, 0, 0, axis_index_groups=groups, tiled=True)


def local(
    charges,
    points,
    leaf_basis,
    leaf_parent,
    leaf_up,
    leaf_down,
    box_up,
    box_down,
    top_up,
    top_down,
    top_coupling,
    leaf_sources,
    leaf_classes,
    leaf_coupling,
    box_sources,
    box_classes,
    box_coupling,
    near_leaves,
    near_count,
):
    device = lax.axis_index(AXES)
    place = device.astype(jnp.int32).reshape(1)
    parents = leaf_parent[0]

    sent, target, ascent = first(charges, points, leaf_basis, leaf_up, box_up, parents)

    blocks = lax.axis_size(AXES) // LOW
    low_groups = [[b * LOW + i for i in range(LOW)] for b in range(blocks)]
    high_groups = [[b * LOW + i for b in range(blocks)] for i in range(LOW)]
    low_nodes = gather_groups(ascent, low_groups)
    near_part, sent = near_own(near_leaves, near_count, place, target, sent)
    sent_left, sent_right = exchange(sent)
    top, low_field = low_tree(place, low_nodes, top_up, top_coupling, blocks)
    high_nodes = gather_groups(top, high_groups)

    near_part, leaf_field, box_field, base, tip = fields(
        (near_leaves, near_count, leaf_sources.T, leaf_classes.T, box_sources, box_classes),
        place,
        low_field,
        top_down,
        top_coupling,
        near_part,
        target,
        leaf_coupling,
        box_coupling,
        (sent_left, sent, sent_right),
    )
    return finish(
        place, high_nodes, top_up, base, tip, parents, leaf_field, box_field, box_down, leaf_down, leaf_basis, near_part
    )


def solution(mesh):
    split = P(AXES)
    return jax.shard_map(
        local,
        mesh=mesh,
        in_specs=(
            P(None, AXES),
            P(None, AXES),
            P(None, AXES),
            split,
            split,
            split,
            split,
            split,
            P(),
            P(),
            P(),
            split,
            split,
            P(),
            split,
            split,
            P(),
            split,
            split,
        ),
        out_specs=P(None, AXES),
        check_vma=False,
    )
```

```python
import math

import jax
import jax.numpy as jnp
import numpy as np
from jax import lax
from jax.experimental import pallas as pl
from jax.experimental.pallas import tpu as pltpu
from jax.sharding import PartitionSpec as P

BF = jnp.bfloat16
F32 = jnp.float32
AXES = ("box", "rhs")

R = 64
K = 64
M = 128
LD = 24
BX = 6
ADM = 16
ADMB = 8
NEAR = 27
FR = 16
ROWS = R + FR
FX = 32
UNROLL = 16
LOW = 32
PAIRS = (LD + BX) // 2
SENT = LD + PAIRS * R // ROWS
SLOTS = LD * (NEAR + 1) + 2 * UNROLL + 32
ALL = 3 * LD
BOTH = 2 * LD

DELTA2 = 0.0001
INV_SCALE = 2.0 * math.sqrt(NEAR * M)
CENTRE = 1.1

PARTS = ((0, 0), (0, 1), (0, 2), (1, 0), (1, 1), (1, 2), (2, 0), (2, 1))

VMEM = pl.BlockSpec(memory_space=pltpu.VMEM)
SMEM = pl.BlockSpec(memory_space=pltpu.SMEM)
ANY = pl.BlockSpec(memory_space=pl.ANY)
HBM = pl.BlockSpec(memory_space=pltpu.HBM)


def params(mib=60.0):
    return pltpu.CompilerParams(vmem_limit_bytes=int(mib * 1024 * 1024))


def sds(shape, dtype):
    return jax.ShapeDtypeStruct(shape, dtype)


def dot(a, b):
    return jnp.dot(a, b, preferred_element_type=F32)


def dot_nt(a, b):
    return lax.dot_general(a, b, (((1,), (1,)), ((), ())), preferred_element_type=F32)


def dot2(x, m):
    hi = x.astype(BF)
    lo = (x - hi.astype(F32)).astype(BF)
    return dot(hi, m) + dot(lo, m)


def expansion(leaf):
    row = lax.broadcasted_iota(jnp.int32, (8 * FR, M), 0) - FR * leaf
    e = lax.broadcasted_iota(jnp.int32, (8 * FR, M), 1)
    third = (e * 43) >> 7
    part = jnp.where(e < 9, 0, jnp.where(e < 18, 3, 6))
    source = jnp.where(e < 24, part + e - 3 * third, jnp.where(e < 27, e - 15, jnp.where(e < 30, 12, -M)))
    return jnp.where(row == source, 1.0, 0.0).astype(BF)


def split3(x):
    hi = x.astype(BF).astype(F32)
    rest = x - hi
    mid = rest.astype(BF).astype(F32)
    return hi, mid, rest - mid


def load(copies):
    for copy in copies:
        copy.start()
    return copies


def first_body(charges_in, points_in, basis_in, leaf_up_in, box_up_in, parents, sent, target, ascent, charges, points, basis, leaf_up, box_up, feat, wide, acc, sems):
    moves = ((points_in, points), (charges_in, charges), (basis_in, basis), (leaf_up_in, leaf_up), (box_up_in, box_up))
    copies = load([pltpu.make_async_copy(a, b, sems.at[n]) for n, (a, b) in enumerate(moves)])
    acc[...] = jnp.zeros(acc.shape, F32)
    copies[1].wait()
    copies[2].wait()
    copies[3].wait()
    for group in range(LD // 8):
        leaves = range(8 * group, 8 * group + 8)
        c = [dot_nt(charges[:, pl.ds(leaf * M, M)], basis[:, pl.ds(leaf * M, M)]) for leaf in leaves]
        raised = [dot(c[i].astype(BF), leaf_up[leaf]) for i, leaf in enumerate(leaves)]
        for i in range(0, 8, 2):
            put_coef(sent, (8 * group + i) // 2, jnp.concatenate([c[i], c[i + 1]], axis=1).astype(BF))
        for i, leaf in enumerate(leaves):
            acc[parents[leaf]] += raised[i]
    copies[4].wait()
    copies[0].wait()
    boxes = [acc[box] for box in range(BX)]
    raised = [dot(boxes[box].astype(BF), box_up[box]) for box in range(BX)]
    total = raised[0] + raised[1] + (raised[2] + raised[3]) + (raised[4] + raised[5])
    packed = jnp.concatenate([total[: R // 2], total[R // 2 :]], axis=1).astype(BF)
    for i in range(LOW):
        ascent[i] = packed
    for box in range(0, BX, 2):
        put_coef(sent, (LD + box) // 2, jnp.concatenate([boxes[box], boxes[box + 1]], axis=1).astype(BF))

    p = (points[...] - CENTRE) * INV_SCALE
    parts = split3(p)
    norm = p[0:1] * p[0:1] + p[1:2] * p[1:2] + p[2:3] * p[2:3]
    source_norm = split3(norm)
    target_norm = split3(norm + DELTA2 * INV_SCALE * INV_SCALE)
    feat[...] = jnp.zeros(feat.shape, F32)
    wide[...] = jnp.zeros(wide.shape, F32)
    one = jnp.ones(norm.shape, F32)
    for a in range(3):
        feat[3 * a : 3 * a + 3, :] = parts[a]
        feat[9 + a : 10 + a, :] = source_norm[a]
    feat[12:13, :] = one
    for n, (_, b) in enumerate(PARTS):
        wide[3 * n : 3 * n + 3, :] = -2.0 * parts[b]
    base = 3 * len(PARTS)
    for a in range(3):
        wide[base + a : base + a + 1, :] = one
        wide[base + 3 + a : base + 4 + a, :] = target_norm[a]
    turned = []
    for o in range(LD // 8):
        rows = jnp.concatenate([feat[:, pl.ds((8 * o + i) * M, M)] for i in range(8)], axis=0)
        turned.append(rows.T.astype(BF))
    for leaf in range(LD):
        cols = pl.ds(leaf * M, M)
        sent[leaf, 0:R, :] = charges[:, cols]
        i = leaf % 8
        sent[leaf, R:ROWS, :] = turned[leaf // 8][FR * i : FR * (i + 1), :]
        target[leaf, :, :] = wide[:, cols].astype(BF)


def coef_places(pair):
    rows = [pair * R + 16 * i for i in range(R // 16)]
    return [(r // ROWS, r % ROWS) for r in rows]


def put_coef(sent, pair, value):
    for i, (block, row) in enumerate(coef_places(pair)):
        sent[LD + block, row : row + 16, :] = value[16 * i : 16 * i + 16]


def first(charges, points, basis, leaf_up, box_up, parents):
    return pl.pallas_call(
        first_body,
        in_specs=[HBM] * 5 + [SMEM],
        out_specs=[VMEM] * 3,
        out_shape=[
            sds((SENT, ROWS, M), BF),
            sds((LD, FX, M), BF),
            sds((LOW, R // 2, 2 * K), BF),
        ],
        scratch_shapes=[
            pltpu.VMEM((R, LD * M), BF),
            pltpu.VMEM((3, LD * M), F32),
            pltpu.VMEM((K, LD * M), BF),
            pltpu.VMEM((LD, K, K), BF),
            pltpu.VMEM((BX, K, K), BF),
            pltpu.VMEM((FR, LD * M), F32),
            pltpu.VMEM((FX, LD * M), F32),
            pltpu.VMEM((BX, R, K), F32),
            pltpu.SemaphoreType.DMA((5,)),
        ],
        compiler_params=params(),
        name="points_to_group",
    )(charges, points, basis, leaf_up, box_up, parents)


def twice(m):
    zero = jnp.zeros_like(m)
    return jnp.concatenate([jnp.concatenate([m, zero], axis=1), jnp.concatenate([zero, m], axis=1)], axis=0)


def unpack(x):
    return jnp.concatenate([x[:, :K], x[:, K:]], axis=0)


def raise_nodes(nodes, matrices):
    count = nodes.shape[0] // 2
    left = jnp.concatenate([nodes[2 * i] for i in range(count)], axis=0)
    right = jnp.concatenate([nodes[2 * i + 1] for i in range(count)], axis=0)
    mul = dot if nodes.dtype == BF else dot2
    return (mul(left, twice(matrices[0])) + mul(right, twice(matrices[1]))).reshape(count, R // 2, 2 * K)


def list_slots(code, lists, at, targets):
    for t in targets:
        for part in range(0, NEAR, 9):
            row = [code[t, part + s] for s in range(9)]
            for x in row:
                for n in range(2):
                    lists[n][at[n]] = x
                    at[n] = at[n] + ((x >> (16 + n)) & 1)
        for n in range(2):
            lists[n][at[n]] = t << 8 | (n + 1) * LD
            at[n] = (at[n] + 1) & -2


def low_body(place, code, nodes_in, up_in, coupling_in, _, top, field, own, halo, sizes, __, nodes, up, coupling, held, sems):
    moves = ((nodes_in, nodes), (up_in.at[pl.ds(0, 4)], up), (coupling_in.at[pl.ds(0, 4)], coupling))
    copies = load([pltpu.make_async_copy(a, b, sems.at[n]) for n, (a, b) in enumerate(moves)])
    lists, at = (own, halo), [jnp.int32(0)] * 2
    list_slots(code, lists, at, range(LD // 2))
    for copy in copies:
        copy.wait()
    levels = [nodes[...]]
    for h in range(4):
        levels.append(raise_nodes(levels[h], (up[h, 0], up[h, 1])))
    list_slots(code, lists, at, range(LD // 2, LD))
    for n in range(2):
        for i in range(2 * UNROLL):
            lists[n][at[n] + i] = LD << 8 | (n + 1) * LD
        sizes[n] = (at[n] // 2 + UNROLL - 1) // UNROLL
    packed = levels[4].astype(BF).reshape(R, 2 * K)
    for i in range(top.shape[0]):
        top[i] = packed
    start = 0
    for h in range(4):
        held[start : start + (LOW >> h)] = levels[h].astype(F32)
        start += LOW >> h
    me = place[0] & (LOW - 1)
    start = 0
    out = []
    for h in range(4):
        q = me >> h
        near, far = unpack(held[(q ^ 2) + start]), unpack(held[(q ^ 3) + start])
        out.append(dot2(near, coupling[h, 0]) + dot2(far, coupling[h, 1]))
        start += LOW >> h
    for h in range(4):
        field[h] = out[h]


def low_tree(place, code, nodes, up, coupling, sent, blocks):
    return pl.pallas_call(
        low_body,
        in_specs=[SMEM] * 2 + [ANY] * 4,
        out_specs=[VMEM, VMEM, SMEM, SMEM, SMEM, ANY],
        out_shape=[
            sds((blocks, R, 2 * K), BF),
            sds((4, R, K), F32),
            sds((SLOTS,), jnp.int32),
            sds((SLOTS,), jnp.int32),
            sds((2,), jnp.int32),
            sds(sent.shape, sent.dtype),
        ],
        input_output_aliases={5: 5},
        scratch_shapes=[
            pltpu.VMEM((LOW, R // 2, 2 * K), BF),
            pltpu.VMEM((4, 2, K, K), BF),
            pltpu.VMEM((4, 2, K, K), BF),
            pltpu.VMEM((2 * LOW, R // 2, 2 * K), F32),
            pltpu.SemaphoreType.DMA((3,)),
        ],
        compiler_params=params(),
        name="coarse_low",
    )(place, code, nodes, up, coupling, sent)


def split2(x):
    hi = x.astype(BF)
    return hi, (x - hi.astype(F32)).astype(BF)


def spread_features(table, feats, count):
    lane = lax.broadcasted_iota(jnp.int32, (M, M), 1)
    ones = 3 * len(PARTS) + 3
    feats[count] = jnp.where((lane >= ones) & (lane < ones + 3), 1.0, 0.0).astype(BF)
    expand = [expansion(i) for i in range(8)]
    for o in range(count // 8):
        rows = jnp.concatenate([table[8 * o + i, R:ROWS, :] for i in range(8)], axis=0)
        spread = [dot(rows, expand[i]).astype(BF) for i in range(8)]
        for i in range(8):
            feats[8 * o + i] = spread[i]


def near_loop(steps, slots, table, feats, target, acc):
    pad = jnp.zeros((M - FX, M), BF)

    def near(it, _):
        t, kernels, weights = [], [], []
        for u in range(UNROLL):
            place_of = (it * UNROLL + u) * 2
            one, two = slots[place_of], slots[place_of + 1]
            s0, s1 = one & 255, two & 255
            t.append((one >> 8) & 255)
            rows = jnp.concatenate([feats[s0], feats[s1]], axis=0)
            square = dot(rows, jnp.concatenate([target[jnp.minimum(t[u], LD - 1)], pad], axis=0))
            kernels.append(lax.rsqrt(square).astype(BF))
            weights.append(jnp.concatenate([table[s0, 0:R, :], table[s1, 0:R, :]], axis=1))
        terms = [dot(weights[u], kernels[u]) for u in range(UNROLL)]
        for u in range(UNROLL):
            acc[t[u]] += terms[u]
        return 0

    lax.fori_loop(0, steps, near, 0)


def own_body(sizes, slots, target_in, sent, acc, table, feats, target, sems):
    moves = ((sent.at[pl.ds(0, LD)], table.at[pl.ds(0, LD)]), (target_in, target))
    copies = load([pltpu.make_async_copy(a, b, sems.at[n]) for n, (a, b) in enumerate(moves)])
    acc[...] = jnp.zeros(acc.shape, F32)
    table[LD] = jnp.zeros((ROWS, M), BF)
    for copy in copies:
        copy.wait()
    spread_features(table, feats, LD)
    near_loop(sizes[0], slots, table, feats, target, acc)


def near_own(sizes, slots, target, sent):
    return pl.pallas_call(
        own_body,
        in_specs=[SMEM] * 2 + [ANY] * 2,
        out_specs=VMEM,
        out_shape=sds((LD + 1, R, M), F32),
        scratch_shapes=[
            pltpu.VMEM((LD + 1, ROWS, M), BF),
            pltpu.VMEM((LD + 1, M, M), BF),
            pltpu.VMEM((LD, FX, M), BF),
            pltpu.SemaphoreType.DMA((2,)),
        ],
        compiler_params=params(63.5),
        cost_estimate=pl.CostEstimate(flops=2 << 30, bytes_accessed=2 << 20, transcendentals=4 << 20),
        name="near_own",
    )(sizes, slots, target, sent)


def fields_body(sizes, slots, leaf_sources, leaf_classes, box_sources, box_classes, place, low_field, down, coupling, near_in, target_in, matrices_in, box_matrices_in, left, mine, right, acc, leaf_field, box_field, base, tip, table, coefs, feats, target, matrices, box_matrices, low, high, sems):
    blocks = SENT - LD
    sources = (left, mine, right)
    moves = [(left.at[pl.ds(0, LD)], table.at[pl.ds(0, LD)]), (right.at[pl.ds(0, LD)], table.at[pl.ds(LD, LD)])]
    moves += [(src.at[pl.ds(LD, blocks)], coefs.at[pl.ds(n * blocks, blocks)]) for n, src in enumerate(sources)]
    moves += [(target_in, target), (matrices_in, matrices), (box_matrices_in, box_matrices), (near_in, acc)]
    copies = load([pltpu.make_async_copy(a, b, sems.at[n]) for n, (a, b) in enumerate(moves)])
    me = place[0]
    total = low_field[3]
    chain = down[3, (me >> 3) & 1].astype(F32)
    for h in range(2, -1, -1):
        both = dot2(jnp.concatenate([total, chain], axis=0), down[h, (me >> h) & 1])
        total = low_field[h] + both[:R]
        chain = both[R:]
    tips = []
    for h in range(4, 8):
        hi, lo = split2(chain)
        stack = jnp.concatenate([coupling[h, 0], coupling[h, 1], down[min(h, 6), (me >> h) & 1]], axis=0)
        product = dot(stack, hi) + dot(stack, lo)
        tips.append((split2(product[0:K]), split2(product[K : 2 * K])))
        chain = product[2 * K :]
    base[...] = total
    for h in range(4):
        for i in range(2):
            for n in range(2):
                tip[h, i, n] = tips[h][i][n]

    table[BOTH] = jnp.zeros((ROWS, M), BF)
    for copy in copies:
        copy.wait()

    first = lax.broadcasted_iota(jnp.int32, (R, 2 * K), 1) < K
    for n in range(3):
        for group in range(PAIRS // 5):
            ready = []
            for i in range(5 * group, 5 * group + 5):
                x = jnp.concatenate(
                    [coefs[n * blocks + b, r : r + 16, :] for b, r in coef_places(i)], axis=0
                ).astype(F32)
                y = pltpu.roll(x, K, 1)
                ready.append(
                    [
                        jnp.where(first, x, 0.0).astype(BF),
                        jnp.where(first, y, 0.0).astype(BF),
                        jnp.where(first, 0.0, y).astype(BF),
                        jnp.where(first, 0.0, x).astype(BF),
                    ]
                )
            for i in range(5):
                at_row = 2 * (5 * group + i)
                row = n * LD + at_row if at_row < LD else ALL + n * BX + at_row - LD
                low[row], low[row + 1], high[row], high[row + 1] = ready[i]

    def gather(source, kind, mats, width):
        total = jnp.zeros((R, K), F32)
        for g in range(width // 4):
            s = [source(4 * g + i) for i in range(4)]
            vec = jnp.concatenate([low[s[0]] + high[s[1]], low[s[2]] + high[s[3]]], axis=1)
            mat = jnp.concatenate([mats[kind(4 * g + i)] for i in range(4)], axis=0)
            total = total + dot(vec, mat)
        return total

    def couple(it, _):
        rows = [it * 8 + u for u in range(8)]
        got = [
            gather(
                lambda a: leaf_sources[a, row] - (me - 1) * LD, lambda a: leaf_classes[a, row], matrices, ADM
            )
            for row in rows
        ]
        for row, value in zip(rows, got):
            leaf_field[row] = value
        return 0

    lax.fori_loop(0, LD // 8, couple, 0)
    got = [
        gather(
            lambda a: box_sources[box, a] - (me - 1) * BX + ALL, lambda a: box_classes[box, a], box_matrices, ADMB
        )
        for box in range(BX)
    ]
    for box in range(BX):
        box_field[box] = got[box]

    spread_features(table, feats, BOTH)
    near_loop(sizes[1], slots, table, feats, target, acc)


def fields(indices, place, low_field, down, coupling, near_part, target, matrices, box_matrices, sents):
    return pl.pallas_call(
        fields_body,
        in_specs=[SMEM] * 7 + [VMEM] * 3 + [ANY] * 7,
        out_specs=[VMEM] * 5,
        out_shape=[
            sds((LD + 1, R, M), F32),
            sds((LD, R, K), F32),
            sds((BX, R, K), F32),
            sds((R, K), F32),
            sds((4, 2, 2, K, K), BF),
        ],
        scratch_shapes=[
            pltpu.VMEM((BOTH + 1, ROWS, M), BF),
            pltpu.VMEM((3 * (SENT - LD), ROWS, M), BF),
            pltpu.VMEM((BOTH + 1, M, M), BF),
            pltpu.VMEM((LD, FX, M), BF),
            pltpu.VMEM((matrices.shape[0], K, K), BF),
            pltpu.VMEM((matrices.shape[0], K, K), BF),
            pltpu.VMEM((6 * PAIRS, R, 2 * K), BF),
            pltpu.VMEM((6 * PAIRS, R, 2 * K), BF),
            pltpu.SemaphoreType.DMA((9,)),
        ],
        compiler_params=params(),
        cost_estimate=pl.CostEstimate(flops=8 << 30, bytes_accessed=4 << 20, transcendentals=8 << 20),
        name="near_and_coupled_fields",
    )(*indices, place, low_field, down, coupling, near_part, target, matrices, box_matrices, *sents)


def final_body(place, nodes_in, up_in, base_in, tip_in, parents, leaf_field_in, box_field_in, box_down_in, leaf_down_in, basis_in, near_in, out, boxes, held, nodes, up, base, tip, box_field, box_down, leaf_field, leaf_down, basis, near_part, sems):
    moves = ((nodes_in, nodes), (up_in.at[pl.ds(4, 3)], up), (base_in, base), (tip_in, tip))
    moves += ((box_field_in, box_field), (box_down_in, box_down), (leaf_down_in, leaf_down))
    moves += ((leaf_field_in, leaf_field), (basis_in, basis), (near_in, near_part))
    copies = load([pltpu.make_async_copy(a, b, sems.at[n]) for n, (a, b) in enumerate(moves)])
    for copy in copies[:4]:
        copy.wait()
    levels = [nodes[...].reshape(LOW, R // 2, 2 * K)]
    for h in range(3):
        levels.append(raise_nodes(levels[h], (up[h, 0], up[h, 1])))
    start = 0
    for h in range(4):
        held[start : start + (LOW >> h)] = levels[h].astype(F32)
        start += LOW >> h
    me = (place[0] >> 4) & (LOW - 1)
    total = base[...]
    start = 0
    for h in range(4):
        for i in range(2):
            hi, lo = split2(unpack(held[((me >> h) ^ (2 + i)) + start]))
            total = total + (dot(hi, tip[h, i, 0]) + dot(hi, tip[h, i, 1]) + dot(lo, tip[h, i, 0]))
        start += LOW >> h
    for copy in copies[4:]:
        copy.wait()
    group = total.astype(BF)
    got = [(box_field[box] + dot(group, box_down[box])).astype(BF) for box in range(BX)]
    for box in range(BX):
        boxes[box] = got[box]
    for part in range(LD // 8):
        leaves = range(8 * part, 8 * part + 8)
        field = [
            (leaf_field[leaf] + dot(boxes[parents[leaf]], leaf_down[leaf])).astype(BF) for leaf in leaves
        ]
        got = [
            near_part[leaf] + dot(field[i], basis[:, pl.ds(leaf * M, M)]) for i, leaf in enumerate(leaves)
        ]
        for i, leaf in enumerate(leaves):
            out[:, pl.ds(leaf * M, M)] = got[i]


def finish(place, nodes, up, base, tip, parents, leaf_field, box_field, box_down, leaf_down, basis, near_part):
    return pl.pallas_call(
        final_body,
        in_specs=[SMEM] + [ANY] * 4 + [SMEM] + [ANY] * 6,
        out_specs=VMEM,
        out_shape=sds((R, LD * M), F32),
        scratch_shapes=[
            pltpu.VMEM((BX, R, K), BF),
            pltpu.VMEM((2 * LOW, R // 2, 2 * K), F32),
            pltpu.VMEM(nodes.shape, BF),
            pltpu.VMEM((3, 2, K, K), BF),
            pltpu.VMEM((R, K), F32),
            pltpu.VMEM((4, 2, 2, K, K), BF),
            pltpu.VMEM((BX, R, K), F32),
            pltpu.VMEM((BX, K, K), BF),
            pltpu.VMEM((LD, R, K), F32),
            pltpu.VMEM((LD, K, K), BF),
            pltpu.VMEM((K, LD * M), BF),
            pltpu.VMEM((LD + 1, R, M), F32),
            pltpu.SemaphoreType.DMA((10,)),
        ],
        compiler_params=params(),
        name="group_to_points",
    )(place, nodes, up, base, tip, parents, leaf_field, box_field, box_down, leaf_down, basis, near_part)


def exchange(x):
    count = lax.axis_size(AXES)
    left = lax.ppermute(x, AXES, [(i, i + 1) for i in range(count - 1)])
    right = lax.ppermute(x, AXES, [(i + 1, i) for i in range(count - 1)])
    return left, right


def gather_groups(copies, groups):
    return lax.all_to_all(copies, AXES, 0, 0, axis_index_groups=groups, tiled=True)


def local(
    charges,
    points,
    leaf_basis,
    leaf_parent,
    leaf_up,
    leaf_down,
    box_up,
    box_down,
    top_up,
    top_down,
    top_coupling,
    leaf_sources,
    leaf_classes,
    leaf_coupling,
    box_sources,
    box_classes,
    box_coupling,
    near_leaves,
    near_count,
):
    device = lax.axis_index(AXES)
    place = device.astype(jnp.int32).reshape(1)
    parents = leaf_parent[0]

    sent, target, ascent = first(charges, points, leaf_basis, leaf_up, box_up, parents)

    blocks = lax.axis_size(AXES) // LOW
    low_groups = [[b * LOW + i for i in range(LOW)] for b in range(blocks)]
    high_groups = [[b * LOW + i for b in range(blocks)] for i in range(LOW)]
    rel = near_leaves - device * LD
    mine = (rel >= 0) & (rel < LD)
    used = jnp.arange(NEAR, dtype=jnp.int32)[None, :] < near_count[:, None]
    row = jnp.where(rel < 0, rel + LD, rel)
    leaf_ids = jnp.arange(LD, dtype=jnp.int32)[:, None]
    code = row | leaf_ids << 8 | jnp.where(used, jnp.where(mine, 1, 2), 0) << 16

    low_nodes = gather_groups(ascent, low_groups)
    top, low_field, own, halo, sizes, sent = low_tree(
        place, code, low_nodes, top_up, top_coupling, sent, blocks
    )
    high_nodes = gather_groups(top, high_groups)
    sent_left, sent_right = exchange(sent)
    near_part = near_own(sizes, own, target, sent)

    near_part, leaf_field, box_field, base, tip = fields(
        (sizes, halo, leaf_sources.T, leaf_classes.T, box_sources, box_classes),
        place,
        low_field,
        top_down,
        top_coupling,
        near_part,
        target,
        leaf_coupling,
        box_coupling,
        (sent_left, sent, sent_right),
    )
    return finish(
        place, high_nodes, top_up, base, tip, parents, leaf_field, box_field, box_down, leaf_down, leaf_basis, near_part
    )


def solution(mesh):
    split = P(AXES)
    return jax.shard_map(
        local,
        mesh=mesh,
        in_specs=(
            P(None, AXES),
            P(None, AXES),
            P(None, AXES),
            split,
            split,
            split,
            split,
            split,
            P(),
            P(),
            P(),
            split,
            split,
            P(),
            split,
            split,
            P(),
            split,
            split,
        ),
        out_specs=P(None, AXES),
        check_vma=False,
    )
```

```python
import math

import jax
import jax.numpy as jnp
import numpy as np
from jax import lax
from jax.experimental import pallas as pl
from jax.experimental.pallas import tpu as pltpu
from jax.sharding import PartitionSpec as P

BF = jnp.bfloat16
F32 = jnp.float32
AXES = ("box", "rhs")

R = 64
K = 64
M = 128
LD = 24
BX = 6
ADM = 16
ADMB = 8
NEAR = 27
FR = 16
ROWS = R + FR
FX = 32
UNROLL = 16
LOW = 32
PAIRS = (LD + BX) // 2
SENT = LD + PAIRS * R // ROWS
SLOTS = LD * (NEAR + 1) + 2 * UNROLL + 32
ALL = 3 * LD
BOTH = 2 * LD

DELTA2 = 0.0001
INV_SCALE = 2.0 * math.sqrt(NEAR * M)
CENTRE = 1.1

PARTS = ((0, 0), (0, 1), (0, 2), (1, 0), (1, 1), (1, 2), (2, 0), (2, 1))

VMEM = pl.BlockSpec(memory_space=pltpu.VMEM)
SMEM = pl.BlockSpec(memory_space=pltpu.SMEM)
ANY = pl.BlockSpec(memory_space=pl.ANY)
HBM = pl.BlockSpec(memory_space=pltpu.HBM)


def params(mib=60.0):
    return pltpu.CompilerParams(vmem_limit_bytes=int(mib * 1024 * 1024))


def sds(shape, dtype):
    return jax.ShapeDtypeStruct(shape, dtype)


def dot(a, b):
    return jnp.dot(a, b, preferred_element_type=F32)


def dot_nt(a, b):
    return lax.dot_general(a, b, (((1,), (1,)), ((), ())), preferred_element_type=F32)


def dot2(x, m):
    hi = x.astype(BF)
    lo = (x - hi.astype(F32)).astype(BF)
    return dot(hi, m) + dot(lo, m)


def expansion(leaf):
    row = lax.broadcasted_iota(jnp.int32, (8 * FR, M), 0) - FR * leaf
    e = lax.broadcasted_iota(jnp.int32, (8 * FR, M), 1)
    third = (e * 43) >> 7
    part = jnp.where(e < 9, 0, jnp.where(e < 18, 3, 6))
    source = jnp.where(e < 24, part + e - 3 * third, jnp.where(e < 27, e - 15, jnp.where(e < 30, 12, -M)))
    return jnp.where(row == source, 1.0, 0.0).astype(BF)


def split3(x):
    hi = x.astype(BF).astype(F32)
    rest = x - hi
    mid = rest.astype(BF).astype(F32)
    return hi, mid, rest - mid


def load(copies):
    for copy in copies:
        copy.start()
    return copies


def climb_body(charges_in, basis_in, leaf_up_in, box_up_in, parents, coef, ascent, charges, basis, leaf_up, box_up, acc, sems):
    moves = ((charges_in, charges), (basis_in, basis), (leaf_up_in, leaf_up), (box_up_in, box_up))
    copies = load([pltpu.make_async_copy(a, b, sems.at[n]) for n, (a, b) in enumerate(moves)])
    acc[...] = jnp.zeros(acc.shape, F32)
    copies[0].wait()
    copies[1].wait()
    copies[2].wait()
    for group in range(LD // 8):
        leaves = range(8 * group, 8 * group + 8)
        c = [dot_nt(charges[:, pl.ds(leaf * M, M)], basis[:, pl.ds(leaf * M, M)]) for leaf in leaves]
        raised = [dot(c[i].astype(BF), leaf_up[leaf]) for i, leaf in enumerate(leaves)]
        for i in range(0, 8, 2):
            put_coef(coef, (8 * group + i) // 2, jnp.concatenate([c[i], c[i + 1]], axis=1).astype(BF))
        for i, leaf in enumerate(leaves):
            acc[parents[leaf]] += raised[i]
    copies[3].wait()
    boxes = [acc[box] for box in range(BX)]
    raised = [dot(boxes[box].astype(BF), box_up[box]) for box in range(BX)]
    total = raised[0] + raised[1] + (raised[2] + raised[3]) + (raised[4] + raised[5])
    packed = jnp.concatenate([total[: R // 2], total[R // 2 :]], axis=1).astype(BF)
    for i in range(LOW):
        ascent[i] = packed
    for box in range(0, BX, 2):
        put_coef(coef, (LD + box) // 2, jnp.concatenate([boxes[box], boxes[box + 1]], axis=1).astype(BF))


def list_slots(code, lists, at, targets):
    for t in targets:
        for part in range(0, NEAR, 9):
            row = [code[t, part + s] for s in range(9)]
            for x in row:
                for n in range(2):
                    lists[n][at[n]] = x
                    at[n] = at[n] + ((x >> (16 + n)) & 1)
        for n in range(2):
            lists[n][at[n]] = t << 8 | (n + 1) * LD
            at[n] = (at[n] + 1) & -2


def pack_body(code, charges_in, points_in, coef_in, sent, target, own, halo, sizes, charges, points, feat, wide, sems):
    moves = ((points_in, points), (charges_in, charges), (coef_in, sent.at[pl.ds(LD, SENT - LD)]))
    copies = load([pltpu.make_async_copy(a, b, sems.at[n]) for n, (a, b) in enumerate(moves)])
    lists, at = (own, halo), [jnp.int32(0)] * 2
    list_slots(code, lists, at, range(LD // 3))
    for copy in copies:
        copy.wait()
    p = (points[...] - CENTRE) * INV_SCALE
    parts = split3(p)
    norm = p[0:1] * p[0:1] + p[1:2] * p[1:2] + p[2:3] * p[2:3]
    source_norm = split3(norm)
    target_norm = split3(norm + DELTA2 * INV_SCALE * INV_SCALE)
    feat[...] = jnp.zeros(feat.shape, F32)
    wide[...] = jnp.zeros(wide.shape, F32)
    one = jnp.ones(norm.shape, F32)
    for a in range(3):
        feat[3 * a : 3 * a + 3, :] = parts[a]
        feat[9 + a : 10 + a, :] = source_norm[a]
    feat[12:13, :] = one
    for n, (_, b) in enumerate(PARTS):
        wide[3 * n : 3 * n + 3, :] = -2.0 * parts[b]
    base = 3 * len(PARTS)
    for a in range(3):
        wide[base + a : base + a + 1, :] = one
        wide[base + 3 + a : base + 4 + a, :] = target_norm[a]
    turned = []
    for o in range(LD // 8):
        rows = jnp.concatenate([feat[:, pl.ds((8 * o + i) * M, M)] for i in range(8)], axis=0)
        turned.append(rows.T.astype(BF))
    for leaf in range(LD):
        cols = pl.ds(leaf * M, M)
        sent[leaf, 0:R, :] = charges[:, cols]
        i = leaf % 8
        sent[leaf, R:ROWS, :] = turned[leaf // 8][FR * i : FR * (i + 1), :]
        target[leaf, :, :] = wide[:, cols].astype(BF)
    list_slots(code, lists, at, range(LD // 3, LD))
    for n in range(2):
        for i in range(2 * UNROLL):
            lists[n][at[n] + i] = LD << 8 | (n + 1) * LD
        sizes[n] = (at[n] // 2 + UNROLL - 1) // UNROLL


def coef_places(pair):
    rows = [pair * R + 16 * i for i in range(R // 16)]
    return [(r // ROWS, r % ROWS) for r in rows]


def put_coef(coef, pair, value):
    for i, (block, row) in enumerate(coef_places(pair)):
        coef[block, row : row + 16, :] = value[16 * i : 16 * i + 16]


def climb(charges, basis, leaf_up, box_up, parents):
    return pl.pallas_call(
        climb_body,
        in_specs=[HBM] * 4 + [SMEM],
        out_specs=[VMEM] * 2,
        out_shape=[sds((SENT - LD, ROWS, M), BF), sds((LOW, R // 2, 2 * K), BF)],
        scratch_shapes=[
            pltpu.VMEM((R, LD * M), BF),
            pltpu.VMEM((K, LD * M), BF),
            pltpu.VMEM((LD, K, K), BF),
            pltpu.VMEM((BX, K, K), BF),
            pltpu.VMEM((BX, R, K), F32),
            pltpu.SemaphoreType.DMA((4,)),
        ],
        compiler_params=params(),
        name="points_to_group",
    )(charges, basis, leaf_up, box_up, parents)


def pack(code, charges, points, coef):
    return pl.pallas_call(
        pack_body,
        in_specs=[SMEM] + [HBM] * 3,
        out_specs=[VMEM] * 2 + [SMEM] * 3,
        out_shape=[
            sds((SENT, ROWS, M), BF),
            sds((LD, FX, M), BF),
            sds((SLOTS,), jnp.int32),
            sds((SLOTS,), jnp.int32),
            sds((2,), jnp.int32),
        ],
        scratch_shapes=[
            pltpu.VMEM((R, LD * M), BF),
            pltpu.VMEM((3, LD * M), F32),
            pltpu.VMEM((FR, LD * M), F32),
            pltpu.VMEM((FX, LD * M), F32),
            pltpu.SemaphoreType.DMA((3,)),
        ],
        compiler_params=params(),
        cost_estimate=pl.CostEstimate(flops=4 << 30, bytes_accessed=4 << 20, transcendentals=0),
        name="pack_and_list",
    )(code, charges, points, coef)


def twice(m):
    zero = jnp.zeros_like(m)
    return jnp.concatenate([jnp.concatenate([m, zero], axis=1), jnp.concatenate([zero, m], axis=1)], axis=0)


def unpack(x):
    return jnp.concatenate([x[:, :K], x[:, K:]], axis=0)


def raise_nodes(nodes, matrices):
    count = nodes.shape[0] // 2
    left = jnp.concatenate([nodes[2 * i] for i in range(count)], axis=0)
    right = jnp.concatenate([nodes[2 * i + 1] for i in range(count)], axis=0)
    mul = dot if nodes.dtype == BF else dot2
    return (mul(left, twice(matrices[0])) + mul(right, twice(matrices[1]))).reshape(count, R // 2, 2 * K)


def low_body(place, nodes_in, up_in, coupling_in, _, top, field, __, nodes, up, coupling, held, sems):
    moves = ((nodes_in, nodes), (up_in.at[pl.ds(0, 4)], up), (coupling_in.at[pl.ds(0, 4)], coupling))
    copies = load([pltpu.make_async_copy(a, b, sems.at[n]) for n, (a, b) in enumerate(moves)])
    for copy in copies:
        copy.wait()
    levels = [nodes[...]]
    for h in range(4):
        levels.append(raise_nodes(levels[h], (up[h, 0], up[h, 1])))
    packed = levels[4].astype(BF).reshape(R, 2 * K)
    for i in range(top.shape[0]):
        top[i] = packed
    start = 0
    for h in range(4):
        held[start : start + (LOW >> h)] = levels[h].astype(F32)
        start += LOW >> h
    me = place[0] & (LOW - 1)
    start = 0
    out = []
    for h in range(4):
        q = me >> h
        near, far = unpack(held[(q ^ 2) + start]), unpack(held[(q ^ 3) + start])
        out.append(dot2(near, coupling[h, 0]) + dot2(far, coupling[h, 1]))
        start += LOW >> h
    for h in range(4):
        field[h] = out[h]


def low_tree(place, nodes, up, coupling, sent, blocks):
    return pl.pallas_call(
        low_body,
        in_specs=[SMEM] + [ANY] * 4,
        out_specs=[VMEM, VMEM, ANY],
        out_shape=[
            sds((blocks, R, 2 * K), BF),
            sds((4, R, K), F32),
            sds(sent.shape, sent.dtype),
        ],
        input_output_aliases={4: 2},
        scratch_shapes=[
            pltpu.VMEM((LOW, R // 2, 2 * K), BF),
            pltpu.VMEM((4, 2, K, K), BF),
            pltpu.VMEM((4, 2, K, K), BF),
            pltpu.VMEM((2 * LOW, R // 2, 2 * K), F32),
            pltpu.SemaphoreType.DMA((3,)),
        ],
        compiler_params=params(),
        name="coarse_low",
    )(place, nodes, up, coupling, sent)


def split2(x):
    hi = x.astype(BF)
    return hi, (x - hi.astype(F32)).astype(BF)


def spread_features(table, feats, count):
    lane = lax.broadcasted_iota(jnp.int32, (M, M), 1)
    ones = 3 * len(PARTS) + 3
    feats[count] = jnp.where((lane >= ones) & (lane < ones + 3), 1.0, 0.0).astype(BF)
    expand = [expansion(i) for i in range(8)]
    for o in range(count // 8):
        rows = jnp.concatenate([table[8 * o + i, R:ROWS, :] for i in range(8)], axis=0)
        spread = [dot(rows, expand[i]).astype(BF) for i in range(8)]
        for i in range(8):
            feats[8 * o + i] = spread[i]


def near_loop(steps, slots, table, feats, target, acc):
    pad = jnp.zeros((M - FX, M), BF)

    def near(it, _):
        t, kernels, weights = [], [], []
        for u in range(UNROLL):
            place_of = (it * UNROLL + u) * 2
            one, two = slots[place_of], slots[place_of + 1]
            s0, s1 = one & 255, two & 255
            t.append((one >> 8) & 255)
            rows = jnp.concatenate([feats[s0], feats[s1]], axis=0)
            square = dot(rows, jnp.concatenate([target[jnp.minimum(t[u], LD - 1)], pad], axis=0))
            kernels.append(lax.rsqrt(square).astype(BF))
            weights.append(jnp.concatenate([table[s0, 0:R, :], table[s1, 0:R, :]], axis=1))
        terms = [dot(weights[u], kernels[u]) for u in range(UNROLL)]
        for u in range(UNROLL):
            acc[t[u]] += terms[u]
        return 0

    lax.fori_loop(0, steps, near, 0)


def own_body(sizes, slots, target_in, sent, acc, table, feats, target, sems):
    moves = ((sent.at[pl.ds(0, LD)], table.at[pl.ds(0, LD)]), (target_in, target))
    copies = load([pltpu.make_async_copy(a, b, sems.at[n]) for n, (a, b) in enumerate(moves)])
    acc[...] = jnp.zeros(acc.shape, F32)
    table[LD] = jnp.zeros((ROWS, M), BF)
    for copy in copies:
        copy.wait()
    spread_features(table, feats, LD)
    near_loop(sizes[0], slots, table, feats, target, acc)


def near_own(sizes, slots, target, sent):
    return pl.pallas_call(
        own_body,
        in_specs=[SMEM] * 2 + [ANY] * 2,
        out_specs=VMEM,
        out_shape=sds((LD + 1, R, M), F32),
        scratch_shapes=[
            pltpu.VMEM((LD + 1, ROWS, M), BF),
            pltpu.VMEM((LD + 1, M, M), BF),
            pltpu.VMEM((LD, FX, M), BF),
            pltpu.SemaphoreType.DMA((2,)),
        ],
        compiler_params=params(63.5),
        cost_estimate=pl.CostEstimate(flops=2 << 30, bytes_accessed=2 << 20, transcendentals=4 << 20),
        name="near_own",
    )(sizes, slots, target, sent)


def fields_body(sizes, slots, leaf_sources, leaf_classes, box_sources, box_classes, place, low_field, down, coupling, near_in, target_in, matrices_in, box_matrices_in, left, mine, right, acc, leaf_field, box_field, base, tip, table, coefs, feats, target, matrices, box_matrices, low, high, sems):
    blocks = SENT - LD
    sources = (left, mine, right)
    moves = [(left.at[pl.ds(0, LD)], table.at[pl.ds(0, LD)]), (right.at[pl.ds(0, LD)], table.at[pl.ds(LD, LD)])]
    moves += [(src.at[pl.ds(LD, blocks)], coefs.at[pl.ds(n * blocks, blocks)]) for n, src in enumerate(sources)]
    moves += [(target_in, target), (matrices_in, matrices), (box_matrices_in, box_matrices), (near_in, acc)]
    copies = load([pltpu.make_async_copy(a, b, sems.at[n]) for n, (a, b) in enumerate(moves)])
    me = place[0]
    total = low_field[3]
    chain = down[3, (me >> 3) & 1].astype(F32)
    for h in range(2, -1, -1):
        both = dot2(jnp.concatenate([total, chain], axis=0), down[h, (me >> h) & 1])
        total = low_field[h] + both[:R]
        chain = both[R:]
    tips = []
    for h in range(4, 8):
        hi, lo = split2(chain)
        stack = jnp.concatenate([coupling[h, 0], coupling[h, 1], down[min(h, 6), (me >> h) & 1]], axis=0)
        product = dot(stack, hi) + dot(stack, lo)
        tips.append((split2(product[0:K]), split2(product[K : 2 * K])))
        chain = product[2 * K :]
    base[...] = total
    for h in range(4):
        for i in range(2):
            for n in range(2):
                tip[h, i, n] = tips[h][i][n]

    table[BOTH] = jnp.zeros((ROWS, M), BF)
    for copy in copies:
        copy.wait()

    first = lax.broadcasted_iota(jnp.int32, (R, 2 * K), 1) < K
    for n in range(3):
        for group in range(PAIRS // 5):
            ready = []
            for i in range(5 * group, 5 * group + 5):
                x = jnp.concatenate(
                    [coefs[n * blocks + b, r : r + 16, :] for b, r in coef_places(i)], axis=0
                ).astype(F32)
                y = pltpu.roll(x, K, 1)
                ready.append(
                    [
                        jnp.where(first, x, 0.0).astype(BF),
                        jnp.where(first, y, 0.0).astype(BF),
                        jnp.where(first, 0.0, y).astype(BF),
                        jnp.where(first, 0.0, x).astype(BF),
                    ]
                )
            for i in range(5):
                at_row = 2 * (5 * group + i)
                row = n * LD + at_row if at_row < LD else ALL + n * BX + at_row - LD
                low[row], low[row + 1], high[row], high[row + 1] = ready[i]

    def gather(source, kind, mats, width):
        total = jnp.zeros((R, K), F32)
        for g in range(width // 4):
            s = [source(4 * g + i) for i in range(4)]
            vec = jnp.concatenate([low[s[0]] + high[s[1]], low[s[2]] + high[s[3]]], axis=1)
            mat = jnp.concatenate([mats[kind(4 * g + i)] for i in range(4)], axis=0)
            total = total + dot(vec, mat)
        return total

    def couple(it, _):
        rows = [it * 8 + u for u in range(8)]
        got = [
            gather(
                lambda a: leaf_sources[a, row] - (me - 1) * LD, lambda a: leaf_classes[a, row], matrices, ADM
            )
            for row in rows
        ]
        for row, value in zip(rows, got):
            leaf_field[row] = value
        return 0

    lax.fori_loop(0, LD // 8, couple, 0)
    got = [
        gather(
            lambda a: box_sources[box, a] - (me - 1) * BX + ALL, lambda a: box_classes[box, a], box_matrices, ADMB
        )
        for box in range(BX)
    ]
    for box in range(BX):
        box_field[box] = got[box]

    spread_features(table, feats, BOTH)
    near_loop(sizes[1], slots, table, feats, target, acc)


def fields(indices, place, low_field, down, coupling, near_part, target, matrices, box_matrices, sents):
    return pl.pallas_call(
        fields_body,
        in_specs=[SMEM] * 7 + [VMEM] * 3 + [ANY] * 7,
        out_specs=[VMEM] * 5,
        out_shape=[
            sds((LD + 1, R, M), F32),
            sds((LD, R, K), F32),
            sds((BX, R, K), F32),
            sds((R, K), F32),
            sds((4, 2, 2, K, K), BF),
        ],
        scratch_shapes=[
            pltpu.VMEM((BOTH + 1, ROWS, M), BF),
            pltpu.VMEM((3 * (SENT - LD), ROWS, M), BF),
            pltpu.VMEM((BOTH + 1, M, M), BF),
            pltpu.VMEM((LD, FX, M), BF),
            pltpu.VMEM((matrices.shape[0], K, K), BF),
            pltpu.VMEM((matrices.shape[0], K, K), BF),
            pltpu.VMEM((6 * PAIRS, R, 2 * K), BF),
            pltpu.VMEM((6 * PAIRS, R, 2 * K), BF),
            pltpu.SemaphoreType.DMA((9,)),
        ],
        compiler_params=params(),
        cost_estimate=pl.CostEstimate(flops=8 << 30, bytes_accessed=4 << 20, transcendentals=8 << 20),
        name="near_and_coupled_fields",
    )(*indices, place, low_field, down, coupling, near_part, target, matrices, box_matrices, *sents)


def final_body(place, nodes_in, up_in, base_in, tip_in, parents, leaf_field_in, box_field_in, box_down_in, leaf_down_in, basis_in, near_in, out, boxes, held, nodes, up, base, tip, box_field, box_down, leaf_field, leaf_down, basis, near_part, sems):
    moves = ((nodes_in, nodes), (up_in.at[pl.ds(4, 3)], up), (base_in, base), (tip_in, tip))
    moves += ((box_field_in, box_field), (box_down_in, box_down), (leaf_down_in, leaf_down))
    moves += ((leaf_field_in, leaf_field), (basis_in, basis), (near_in, near_part))
    copies = load([pltpu.make_async_copy(a, b, sems.at[n]) for n, (a, b) in enumerate(moves)])
    for copy in copies[:4]:
        copy.wait()
    levels = [nodes[...].reshape(LOW, R // 2, 2 * K)]
    for h in range(3):
        levels.append(raise_nodes(levels[h], (up[h, 0], up[h, 1])))
    start = 0
    for h in range(4):
        held[start : start + (LOW >> h)] = levels[h].astype(F32)
        start += LOW >> h
    me = (place[0] >> 4) & (LOW - 1)
    total = base[...]
    start = 0
    for h in range(4):
        for i in range(2):
            hi, lo = split2(unpack(held[((me >> h) ^ (2 + i)) + start]))
            total = total + (dot(hi, tip[h, i, 0]) + dot(hi, tip[h, i, 1]) + dot(lo, tip[h, i, 0]))
        start += LOW >> h
    for copy in copies[4:]:
        copy.wait()
    group = total.astype(BF)
    got = [(box_field[box] + dot(group, box_down[box])).astype(BF) for box in range(BX)]
    for box in range(BX):
        boxes[box] = got[box]
    for part in range(LD // 8):
        leaves = range(8 * part, 8 * part + 8)
        field = [
            (leaf_field[leaf] + dot(boxes[parents[leaf]], leaf_down[leaf])).astype(BF) for leaf in leaves
        ]
        got = [
            near_part[leaf] + dot(field[i], basis[:, pl.ds(leaf * M, M)]) for i, leaf in enumerate(leaves)
        ]
        for i, leaf in enumerate(leaves):
            out[:, pl.ds(leaf * M, M)] = got[i]


def finish(place, nodes, up, base, tip, parents, leaf_field, box_field, box_down, leaf_down, basis, near_part):
    return pl.pallas_call(
        final_body,
        in_specs=[SMEM] + [ANY] * 4 + [SMEM] + [ANY] * 6,
        out_specs=VMEM,
        out_shape=sds((R, LD * M), F32),
        scratch_shapes=[
            pltpu.VMEM((BX, R, K), BF),
            pltpu.VMEM((2 * LOW, R // 2, 2 * K), F32),
            pltpu.VMEM(nodes.shape, BF),
            pltpu.VMEM((3, 2, K, K), BF),
            pltpu.VMEM((R, K), F32),
            pltpu.VMEM((4, 2, 2, K, K), BF),
            pltpu.VMEM((BX, R, K), F32),
            pltpu.VMEM((BX, K, K), BF),
            pltpu.VMEM((LD, R, K), F32),
            pltpu.VMEM((LD, K, K), BF),
            pltpu.VMEM((K, LD * M), BF),
            pltpu.VMEM((LD + 1, R, M), F32),
            pltpu.SemaphoreType.DMA((10,)),
        ],
        compiler_params=params(),
        name="group_to_points",
    )(place, nodes, up, base, tip, parents, leaf_field, box_field, box_down, leaf_down, basis, near_part)


def exchange(x):
    count = lax.axis_size(AXES)
    left = lax.ppermute(x, AXES, [(i, i + 1) for i in range(count - 1)])
    right = lax.ppermute(x, AXES, [(i + 1, i) for i in range(count - 1)])
    return left, right


def gather_groups(copies, groups):
    return lax.all_to_all(copies, AXES, 0, 0, axis_index_groups=groups, tiled=True)


def local(
    charges,
    points,
    leaf_basis,
    leaf_parent,
    leaf_up,
    leaf_down,
    box_up,
    box_down,
    top_up,
    top_down,
    top_coupling,
    leaf_sources,
    leaf_classes,
    leaf_coupling,
    box_sources,
    box_classes,
    box_coupling,
    near_leaves,
    near_count,
):
    device = lax.axis_index(AXES)
    place = device.astype(jnp.int32).reshape(1)
    parents = leaf_parent[0]

    coef, ascent = climb(charges, leaf_basis, leaf_up, box_up, parents)

    blocks = lax.axis_size(AXES) // LOW
    low_groups = [[b * LOW + i for i in range(LOW)] for b in range(blocks)]
    high_groups = [[b * LOW + i for b in range(blocks)] for i in range(LOW)]
    rel = near_leaves - device * LD
    mine = (rel >= 0) & (rel < LD)
    used = jnp.arange(NEAR, dtype=jnp.int32)[None, :] < near_count[:, None]
    row = jnp.where(rel < 0, rel + LD, rel)
    leaf_ids = jnp.arange(LD, dtype=jnp.int32)[:, None]
    code = row | leaf_ids << 8 | jnp.where(used, jnp.where(mine, 1, 2), 0) << 16

    low_nodes = gather_groups(ascent, low_groups)
    sent, target, own, halo, sizes = pack(code, charges, points, coef)
    top, low_field, sent = low_tree(place, low_nodes, top_up, top_coupling, sent, blocks)
    high_nodes = gather_groups(top, high_groups)
    sent_left, sent_right = exchange(sent)
    near_part = near_own(sizes, own, target, sent)

    near_part, leaf_field, box_field, base, tip = fields(
        (sizes, halo, leaf_sources.T, leaf_classes.T, box_sources, box_classes),
        place,
        low_field,
        top_down,
        top_coupling,
        near_part,
        target,
        leaf_coupling,
        box_coupling,
        (sent_left, sent, sent_right),
    )
    return finish(
        place, high_nodes, top_up, base, tip, parents, leaf_field, box_field, box_down, leaf_down, leaf_basis, near_part
    )


def solution(mesh):
    split = P(AXES)
    return jax.shard_map(
        local,
        mesh=mesh,
        in_specs=(
            P(None, AXES),
            P(None, AXES),
            P(None, AXES),
            split,
            split,
            split,
            split,
            split,
            P(),
            P(),
            P(),
            split,
            split,
            P(),
            split,
            split,
            P(),
            split,
            split,
        ),
        out_specs=P(None, AXES),
        check_vma=False,
    )
```

```python
import math

import jax
import jax.numpy as jnp
import numpy as np
from jax import lax
from jax.experimental import pallas as pl
from jax.experimental.pallas import tpu as pltpu
from jax.sharding import PartitionSpec as P

BF = jnp.bfloat16
F32 = jnp.float32
AXES = ("box", "rhs")

R = 64
K = 64
M = 128
LD = 24
BX = 6
ADM = 16
ADMB = 8
NEAR = 27
FR = 16
ROWS = R + FR
FX = 32
UNROLL = 16
LOW = 32
PAIRS = (LD + BX) // 2
SENT = LD + PAIRS * R // ROWS
SLOTS = LD * (NEAR + 1) + 2 * UNROLL + 32
ALL = 3 * LD
BOTH = 2 * LD

DELTA2 = 0.0001
INV_SCALE = 2.0 * math.sqrt(NEAR * M)
CENTRE = 1.1

PARTS = ((0, 0), (0, 1), (0, 2), (1, 0), (1, 1), (1, 2), (2, 0), (2, 1))

VMEM = pl.BlockSpec(memory_space=pltpu.VMEM)
SMEM = pl.BlockSpec(memory_space=pltpu.SMEM)
ANY = pl.BlockSpec(memory_space=pl.ANY)
HBM = pl.BlockSpec(memory_space=pltpu.HBM)


def params(mib=60.0):
    return pltpu.CompilerParams(vmem_limit_bytes=int(mib * 1024 * 1024))


def sds(shape, dtype):
    return jax.ShapeDtypeStruct(shape, dtype)


def dot(a, b):
    return jnp.dot(a, b, preferred_element_type=F32)


def dot_nt(a, b):
    return lax.dot_general(a, b, (((1,), (1,)), ((), ())), preferred_element_type=F32)


def dot2(x, m):
    hi = x.astype(BF)
    lo = (x - hi.astype(F32)).astype(BF)
    return dot(hi, m) + dot(lo, m)


def expansion(leaf):
    row = lax.broadcasted_iota(jnp.int32, (8 * FR, M), 0) - FR * leaf
    e = lax.broadcasted_iota(jnp.int32, (8 * FR, M), 1)
    third = (e * 43) >> 7
    part = jnp.where(e < 9, 0, jnp.where(e < 18, 3, 6))
    source = jnp.where(e < 24, part + e - 3 * third, jnp.where(e < 27, e - 15, jnp.where(e < 30, 12, -M)))
    return jnp.where(row == source, 1.0, 0.0).astype(BF)


def split3(x):
    hi = x.astype(BF).astype(F32)
    rest = x - hi
    mid = rest.astype(BF).astype(F32)
    return hi, mid, rest - mid


def load(copies):
    for copy in copies:
        copy.start()
    return copies


def climb_body(charges_in, basis_in, leaf_up_in, box_up_in, parents, coef, ascent, charges, basis, leaf_up, box_up, acc, sems):
    moves = ((charges_in, charges), (basis_in, basis), (leaf_up_in, leaf_up), (box_up_in, box_up))
    copies = load([pltpu.make_async_copy(a, b, sems.at[n]) for n, (a, b) in enumerate(moves)])
    acc[...] = jnp.zeros(acc.shape, F32)
    copies[0].wait()
    copies[1].wait()
    copies[2].wait()
    for group in range(LD // 8):
        leaves = range(8 * group, 8 * group + 8)
        c = [dot_nt(charges[:, pl.ds(leaf * M, M)], basis[:, pl.ds(leaf * M, M)]) for leaf in leaves]
        raised = [dot(c[i].astype(BF), leaf_up[leaf]) for i, leaf in enumerate(leaves)]
        for i in range(0, 8, 2):
            put_coef(coef, (8 * group + i) // 2, jnp.concatenate([c[i], c[i + 1]], axis=1).astype(BF))
        for i, leaf in enumerate(leaves):
            acc[parents[leaf]] += raised[i]
    copies[3].wait()
    boxes = [acc[box] for box in range(BX)]
    raised = [dot(boxes[box].astype(BF), box_up[box]) for box in range(BX)]
    total = raised[0] + raised[1] + (raised[2] + raised[3]) + (raised[4] + raised[5])
    packed = jnp.concatenate([total[: R // 2], total[R // 2 :]], axis=1).astype(BF)
    for i in range(LOW):
        ascent[i] = packed
    for box in range(0, BX, 2):
        put_coef(coef, (LD + box) // 2, jnp.concatenate([boxes[box], boxes[box + 1]], axis=1).astype(BF))


def list_slots(code, lists, at, targets):
    for t in targets:
        for part in range(0, NEAR, 9):
            row = [code[t, part + s] for s in range(9)]
            for x in row:
                for n in range(2):
                    lists[n][at[n]] = x
                    at[n] = at[n] + ((x >> (16 + n)) & 1)
        for n in range(2):
            lists[n][at[n]] = t << 8 | (n + 1) * LD
            at[n] = (at[n] + 1) & -2


def pack_body(code, charges_in, points_in, coef_in, sent, target, own, halo, sizes, charges, points, feat, wide, sems):
    moves = ((points_in, points), (charges_in, charges), (coef_in, sent.at[pl.ds(LD, SENT - LD)]))
    copies = load([pltpu.make_async_copy(a, b, sems.at[n]) for n, (a, b) in enumerate(moves)])
    lists, at = (own, halo), [jnp.int32(0)] * 2
    list_slots(code, lists, at, range(LD // 3))
    for copy in copies:
        copy.wait()
    p = (points[...] - CENTRE) * INV_SCALE
    parts = split3(p)
    norm = p[0:1] * p[0:1] + p[1:2] * p[1:2] + p[2:3] * p[2:3]
    source_norm = split3(norm)
    target_norm = split3(norm + DELTA2 * INV_SCALE * INV_SCALE)
    feat[...] = jnp.zeros(feat.shape, F32)
    wide[...] = jnp.zeros(wide.shape, F32)
    one = jnp.ones(norm.shape, F32)
    for a in range(3):
        feat[3 * a : 3 * a + 3, :] = parts[a]
        feat[9 + a : 10 + a, :] = source_norm[a]
    feat[12:13, :] = one
    for n, (_, b) in enumerate(PARTS):
        wide[3 * n : 3 * n + 3, :] = -2.0 * parts[b]
    base = 3 * len(PARTS)
    for a in range(3):
        wide[base + a : base + a + 1, :] = one
        wide[base + 3 + a : base + 4 + a, :] = target_norm[a]
    turned = []
    for o in range(LD // 8):
        rows = jnp.concatenate([feat[:, pl.ds((8 * o + i) * M, M)] for i in range(8)], axis=0)
        turned.append(rows.T.astype(BF))
    for leaf in range(LD):
        cols = pl.ds(leaf * M, M)
        sent[leaf, 0:R, :] = charges[:, cols]
        i = leaf % 8
        sent[leaf, R:ROWS, :] = turned[leaf // 8][FR * i : FR * (i + 1), :]
        target[leaf, :, :] = wide[:, cols].astype(BF)
    list_slots(code, lists, at, range(LD // 3, LD))
    for n in range(2):
        for i in range(2 * UNROLL):
            lists[n][at[n] + i] = LD << 8 | (n + 1) * LD
        sizes[n] = (at[n] // 2 + UNROLL - 1) // UNROLL


def coef_places(pair):
    rows = [pair * R + 16 * i for i in range(R // 16)]
    return [(r // ROWS, r % ROWS) for r in rows]


def put_coef(coef, pair, value):
    for i, (block, row) in enumerate(coef_places(pair)):
        coef[block, row : row + 16, :] = value[16 * i : 16 * i + 16]


def climb(charges, basis, leaf_up, box_up, parents):
    return pl.pallas_call(
        climb_body,
        in_specs=[HBM] * 4 + [SMEM],
        out_specs=[VMEM] * 2,
        out_shape=[sds((SENT - LD, ROWS, M), BF), sds((LOW, R // 2, 2 * K), BF)],
        scratch_shapes=[
            pltpu.VMEM((R, LD * M), BF),
            pltpu.VMEM((K, LD * M), BF),
            pltpu.VMEM((LD, K, K), BF),
            pltpu.VMEM((BX, K, K), BF),
            pltpu.VMEM((BX, R, K), F32),
            pltpu.SemaphoreType.DMA((4,)),
        ],
        compiler_params=params(),
        name="points_to_group",
    )(charges, basis, leaf_up, box_up, parents)


def pack(code, charges, points, coef):
    return pl.pallas_call(
        pack_body,
        in_specs=[SMEM] + [HBM] * 3,
        out_specs=[VMEM] * 2 + [SMEM] * 3,
        out_shape=[
            sds((SENT, ROWS, M), BF),
            sds((LD, FX, M), BF),
            sds((SLOTS,), jnp.int32),
            sds((SLOTS,), jnp.int32),
            sds((2,), jnp.int32),
        ],
        scratch_shapes=[
            pltpu.VMEM((R, LD * M), BF),
            pltpu.VMEM((3, LD * M), F32),
            pltpu.VMEM((FR, LD * M), F32),
            pltpu.VMEM((FX, LD * M), F32),
            pltpu.SemaphoreType.DMA((3,)),
        ],
        compiler_params=params(),
        cost_estimate=pl.CostEstimate(flops=4 << 30, bytes_accessed=4 << 20, transcendentals=0),
        name="pack_and_list",
    )(code, charges, points, coef)


def twice(m):
    zero = jnp.zeros_like(m)
    return jnp.concatenate([jnp.concatenate([m, zero], axis=1), jnp.concatenate([zero, m], axis=1)], axis=0)


def unpack(x):
    return jnp.concatenate([x[:, :K], x[:, K:]], axis=0)


def raise_nodes(nodes, matrices):
    count = nodes.shape[0] // 2
    left = jnp.concatenate([nodes[2 * i] for i in range(count)], axis=0)
    right = jnp.concatenate([nodes[2 * i + 1] for i in range(count)], axis=0)
    mul = dot if nodes.dtype == BF else dot2
    return (mul(left, twice(matrices[0])) + mul(right, twice(matrices[1]))).reshape(count, R // 2, 2 * K)


def low_body(place, nodes_in, up_in, coupling_in, _, top, field, __, nodes, up, coupling, held, sems):
    moves = ((nodes_in, nodes), (up_in.at[pl.ds(0, 4)], up), (coupling_in.at[pl.ds(0, 4)], coupling))
    copies = load([pltpu.make_async_copy(a, b, sems.at[n]) for n, (a, b) in enumerate(moves)])
    for copy in copies:
        copy.wait()
    levels = [nodes[...]]
    for h in range(4):
        levels.append(raise_nodes(levels[h], (up[h, 0], up[h, 1])))
    packed = levels[4].astype(BF).reshape(R, 2 * K)
    for i in range(top.shape[0]):
        top[i] = packed
    start = 0
    for h in range(4):
        held[start : start + (LOW >> h)] = levels[h].astype(F32)
        start += LOW >> h
    me = place[0] & (LOW - 1)
    start = 0
    out = []
    for h in range(4):
        q = me >> h
        near, far = unpack(held[(q ^ 2) + start]), unpack(held[(q ^ 3) + start])
        out.append(dot2(near, coupling[h, 0]) + dot2(far, coupling[h, 1]))
        start += LOW >> h
    for h in range(4):
        field[h] = out[h]


def low_tree(place, nodes, up, coupling, sent, blocks):
    return pl.pallas_call(
        low_body,
        in_specs=[SMEM] + [ANY] * 4,
        out_specs=[VMEM, VMEM, ANY],
        out_shape=[
            sds((blocks, R, 2 * K), BF),
            sds((4, R, K), F32),
            sds(sent.shape, sent.dtype),
        ],
        input_output_aliases={4: 2},
        scratch_shapes=[
            pltpu.VMEM((LOW, R // 2, 2 * K), BF),
            pltpu.VMEM((4, 2, K, K), BF),
            pltpu.VMEM((4, 2, K, K), BF),
            pltpu.VMEM((2 * LOW, R // 2, 2 * K), F32),
            pltpu.SemaphoreType.DMA((3,)),
        ],
        compiler_params=params(),
        name="coarse_low",
    )(place, nodes, up, coupling, sent)


def split2(x):
    hi = x.astype(BF)
    return hi, (x - hi.astype(F32)).astype(BF)


def spread_features(table, feats, count):
    lane = lax.broadcasted_iota(jnp.int32, (M, M), 1)
    ones = 3 * len(PARTS) + 3
    feats[count] = jnp.where((lane >= ones) & (lane < ones + 3), 1.0, 0.0).astype(BF)
    expand = [expansion(i) for i in range(8)]
    for o in range(count // 8):
        rows = jnp.concatenate([table[8 * o + i, R:ROWS, :] for i in range(8)], axis=0)
        spread = [dot(rows, expand[i]).astype(BF) for i in range(8)]
        for i in range(8):
            feats[8 * o + i] = spread[i]


def near_loop(steps, slots, table, feats, target, acc):
    pad = jnp.zeros((M - FX, M), BF)

    def near(it, _):
        t, kernels, weights = [], [], []
        for u in range(UNROLL):
            place_of = (it * UNROLL + u) * 2
            one, two = slots[place_of], slots[place_of + 1]
            s0, s1 = one & 255, two & 255
            t.append((one >> 8) & 255)
            rows = jnp.concatenate([feats[s0], feats[s1]], axis=0)
            square = dot(rows, jnp.concatenate([target[jnp.minimum(t[u], LD - 1)], pad], axis=0))
            kernels.append(lax.rsqrt(square.astype(BF)))
            weights.append(jnp.concatenate([table[s0, 0:R, :], table[s1, 0:R, :]], axis=1))
        terms = [dot(weights[u], kernels[u]) for u in range(UNROLL)]
        for u in range(UNROLL):
            acc[t[u]] += terms[u]
        return 0

    lax.fori_loop(0, steps, near, 0)


def own_body(sizes, slots, target_in, sent, acc, table, feats, target, sems):
    moves = ((sent.at[pl.ds(0, LD)], table.at[pl.ds(0, LD)]), (target_in, target))
    copies = load([pltpu.make_async_copy(a, b, sems.at[n]) for n, (a, b) in enumerate(moves)])
    acc[...] = jnp.zeros(acc.shape, F32)
    table[LD] = jnp.zeros((ROWS, M), BF)
    for copy in copies:
        copy.wait()
    spread_features(table, feats, LD)
    near_loop(sizes[0], slots, table, feats, target, acc)


def near_own(sizes, slots, target, sent):
    return pl.pallas_call(
        own_body,
        in_specs=[SMEM] * 2 + [ANY] * 2,
        out_specs=VMEM,
        out_shape=sds((LD + 1, R, M), F32),
        scratch_shapes=[
            pltpu.VMEM((LD + 1, ROWS, M), BF),
            pltpu.VMEM((LD + 1, M, M), BF),
            pltpu.VMEM((LD, FX, M), BF),
            pltpu.SemaphoreType.DMA((2,)),
        ],
        compiler_params=params(63.5),
        cost_estimate=pl.CostEstimate(flops=2 << 30, bytes_accessed=2 << 20, transcendentals=4 << 20),
        name="near_own",
    )(sizes, slots, target, sent)


def fields_body(sizes, slots, leaf_sources, leaf_classes, box_sources, box_classes, place, low_field, down, coupling, near_in, target_in, matrices_in, box_matrices_in, left, mine, right, acc, leaf_field, box_field, base, tip, table, coefs, feats, target, matrices, box_matrices, low, high, sems):
    blocks = SENT - LD
    sources = (left, mine, right)
    moves = [(left.at[pl.ds(0, LD)], table.at[pl.ds(0, LD)]), (right.at[pl.ds(0, LD)], table.at[pl.ds(LD, LD)])]
    moves += [(src.at[pl.ds(LD, blocks)], coefs.at[pl.ds(n * blocks, blocks)]) for n, src in enumerate(sources)]
    moves += [(target_in, target), (matrices_in, matrices), (box_matrices_in, box_matrices), (near_in, acc)]
    copies = load([pltpu.make_async_copy(a, b, sems.at[n]) for n, (a, b) in enumerate(moves)])
    me = place[0]
    total = low_field[3]
    chain = down[3, (me >> 3) & 1].astype(F32)
    for h in range(2, -1, -1):
        both = dot2(jnp.concatenate([total, chain], axis=0), down[h, (me >> h) & 1])
        total = low_field[h] + both[:R]
        chain = both[R:]
    tips = []
    for h in range(4, 8):
        hi, lo = split2(chain)
        stack = jnp.concatenate([coupling[h, 0], coupling[h, 1], down[min(h, 6), (me >> h) & 1]], axis=0)
        product = dot(stack, hi) + dot(stack, lo)
        tips.append((split2(product[0:K]), split2(product[K : 2 * K])))
        chain = product[2 * K :]
    base[...] = total
    for h in range(4):
        for i in range(2):
            for n in range(2):
                tip[h, i, n] = tips[h][i][n]

    table[BOTH] = jnp.zeros((ROWS, M), BF)
    for copy in copies:
        copy.wait()

    first = lax.broadcasted_iota(jnp.int32, (R, 2 * K), 1) < K
    for n in range(3):
        for group in range(PAIRS // 5):
            ready = []
            for i in range(5 * group, 5 * group + 5):
                x = jnp.concatenate(
                    [coefs[n * blocks + b, r : r + 16, :] for b, r in coef_places(i)], axis=0
                ).astype(F32)
                y = pltpu.roll(x, K, 1)
                ready.append(
                    [
                        jnp.where(first, x, 0.0).astype(BF),
                        jnp.where(first, y, 0.0).astype(BF),
                        jnp.where(first, 0.0, y).astype(BF),
                        jnp.where(first, 0.0, x).astype(BF),
                    ]
                )
            for i in range(5):
                at_row = 2 * (5 * group + i)
                row = n * LD + at_row if at_row < LD else ALL + n * BX + at_row - LD
                low[row], low[row + 1], high[row], high[row + 1] = ready[i]

    def gather(source, kind, mats, width):
        total = jnp.zeros((R, K), F32)
        for g in range(width // 4):
            s = [source(4 * g + i) for i in range(4)]
            vec = jnp.concatenate([low[s[0]] + high[s[1]], low[s[2]] + high[s[3]]], axis=1)
            mat = jnp.concatenate([mats[kind(4 * g + i)] for i in range(4)], axis=0)
            total = total + dot(vec, mat)
        return total

    def couple(it, _):
        rows = [it * 8 + u for u in range(8)]
        got = [
            gather(
                lambda a: leaf_sources[a, row] - (me - 1) * LD, lambda a: leaf_classes[a, row], matrices, ADM
            )
            for row in rows
        ]
        for row, value in zip(rows, got):
            leaf_field[row] = value
        return 0

    lax.fori_loop(0, LD // 8, couple, 0)
    got = [
        gather(
            lambda a: box_sources[box, a] - (me - 1) * BX + ALL, lambda a: box_classes[box, a], box_matrices, ADMB
        )
        for box in range(BX)
    ]
    for box in range(BX):
        box_field[box] = got[box]

    spread_features(table, feats, BOTH)
    near_loop(sizes[1], slots, table, feats, target, acc)


def fields(indices, place, low_field, down, coupling, near_part, target, matrices, box_matrices, sents):
    return pl.pallas_call(
        fields_body,
        in_specs=[SMEM] * 7 + [VMEM] * 3 + [ANY] * 7,
        out_specs=[VMEM] * 5,
        out_shape=[
            sds((LD + 1, R, M), F32),
            sds((LD, R, K), F32),
            sds((BX, R, K), F32),
            sds((R, K), F32),
            sds((4, 2, 2, K, K), BF),
        ],
        scratch_shapes=[
            pltpu.VMEM((BOTH + 1, ROWS, M), BF),
            pltpu.VMEM((3 * (SENT - LD), ROWS, M), BF),
            pltpu.VMEM((BOTH + 1, M, M), BF),
            pltpu.VMEM((LD, FX, M), BF),
            pltpu.VMEM((matrices.shape[0], K, K), BF),
            pltpu.VMEM((matrices.shape[0], K, K), BF),
            pltpu.VMEM((6 * PAIRS, R, 2 * K), BF),
            pltpu.VMEM((6 * PAIRS, R, 2 * K), BF),
            pltpu.SemaphoreType.DMA((9,)),
        ],
        compiler_params=params(),
        cost_estimate=pl.CostEstimate(flops=8 << 30, bytes_accessed=4 << 20, transcendentals=8 << 20),
        name="near_and_coupled_fields",
    )(*indices, place, low_field, down, coupling, near_part, target, matrices, box_matrices, *sents)


def final_body(place, nodes_in, up_in, base_in, tip_in, parents, leaf_field_in, box_field_in, box_down_in, leaf_down_in, basis_in, near_in, out, boxes, held, nodes, up, base, tip, box_field, box_down, leaf_field, leaf_down, basis, near_part, sems):
    moves = ((nodes_in, nodes), (up_in.at[pl.ds(4, 3)], up), (base_in, base), (tip_in, tip))
    moves += ((box_field_in, box_field), (box_down_in, box_down), (leaf_down_in, leaf_down))
    moves += ((leaf_field_in, leaf_field), (basis_in, basis), (near_in, near_part))
    copies = load([pltpu.make_async_copy(a, b, sems.at[n]) for n, (a, b) in enumerate(moves)])
    for copy in copies[:4]:
        copy.wait()
    levels = [nodes[...].reshape(LOW, R // 2, 2 * K)]
    for h in range(3):
        levels.append(raise_nodes(levels[h], (up[h, 0], up[h, 1])))
    start = 0
    for h in range(4):
        held[start : start + (LOW >> h)] = levels[h].astype(F32)
        start += LOW >> h
    me = (place[0] >> 4) & (LOW - 1)
    total = base[...]
    start = 0
    for h in range(4):
        for i in range(2):
            hi, lo = split2(unpack(held[((me >> h) ^ (2 + i)) + start]))
            total = total + (dot(hi, tip[h, i, 0]) + dot(hi, tip[h, i, 1]) + dot(lo, tip[h, i, 0]))
        start += LOW >> h
    for copy in copies[4:]:
        copy.wait()
    group = total.astype(BF)
    got = [(box_field[box] + dot(group, box_down[box])).astype(BF) for box in range(BX)]
    for box in range(BX):
        boxes[box] = got[box]
    for part in range(LD // 8):
        leaves = range(8 * part, 8 * part + 8)
        field = [
            (leaf_field[leaf] + dot(boxes[parents[leaf]], leaf_down[leaf])).astype(BF) for leaf in leaves
        ]
        got = [
            near_part[leaf] + dot(field[i], basis[:, pl.ds(leaf * M, M)]) for i, leaf in enumerate(leaves)
        ]
        for i, leaf in enumerate(leaves):
            out[:, pl.ds(leaf * M, M)] = got[i]


def finish(place, nodes, up, base, tip, parents, leaf_field, box_field, box_down, leaf_down, basis, near_part):
    return pl.pallas_call(
        final_body,
        in_specs=[SMEM] + [ANY] * 4 + [SMEM] + [ANY] * 6,
        out_specs=VMEM,
        out_shape=sds((R, LD * M), F32),
        scratch_shapes=[
            pltpu.VMEM((BX, R, K), BF),
            pltpu.VMEM((2 * LOW, R // 2, 2 * K), F32),
            pltpu.VMEM(nodes.shape, BF),
            pltpu.VMEM((3, 2, K, K), BF),
            pltpu.VMEM((R, K), F32),
            pltpu.VMEM((4, 2, 2, K, K), BF),
            pltpu.VMEM((BX, R, K), F32),
            pltpu.VMEM((BX, K, K), BF),
            pltpu.VMEM((LD, R, K), F32),
            pltpu.VMEM((LD, K, K), BF),
            pltpu.VMEM((K, LD * M), BF),
            pltpu.VMEM((LD + 1, R, M), F32),
            pltpu.SemaphoreType.DMA((10,)),
        ],
        compiler_params=params(),
        name="group_to_points",
    )(place, nodes, up, base, tip, parents, leaf_field, box_field, box_down, leaf_down, basis, near_part)


def exchange(x):
    count = lax.axis_size(AXES)
    left = lax.ppermute(x, AXES, [(i, i + 1) for i in range(count - 1)])
    right = lax.ppermute(x, AXES, [(i + 1, i) for i in range(count - 1)])
    return left, right


def gather_groups(copies, groups):
    return lax.all_to_all(copies, AXES, 0, 0, axis_index_groups=groups, tiled=True)


def local(
    charges,
    points,
    leaf_basis,
    leaf_parent,
    leaf_up,
    leaf_down,
    box_up,
    box_down,
    top_up,
    top_down,
    top_coupling,
    leaf_sources,
    leaf_classes,
    leaf_coupling,
    box_sources,
    box_classes,
    box_coupling,
    near_leaves,
    near_count,
):
    device = lax.axis_index(AXES)
    place = device.astype(jnp.int32).reshape(1)
    parents = leaf_parent[0]

    coef, ascent = climb(charges, leaf_basis, leaf_up, box_up, parents)

    blocks = lax.axis_size(AXES) // LOW
    low_groups = [[b * LOW + i for i in range(LOW)] for b in range(blocks)]
    high_groups = [[b * LOW + i for b in range(blocks)] for i in range(LOW)]
    rel = near_leaves - device * LD
    mine = (rel >= 0) & (rel < LD)
    used = jnp.arange(NEAR, dtype=jnp.int32)[None, :] < near_count[:, None]
    row = jnp.where(rel < 0, rel + LD, rel)
    leaf_ids = jnp.arange(LD, dtype=jnp.int32)[:, None]
    code = row | leaf_ids << 8 | jnp.where(used, jnp.where(mine, 1, 2), 0) << 16

    low_nodes = gather_groups(ascent, low_groups)
    sent, target, own, halo, sizes = pack(code, charges, points, coef)
    top, low_field, sent = low_tree(place, low_nodes, top_up, top_coupling, sent, blocks)
    high_nodes = gather_groups(top, high_groups)
    sent_left, sent_right = exchange(sent)
    near_part = near_own(sizes, own, target, sent)

    near_part, leaf_field, box_field, base, tip = fields(
        (sizes, halo, leaf_sources.T, leaf_classes.T, box_sources, box_classes),
        place,
        low_field,
        top_down,
        top_coupling,
        near_part,
        target,
        leaf_coupling,
        box_coupling,
        (sent_left, sent, sent_right),
    )
    return finish(
        place, high_nodes, top_up, base, tip, parents, leaf_field, box_field, box_down, leaf_down, leaf_basis, near_part
    )


def solution(mesh):
    split = P(AXES)
    return jax.shard_map(
        local,
        mesh=mesh,
        in_specs=(
            P(None, AXES),
            P(None, AXES),
            P(None, AXES),
            split,
            split,
            split,
            split,
            split,
            P(),
            P(),
            P(),
            split,
            split,
            P(),
            split,
            split,
            P(),
            split,
            split,
        ),
        out_specs=P(None, AXES),
        check_vma=False,
    )
```
